512 devices in a mesh: dp: 64 (over y, x, z_lo), tensor: 8 (over z_hi, core).
Axes of the slice: x: 4, y: 8, z: 8 (z_hi: 4, z_lo: 2; z = z_hi * 2 + z_lo), core: 2. Of those that a mesh axis runs over, the one named last changes fastest.
Arguments:
- patches: bfloat16 [32768, 1152], P('dp'), may hold values from -6 to 6
- ln_gain: float32 [1152], replicated, may hold values from 0.1 to 1.9
- w_up: bfloat16 [1152, 4304], P(None, 'tensor'), may hold values from -0.1875 to 0.1875
- b_up: float32 [4304], P('tensor'), may hold values from -3 to 3
- w_down: bfloat16 [4304, 1152], P('tensor'), may hold values from -0.09375 to 0.09375
- b_down: float32 [1152], replicated, may hold values from -0.6 to 0.6
- head_gain: float32 [1152], replicated, may hold values from 0.1 to 1.9
- text_feats: bfloat16 [128, 1152], P('dp'), may hold values from -24 to 24
- pair_ids: int32 [128], P('dp'), may hold values from 0 to 63
- log_sharpness: float32 [1], replicated, may hold values from 1 to 2
- pairwise_logit_shift: float32 [1], replicated, may hold values from -3 to -1
Outputs:
- grad_patches: bfloat16 [32768, 1152], P('dp')
- grad_text: float32 [128, 1152], P('dp')
The draws below stay inside these ranges and needn't reach their ends.
All inputs are finite; a program needn't handle non-finite values.
Results may differ from the reference program's by a relative error of at most 0.015.
Values may be sent and summed in bfloat16 or wider, within the bound.
No kernel may reach another device: no remote copies, remote signals or barrier semaphores. Data moves between devices by JAX's collectives and lax.ppermute only.
A program may use at most 64 MiB of HBM per device.

```python
import jax
import jax.numpy as jnp
from jax import lax

D = 1152
FF = 4304
PATCHES = 256
IMG_DEV = 2
BATCH = 128
TOKENS = 32768
N_DP = 64
N_TENSOR = 8


def with_ends(drawn, stream_key, least, high):
    longest = drawn.shape.index(max(drawn.shape))
    spots = []
    for shift in (0, 1):
        where = [jax.random.randint(jax.random.fold_in(stream_key, axis), (), 0, length) for axis, length in enumerate(drawn.shape)]
        where[longest] = (where[longest] + shift) % drawn.shape[longest]
        spots.append(tuple(where))
    return drawn.at[spots[0]].set(least).at[spots[1]].set(high)


def level_of(key, extent, split, smallest, largest):
    factor_of = 1.0
    for position, blocks in split:
        steps = jax.random.uniform(jax.random.fold_in(jax.random.fold_in(key, 6), position), (blocks,), jnp.float32, smallest / len(split), largest / len(split))
        factor_of = factor_of * jnp.repeat(jnp.exp(steps), extent[position] // blocks).reshape((-1,) + (1,) * (len(extent) - 1 - position))
    return factor_of


def gaussian(stream_key, shape, width, most, cuts=(), held_as=jnp.bfloat16):
    factor_of = level_of(stream_key, shape, cuts, -0.22, 0.18) if cuts else 1.0
    values = jax.random.normal(stream_key, shape, jnp.float32) * width * factor_of
    return jnp.minimum(jnp.maximum(values, -most), most).astype(held_as)


def setup_inputs(seed: int = 0) -> dict:
    seeds = jax.random.split(jax.random.key(seed), 12)
    patches = gaussian(seeds[0], (TOKENS, D), 1.0, 6.0, ((0, 64),))
    ln_gain = jnp.clip(1.0 + 0.18 * jax.random.normal(seeds[1], (D,), jnp.float32), 0.1, 1.9)
    w_up = gaussian(seeds[2], (D, FF), D ** -0.5, 0.1875, ((1, 8),))
    b_up = gaussian(seeds[3], (FF,), 0.5, 3.0, ((0, 8),), jnp.float32)
    w_down = gaussian(seeds[4], (FF, D), FF ** -0.5, 0.09375, ((0, 8),))
    b_down = gaussian(seeds[5], (D,), 0.1, 0.6, (), jnp.float32)
    head_gain = jnp.clip(1.0 + 0.18 * jax.random.normal(seeds[6], (D,), jnp.float32), 0.1, 1.9)
    text_feats = gaussian(seeds[7], (BATCH, D), 4.0, 24.0, ((0, 64),))
    pair_ids = with_ends(jax.random.randint(seeds[8], (BATCH,), 0, BATCH // 2), jax.random.fold_in(seeds[8], 1), 0, (BATCH // 2) - 1).astype(jnp.int32)
    log_sharpness = jnp.clip(jax.random.uniform(seeds[9], (1,), jnp.float32, 1.0, 2.0), 1.0, 2.0)
    pairwise_logit_shift = jnp.clip(jax.random.uniform(seeds[10], (1,), jnp.float32, -3.0, -1.0), -3.0, -1.0)
    return dict(patches=patches, ln_gain=ln_gain, w_up=w_up, b_up=b_up, w_down=w_down, b_down=b_down, head_gain=head_gain, text_feats=text_feats, pair_ids=pair_ids, log_sharpness=log_sharpness, pairwise_logit_shift=pairwise_logit_shift)


epsilon = 1e-06
loss_scale = 131072.0

def norm_parts(values):
    centre = values - lax.optimization_barrier(jnp.mean(values, axis=-1, keepdims=True))
    inverse = lax.rsqrt(lax.optimization_barrier(jnp.mean(centre * centre, axis=-1, keepdims=True)) + epsilon)
    return (centre * inverse, inverse)

def norm_back(grad_out, norm_gain, normed_vals, inverse):
    scaled = grad_out * norm_gain
    return inverse * (scaled - lax.optimization_barrier(jnp.mean(scaled, axis=-1, keepdims=True)) - normed_vals * lax.optimization_barrier(jnp.mean(scaled * normed_vals, axis=-1, keepdims=True)))

def gelu_tanh(values):
    return jax.nn.gelu(values, approximate=True)

def grouped_sum(first_mat, second_mat, groups):
    group_width = second_mat.shape[0] // groups
    running = jnp.zeros((first_mat.shape[0], second_mat.shape[1]), jnp.float32)
    for group in range(groups):
        lower = group * group_width
        part_prod = jnp.dot(first_mat[:, lower:lower + group_width], second_mat[lower:lower + group_width], preferred_element_type=jnp.float32)
        rounded = lax.optimization_barrier(part_prod.astype(jnp.bfloat16))
        running = running + rounded.astype(jnp.float32)
    return running

def block_forward(token_rows, ln_gain, w_up, b_up, w_down, b_down):
    inputs = token_rows.astype(jnp.float32)
    normed_in, inverse_in = norm_parts(inputs)
    normed = (normed_in * ln_gain).astype(jnp.bfloat16)
    pre_act = jnp.dot(normed, w_up, preferred_element_type=jnp.float32) + b_up
    activation = gelu_tanh(pre_act).astype(jnp.bfloat16)
    hidden = inputs + jnp.dot(activation, w_down, preferred_element_type=jnp.float32) + b_down
    return (hidden, pre_act, normed_in, inverse_in)

def block_backward(token_rows, g_pool, ln_gain, w_up, b_up, w_down, b_down):
    hidden, pre_act, normed_in, inverse_in = block_forward(token_rows, ln_gain, w_up, b_up, w_down, b_down)
    images = g_pool.shape[0]
    g_hidden = jnp.broadcast_to((g_pool / PATCHES)[:, None, :], (images, PATCHES, D)).reshape(images * PATCHES, D)
    g_rows = g_hidden.astype(jnp.bfloat16)
    g_act = jnp.dot(g_rows, w_down.T, preferred_element_type=jnp.float32)
    g_pre = jax.vjp(gelu_tanh, pre_act)[1](g_act)[0].astype(jnp.bfloat16)
    g_normed = grouped_sum(g_pre, w_up.T, N_TENSOR)
    return (g_hidden + norm_back(g_normed, ln_gain, normed_in, inverse_in)).astype(jnp.bfloat16)

def reference(patches, ln_gain, w_up, b_up, w_down, b_down, head_gain, text_feats, pair_ids, log_sharpness, pairwise_logit_shift):
    blocks = patches.reshape(N_DP, IMG_DEV * PATCHES, D)

    def pool_block(token_rows):
        hidden = block_forward(token_rows, ln_gain, w_up, b_up, w_down, b_down)[0]
        return hidden.reshape(IMG_DEV, PATCHES, D).mean(axis=1)
    pooled = lax.map(pool_block, blocks).reshape(BATCH, D)
    feat_n, feat_s = norm_parts(pooled)
    features = feat_n * head_gain
    feat_len = jnp.sqrt(lax.optimization_barrier(jnp.sum(features * features, axis=-1, keepdims=True)) + epsilon)
    picture_feature_vector = features / feat_len
    text_vals = text_feats.astype(jnp.float32)
    text_len = jnp.sqrt(lax.optimization_barrier(jnp.sum(text_vals * text_vals, axis=-1, keepdims=True)) + epsilon)
    unit_text = text_vals / text_len
    caption_normalized_directions = lax.optimization_barrier(unit_text.astype(jnp.bfloat16)).astype(jnp.float32)
    sharpness_multiplier = jnp.exp(log_sharpness[0])
    pairwise_logit_matrix = sharpness_multiplier * jnp.dot(picture_feature_vector, caption_normalized_directions.T, precision=lax.Precision.HIGHEST) + pairwise_logit_shift[0]
    pair_sign = jnp.where(pair_ids[:, None] == pair_ids[None, :], 1.0, -1.0).astype(jnp.float32)
    pairwise_logit_derivative = -loss_scale * pair_sign * jax.nn.sigmoid(-pair_sign * pairwise_logit_matrix) / BATCH
    picture_loss_derivative = sharpness_multiplier * jnp.dot(pairwise_logit_derivative, caption_normalized_directions, precision=lax.Precision.HIGHEST)
    caption_loss_derivative = sharpness_multiplier * jnp.dot(pairwise_logit_derivative.T, picture_feature_vector, precision=lax.Precision.HIGHEST)
    grad_text = (caption_loss_derivative - unit_text * lax.optimization_barrier(jnp.sum(unit_text * caption_loss_derivative, axis=-1, keepdims=True))) / text_len
    g_feat = (picture_loss_derivative - picture_feature_vector * lax.optimization_barrier(jnp.sum(picture_feature_vector * picture_loss_derivative, axis=-1, keepdims=True))) / feat_len
    g_pool = norm_back(g_feat, head_gain, feat_n, feat_s)

    def back_block(pair):
        return block_backward(pair[0], pair[1], ln_gain, w_up, b_up, w_down, b_down)
    grad_patches = lax.map(back_block, (blocks, g_pool.reshape(N_DP, IMG_DEV, D))).reshape(TOKENS, D)
    return (grad_patches, grad_text)
```

```python
import jax
import jax.numpy as jnp
from jax import lax
from jax.sharding import PartitionSpec as P

PATCHES = 256
EPS = 1e-06
LOSS_SCALE = 131072.0
HIGH = lax.Precision.HIGHEST


def norm_parts(values):
    centre = values - jnp.mean(values, axis=-1, keepdims=True)
    inverse = lax.rsqrt(jnp.mean(centre * centre, axis=-1, keepdims=True) + EPS)
    return centre * inverse, inverse


def norm_back(grad_out, gain, normed, inverse):
    scaled = grad_out * gain
    return inverse * (
        scaled
        - jnp.mean(scaled, axis=-1, keepdims=True)
        - normed * jnp.mean(scaled * normed, axis=-1, keepdims=True)
    )


def gelu_tanh(values):
    return jax.nn.gelu(values, approximate=True)


def swap(value, axis, partner):
    size = lax.axis_size(axis)
    return lax.ppermute(value, axis, [(i, partner(i)) for i in range(size)])


def swap_xor(value, axis, mask):
    return swap(value, axis, lambda i: i ^ mask)


def gather_dp(rows):
    for masks in ((16, 32, 48), (8, 1, 9), (2, 4, 6)):
        parts = [rows] + [swap_xor(rows, "dp", mask) for mask in masks]
        rows = jnp.concatenate(parts, axis=0)
    return rows


def z_next(i):
    return i ^ 2


def z_prev(i):
    return (3 - i // 2) * 2 + i % 2


def rows_at(array, start, count):
    return lax.dynamic_slice_in_dim(array, start, count, 0)


def on_device(
    patches,
    ln_gain,
    w_up,
    b_up,
    w_down,
    b_down,
    head_gain,
    text_feats,
    pair_ids,
    log_sharpness,
    pairwise_logit_shift,
):
    img_dev, width = text_feats.shape
    batch = img_dev * lax.axis_size("dp")
    position = lax.axis_index("tensor")
    core = position % 2
    ring = position // 2
    u = ((ring == 1) | (ring == 2)).astype(jnp.int32)
    v = (ring >= 2).astype(jnp.int32)

    text_vals = text_feats.astype(jnp.float32)
    text_len = jnp.sqrt(jnp.sum(text_vals * text_vals, axis=-1, keepdims=True) + EPS)
    unit_text = text_vals / text_len
    text_own = unit_text.astype(jnp.bfloat16)
    id_cols = jnp.pad(pair_ids.astype(jnp.bfloat16)[:, None], ((0, 0), (0, 127)))
    all_rows = gather_dp(jnp.concatenate([text_own, id_cols], axis=1))
    text_all = all_rows[:, :width].astype(jnp.float32)
    ids_all = all_rows[:, width].astype(jnp.int32)

    inputs = patches.astype(jnp.float32)
    normed_in, _ = norm_parts(inputs)
    normed = (normed_in * ln_gain).astype(jnp.bfloat16)
    pre_act = jnp.dot(normed, w_up, preferred_element_type=jnp.float32) + b_up
    activation = gelu_tanh(pre_act).astype(jnp.bfloat16).astype(jnp.float32)
    act_mean = activation.reshape(img_dev, PATCHES, -1).mean(axis=1)
    part = jnp.dot(act_mean, w_down.astype(jnp.float32), precision=HIGH)
    got = [part] + [swap_xor(part, "tensor", mask) for mask in range(1, 8)]
    mlp_mean = ((got[0] + got[1]) + (got[2] + got[3])) + (
        (got[4] + got[5]) + (got[6] + got[7])
    )
    pooled = inputs.reshape(img_dev, PATCHES, width).mean(axis=1) + mlp_mean + b_down

    feat_n, feat_s = norm_parts(pooled)
    features = feat_n * head_gain
    feat_len = jnp.sqrt(jnp.sum(features * features, axis=-1, keepdims=True) + EPS)
    img_emb = features / feat_len
    sharp = jnp.exp(log_sharpness[0])
    shift = pairwise_logit_shift[0]

    def logit_grad(rows, columns):
        logits = sharp * jnp.dot(rows, columns.T, precision=HIGH) + shift
        sign = jnp.where(pair_ids[:, None] == ids_all[None, :], 1.0, -1.0)
        return -LOSS_SCALE * sign * jax.nn.sigmoid(-sign * logits) / batch

    g_img = sharp * jnp.dot(logit_grad(img_emb, text_all), text_all, precision=HIGH)
    g_feat = (
        g_img - img_emb * jnp.sum(img_emb * g_img, axis=-1, keepdims=True)
    ) / feat_len
    g_hidden = norm_back(g_feat, head_gain, feat_n, feat_s) / PATCHES

    g_act = lax.dot_general(
        g_hidden.astype(jnp.bfloat16),
        w_down,
        (((1,), (1,)), ((), ())),
        preferred_element_type=jnp.float32,
    )
    g_act = jnp.broadcast_to(g_act[:, None, :], (img_dev, PATCHES, g_act.shape[1]))
    g_act = g_act.reshape(pre_act.shape)
    g_pre = jax.vjp(gelu_tanh, pre_act)[1](g_act)[0].astype(jnp.bfloat16)

    def up_back(rows):
        return lax.dot_general(
            rows, w_up, (((1,), (1,)), ((), ())), preferred_element_type=jnp.float32
        ).astype(jnp.bfloat16)

    away = up_back(rows_at(g_pre, (1 - core) * PATCHES, PATCHES))
    other = swap_xor(away, "tensor", 1)
    keep = up_back(rows_at(g_pre, core * PATCHES, PATCHES))

    def wide(array, start, count):
        return rows_at(array, start, count).astype(jnp.float32)

    def first(start):
        return wide(keep, start, 64) + wide(other, start, 64)

    send_a = first(64 * (1 - u)).astype(jnp.bfloat16)
    send_b = first(128 + 64 * (1 - v)).astype(jnp.bfloat16)
    got_a = swap(send_a, "tensor", z_next)
    got_b = swap(send_b, "tensor", z_prev)
    sum_a = first(64 * u) + got_a.astype(jnp.float32)
    sum_b = first(128 + 64 * v) + got_b.astype(jnp.float32)
    send_a = rows_at(sum_a, 32 * (1 - v), 32).astype(jnp.bfloat16)
    send_b = rows_at(sum_b, 32 * (1 - u), 32).astype(jnp.bfloat16)
    got_a = swap(send_a, "tensor", z_prev)
    got_b = swap(send_b, "tensor", z_next)
    sum_a = rows_at(sum_a, 32 * v, 32) + got_a.astype(jnp.float32)
    sum_b = rows_at(sum_b, 32 * u, 32) + got_b.astype(jnp.float32)

    def start_a(uu, vv):
        return 64 * uu + 32 * vv

    def start_b(uu, vv):
        return 128 + 64 * vv + 32 * uu

    own_x = jnp.concatenate(
        [
            rows_at(patches, core * PATCHES + start_a(u, v), 32),
            rows_at(patches, core * PATCHES + start_b(u, v), 32),
        ]
    ).astype(jnp.float32)
    own_n, own_s = norm_parts(own_x)
    g_own = rows_at(g_hidden, core, 1)
    done = norm_back(jnp.concatenate([sum_a, sum_b]), ln_gain, own_n, own_s) + g_own
    done = done.astype(jnp.bfloat16)

    from_next = swap(done, "tensor", z_next)
    from_prev = swap(done, "tensor", z_prev)
    far_a = swap(from_prev[:32], "tensor", z_next)
    far_b = swap(from_next[32:], "tensor", z_prev)
    mine = [done, from_next, from_prev, far_a, far_b]
    theirs = [swap_xor(piece, "tensor", 1) for piece in mine]
    grad_patches = jnp.zeros(patches.shape, jnp.bfloat16)
    for side, pieces in ((core, mine), (1 - core, theirs)):
        base = side * PATCHES
        blocks = [
            (pieces[0][:32], start_a(u, v)),
            (pieces[0][32:], start_b(u, v)),
            (pieces[1][:32], start_a(1 - u, v)),
            (pieces[1][32:], start_b(1 - u, v)),
            (pieces[2][:32], start_a(u, 1 - v)),
            (pieces[2][32:], start_b(u, 1 - v)),
            (pieces[3], start_a(1 - u, 1 - v)),
            (pieces[4], start_b(1 - u, 1 - v)),
        ]
        for block, start in blocks:
            grad_patches = lax.dynamic_update_slice_in_dim(
                grad_patches, block, base + start, 0
            )

    img_all = gather_dp(img_emb)
    lg_text = logit_grad(text_own.astype(jnp.float32), img_all)
    g_text = sharp * jnp.dot(lg_text, img_all, precision=HIGH)
    grad_text = (
        g_text - unit_text * jnp.sum(unit_text * g_text, axis=-1, keepdims=True)
    ) / text_len
    return grad_patches, grad_text


def solution(mesh):
    in_specs = (
        P("dp", None),
        P(),
        P(None, "tensor"),
        P("tensor"),
        P("tensor", None),
        P(),
        P(),
        P("dp", None),
        P("dp"),
        P(),
        P(),
    )
    out_specs = (P("dp", None), P("dp", None))
    return jax.shard_map(
        on_device, mesh=mesh, in_specs=in_specs, out_specs=out_specs, check_vma=False
    )
```

```python
import jax
import jax.numpy as jnp
from jax import lax
from jax.sharding import PartitionSpec as P

PATCHES = 256
EPS = 1e-06
LOSS_SCALE = 131072.0
HIGH = lax.Precision.HIGHEST


def norm_parts(values):
    centre = values - jnp.mean(values, axis=-1, keepdims=True)
    inverse = lax.rsqrt(jnp.mean(centre * centre, axis=-1, keepdims=True) + EPS)
    return centre * inverse, inverse


def norm_back(grad_out, gain, normed, inverse):
    scaled = grad_out * gain
    return inverse * (
        scaled
        - jnp.mean(scaled, axis=-1, keepdims=True)
        - normed * jnp.mean(scaled * normed, axis=-1, keepdims=True)
    )


def gelu_tanh(values):
    return jax.nn.gelu(values, approximate=True)


def swap(value, axis, partner):
    size = lax.axis_size(axis)
    return lax.ppermute(value, axis, [(i, partner(i)) for i in range(size)])


def swap_xor(value, axis, mask):
    return swap(value, axis, lambda i: i ^ mask)


def spread(value, axis, groups=None):
    size = lax.axis_size(axis) if groups is None else len(groups[0])
    copies = jnp.broadcast_to(value[None], (size,) + value.shape)
    return lax.all_to_all(
        copies, axis, split_axis=0, concat_axis=0, axis_index_groups=groups
    )


def gather_dp(rows):
    return spread(rows, "dp").reshape(-1, rows.shape[1])


def step_one(i):
    return i ^ 2 if i % 2 == 0 else (3 - i // 2) * 2 + 1


def step_two(i):
    return (3 - i // 2) * 2 if i % 2 == 0 else i ^ 2


def rows_at(array, start, count):
    return lax.dynamic_slice_in_dim(array, start, count, 0)


def on_device(
    patches,
    ln_gain,
    w_up,
    b_up,
    w_down,
    b_down,
    head_gain,
    text_feats,
    pair_ids,
    log_sharpness,
    pairwise_logit_shift,
):
    img_dev, width = text_feats.shape
    batch = img_dev * lax.axis_size("dp")
    position = lax.axis_index("tensor")
    core = position % 2
    ring = position // 2
    u = ((ring == 1) | (ring == 2)).astype(jnp.int32)
    v = (ring >= 2).astype(jnp.int32)

    text_vals = text_feats.astype(jnp.float32)
    text_len = jnp.sqrt(jnp.sum(text_vals * text_vals, axis=-1, keepdims=True) + EPS)
    unit_text = text_vals / text_len
    text_own = unit_text.astype(jnp.bfloat16)
    id_cols = jnp.pad(pair_ids.astype(jnp.bfloat16)[:, None], ((0, 0), (0, 127)))
    all_rows = gather_dp(jnp.concatenate([text_own, id_cols], axis=1))
    text_all = all_rows[:, :width].astype(jnp.float32)
    ids_all = all_rows[:, width].astype(jnp.int32)

    inputs = patches.astype(jnp.float32)
    normed_in, _ = norm_parts(inputs)
    normed = (normed_in * ln_gain).astype(jnp.bfloat16)
    pre_act = jnp.dot(normed, w_up, preferred_element_type=jnp.float32) + b_up
    activation = gelu_tanh(pre_act).astype(jnp.bfloat16).astype(jnp.float32)
    act_mean = activation.reshape(img_dev, PATCHES, -1).mean(axis=1)
    part = jnp.dot(act_mean, w_down.astype(jnp.float32), precision=HIGH)
    mlp_mean = jnp.sum(spread(part, "tensor"), axis=0)
    pooled = inputs.reshape(img_dev, PATCHES, width).mean(axis=1) + mlp_mean + b_down

    feat_n, feat_s = norm_parts(pooled)
    features = feat_n * head_gain
    feat_len = jnp.sqrt(jnp.sum(features * features, axis=-1, keepdims=True) + EPS)
    img_emb = features / feat_len
    sharp = jnp.exp(log_sharpness[0])
    shift = pairwise_logit_shift[0]

    def logit_grad(rows, columns):
        logits = sharp * jnp.dot(rows, columns.T, precision=HIGH) + shift
        sign = jnp.where(pair_ids[:, None] == ids_all[None, :], 1.0, -1.0)
        return -LOSS_SCALE * sign * jax.nn.sigmoid(-sign * logits) / batch

    g_img = sharp * jnp.dot(logit_grad(img_emb, text_all), text_all, precision=HIGH)
    g_feat = (
        g_img - img_emb * jnp.sum(img_emb * g_img, axis=-1, keepdims=True)
    ) / feat_len
    g_hidden = norm_back(g_feat, head_gain, feat_n, feat_s) / PATCHES

    g_act = lax.dot_general(
        g_hidden.astype(jnp.bfloat16),
        w_down,
        (((1,), (1,)), ((), ())),
        preferred_element_type=jnp.float32,
    )
    g_act = jnp.broadcast_to(g_act[:, None, :], (img_dev, PATCHES, g_act.shape[1]))
    g_act = g_act.reshape(pre_act.shape)
    g_pre = jax.vjp(gelu_tanh, pre_act)[1](g_act)[0].astype(jnp.bfloat16)

    def up_back(rows):
        return lax.dot_general(
            rows, w_up, (((1,), (1,)), ((), ())), preferred_element_type=jnp.float32
        ).astype(jnp.bfloat16)

    away = up_back(rows_at(g_pre, (1 - core) * PATCHES, PATCHES))
    other = swap_xor(away, "tensor", 1)
    keep = up_back(rows_at(g_pre, core * PATCHES, PATCHES))

    def wide(array, start, count):
        return rows_at(array, start, count).astype(jnp.float32)

    one = jnp.where(core == 0, u, v)
    two = jnp.where(core == 0, v, u)

    def second(start):
        return first_rows(start) + wide(got_one, start - 128 * one, 64)

    def first_rows(start):
        return wide(keep, start, 64) + wide(other, start, 64)

    send_one = wide(keep, 128 * (1 - one), 128) + wide(other, 128 * (1 - one), 128)
    got_one = swap(send_one.astype(jnp.bfloat16), "tensor", step_one)
    send_two = second(128 * one + 64 * (1 - two)).astype(jnp.bfloat16)
    got_two = swap(send_two, "tensor", step_two)
    block = 128 * one + 64 * two
    g_normed = second(block) + got_two.astype(jnp.float32)

    own_x = rows_at(patches, core * PATCHES + block, 64).astype(jnp.float32)
    own_n, own_s = norm_parts(own_x)
    g_own = rows_at(g_hidden, core, 1)
    done = (norm_back(g_normed, ln_gain, own_n, own_s) + g_own).astype(jnp.bfloat16)

    rings = [[0, 2, 4, 6], [1, 3, 5, 7]]
    ours = spread(done, "tensor", rings)
    even = jnp.concatenate([ours[0], ours[3], ours[1], ours[2]])
    odd = jnp.concatenate([ours[0], ours[1], ours[3], ours[2]])
    ours = jnp.where(core == 0, even, odd)
    theirs = swap_xor(ours, "tensor", 1)
    grad_patches = jnp.where(
        core == 0, jnp.concatenate([ours, theirs]), jnp.concatenate([theirs, ours])
    )

    img_all = gather_dp(img_emb)
    lg_text = logit_grad(text_own.astype(jnp.float32), img_all)
    g_text = sharp * jnp.dot(lg_text, img_all, precision=HIGH)
    grad_text = (
        g_text - unit_text * jnp.sum(unit_text * g_text, axis=-1, keepdims=True)
    ) / text_len
    return grad_patches, grad_text


def solution(mesh):
    in_specs = (
        P("dp", None),
        P(),
        P(None, "tensor"),
        P("tensor"),
        P("tensor", None),
        P(),
        P(),
        P("dp", None),
        P("dp"),
        P(),
        P(),
    )
    out_specs = (P("dp", None), P("dp", None))
    return jax.shard_map(
        on_device, mesh=mesh, in_specs=in_specs, out_specs=out_specs, check_vma=False
    )
```

```python
import functools
import math

import jax
import jax.numpy as jnp
from jax import lax
from jax.experimental import pallas as pl
from jax.experimental.pallas import tpu as pltpu
from jax.sharding import PartitionSpec as P

PATCHES = 256
BLOCK = 64
EPS = 1e-06
LOSS_SCALE = 131072.0
HIGH = lax.Precision.HIGHEST
F32 = jnp.float32
BF16 = jnp.bfloat16
LAST = (((1,), (1,)), ((), ()))
SMEM = pl.BlockSpec(memory_space=pltpu.SMEM)
HBM = pl.BlockSpec(memory_space=pltpu.HBM)
VMEM = pl.BlockSpec(memory_space=pltpu.VMEM)
LARGE = pltpu.CompilerParams(vmem_limit_bytes=60 * 1024 * 1024)
SMALL = pltpu.CompilerParams(vmem_limit_bytes=16 * 1024 * 1024)


def norm_parts(values):
    centre = values - jnp.mean(values, axis=-1, keepdims=True)
    inverse = lax.rsqrt(jnp.mean(centre * centre, axis=-1, keepdims=True) + EPS)
    return centre * inverse, inverse


def norm_back(grad_out, gain, normed, inverse):
    scaled = grad_out * gain
    return inverse * (
        scaled
        - jnp.mean(scaled, axis=-1, keepdims=True)
        - normed * jnp.mean(scaled * normed, axis=-1, keepdims=True)
    )


def split_stack(values):
    high = values.astype(BF16).astype(F32)
    rest = values - high
    mid = rest.astype(BF16).astype(F32)
    low = rest - mid
    return jnp.concatenate([high, mid, low, jnp.zeros_like(high)], axis=0).astype(BF16)


def unstack(sums):
    return (sums[0:8] + sums[8:16]) + sums[16:24]


def pack_kernel(ids_ref, text_ref, pack_ref, unit_ref, len_ref):
    text = text_ref[...].astype(F32)
    length = jnp.sqrt(jnp.sum(text * text, axis=-1, keepdims=True) + EPS)
    unit = text / length
    unit_ref[...] = unit
    len_ref[...] = jnp.broadcast_to(length, len_ref.shape)
    row = lax.broadcasted_iota(jnp.int32, (2, 128), 0)
    lane = lax.broadcasted_iota(jnp.int32, (2, 128), 1)
    ids = jnp.where(row == 0, ids_ref[0], ids_ref[1])
    ids = jnp.where(lane == 0, ids, 0).astype(F32)
    packed = jnp.concatenate([unit, ids], axis=1).astype(BF16)
    for copy in range(pack_ref.shape[0]):
        pack_ref[copy] = packed


def pack_text(pair_ids, text_feats, copies):
    width = text_feats.shape[1]
    return pl.pallas_call(
        pack_kernel,
        in_specs=[SMEM, pl.BlockSpec(memory_space=pltpu.VMEM)],
        out_shape=[
            jax.ShapeDtypeStruct((copies, 2, width + 128), BF16),
            jax.ShapeDtypeStruct((2, width), F32),
            jax.ShapeDtypeStruct((2, 128), F32),
        ],
        compiler_params=SMALL,
        name="pack_text",
    )(pair_ids, text_feats)


def forward_kernel(
    n_tensor, x_ref, gain_ref, bias_ref, b_down_ref, up_hbm, down_hbm,
    slope_ref, part_ref, up_ref, down_ref, act_sum, x_sum, sems,
):
    step = pl.program_id(0)
    image = step // 2
    up_copy = pltpu.make_async_copy(up_hbm, up_ref, sems.at[0])
    down_copy = pltpu.make_async_copy(down_hbm, down_ref, sems.at[1])

    @pl.when(step == 0)
    def _():
        up_copy.start()
        down_copy.start()
        act_sum[...] = jnp.zeros_like(act_sum)
        x_sum[...] = jnp.zeros_like(x_sum)

    x = x_ref[...].astype(F32)
    normed, _ = norm_parts(x)
    normed = (normed * gain_ref[...][None, :]).astype(BF16)

    @pl.when(step == 0)
    def _():
        up_copy.wait()

    pre = lax.dot_general(normed, up_ref[...], LAST, preferred_element_type=F32)
    pre = pre + bias_ref[...][None, :]
    root = math.sqrt(2.0 / math.pi)
    square = pre * pre
    tanh = jnp.tanh(root * (pre + 0.044715 * (square * pre)))
    half = 0.5 * (1.0 + tanh)
    act = (pre * half).astype(BF16).astype(F32)
    slope_ref[...] = half + (0.5 * root) * pre * (1.0 - tanh * tanh) * (
        1.0 + (3.0 * 0.044715) * square
    )

    def add(total, values):
        row = lax.broadcasted_iota(jnp.int32, total.shape, 0)
        sums = jnp.sum(values, axis=0, keepdims=True)
        total[...] += jnp.where(row == image, sums, 0.0)

    add(act_sum, act)
    add(x_sum, x)

    @pl.when(step == pl.num_programs(0) - 1)
    def _():
        down_copy.wait()
        stack = split_stack(act_sum[...] * (1.0 / PATCHES))
        mlp = unstack(jnp.dot(stack, down_ref[...], preferred_element_type=F32))
        rest = x_sum[...] * (1.0 / PATCHES) + b_down_ref[...][None, :]
        part_ref[...] = (mlp + rest * (1.0 / n_tensor))[0:2]


def forward(patches, ln_gain, up_t, b_up, w_down, b_down, n_tensor):
    tokens, width = patches.shape
    units = up_t.shape[0]
    rows = 128
    vector = lambda size: pl.BlockSpec((size,), lambda i: (0,))
    return pl.pallas_call(
        functools.partial(forward_kernel, n_tensor),
        grid=(tokens // rows,),
        in_specs=[
            pl.BlockSpec((rows, width), lambda i: (i, 0)),
            vector(width),
            vector(units),
            vector(width),
            HBM,
            HBM,
        ],
        out_specs=[
            pl.BlockSpec((rows, units), lambda i: (i, 0)),
            pl.BlockSpec((2, width), lambda i: (0, 0)),
        ],
        out_shape=[
            jax.ShapeDtypeStruct((tokens, units), F32),
            jax.ShapeDtypeStruct((2, width), F32),
        ],
        scratch_shapes=[
            pltpu.VMEM((units, width), BF16),
            pltpu.VMEM((units, width), BF16),
            pltpu.VMEM((8, units), F32),
            pltpu.VMEM((8, width), F32),
            pltpu.SemaphoreType.DMA((2,)),
        ],
        compiler_params=LARGE,
        cost_estimate=pl.CostEstimate(
            flops=2 * tokens * width * units,
            bytes_accessed=2 * tokens * width + 4 * units * width + 4 * tokens * units,
            transcendentals=tokens * units,
        ),
        name="forward",
    )(patches, ln_gain, b_up, b_down, up_t, w_down)


def back_rows(blocks, slope_ref, g_act, up_ref, g_pre, out_ref):
    for place, block in enumerate(blocks):
        start = pl.multiple_of(block * BLOCK, BLOCK)
        g_pre[place * BLOCK : (place + 1) * BLOCK, :] = (
            slope_ref[pl.ds(start, BLOCK), :] * g_act
        ).astype(BF16)
    out_ref[...] = jnp.dot(
        g_pre[...], up_ref[...], preferred_element_type=F32
    ).astype(BF16)


def pick_row(rows, index):
    row = lax.broadcasted_iota(jnp.int32, rows.shape, 0)
    return jnp.sum(jnp.where(row == index, rows, 0.0), axis=0, keepdims=True)


def loss_kernel(
    place_ref, scale_ref, ids_ref, pooled_ref, gain_ref, text_ref, down_hbm, up_hbm,
    slope_hbm, img_ref, spread_ref, hidden_ref, g_act_ref, away_ref, pooled, g_pre,
    down_ref, up_ref, slope_ref, sems,
):
    image = 1 - place_ref[0]
    rows = pl.ds(pl.multiple_of(image * PATCHES, PATCHES), PATCHES)
    down_copy = pltpu.make_async_copy(down_hbm, down_ref, sems.at[0])
    slope_copy = pltpu.make_async_copy(slope_hbm.at[rows, :], slope_ref, sems.at[1])
    up_copy = pltpu.make_async_copy(up_hbm, up_ref, sems.at[2])
    down_copy.start()
    slope_copy.start()
    up_copy.start()
    gain = gain_ref[...][None, :]
    batch, width = text_ref.shape[0], pooled_ref.shape[1]
    sharp, shift = scale_ref[0], scale_ref[1]
    pooled[...] = jnp.zeros_like(pooled)
    pooled[0:2, :] = pooled_ref[...]
    feat_n, feat_s = norm_parts(pooled[...])
    features = feat_n * gain
    feat_len = jnp.sqrt(jnp.sum(features * features, axis=-1, keepdims=True) + EPS)
    img_emb = features / feat_len
    img_ref[...] = img_emb[0:2]
    own_img = pick_row(img_emb, place_ref[0])
    for copy in range(spread_ref.shape[0]):
        spread_ref[copy] = own_img

    text = text_ref[:, 0:width]
    logits = sharp * unstack(
        lax.dot_general(split_stack(img_emb), text, LAST, preferred_element_type=F32)
    ) + shift
    lane = lax.broadcasted_iota(jnp.int32, (16, 128), 1)
    first_lane = jnp.where(lane == 0, 1.0, 0.0).astype(BF16)
    ids = lax.dot_general(
        first_lane, text_ref[:, width:], LAST, preferred_element_type=F32
    )[0:8]
    row = lax.broadcasted_iota(jnp.int32, (8, batch), 0)
    own = jnp.where(row == 0, ids_ref[0], ids_ref[1]).astype(F32)
    sign = jnp.where(ids == own, 1.0, -1.0)
    logit_grad = -LOSS_SCALE * sign * jax.nn.sigmoid(-sign * logits) / batch
    logit_grad = jnp.where(row < 2, logit_grad, 0.0)
    g_img = sharp * unstack(
        jnp.dot(split_stack(logit_grad), text, preferred_element_type=F32)
    )
    g_feat = (
        g_img - img_emb * jnp.sum(img_emb * g_img, axis=-1, keepdims=True)
    ) / feat_len
    g_hidden = norm_back(g_feat, gain, feat_n, feat_s) * (1.0 / PATCHES)
    hidden_ref[...] = g_hidden[0:2]
    g_rows = jnp.concatenate([g_hidden, jnp.zeros_like(g_hidden)], axis=0).astype(BF16)
    down_copy.wait()
    g_act = lax.dot_general(g_rows, down_ref[...], LAST, preferred_element_type=F32)
    g_act_ref[...] = g_act[0:2]
    blocks = [place_ref[5 + i] for i in range(4)]
    slope_copy.wait()
    up_copy.wait()
    back_rows(blocks, slope_ref, pick_row(g_act[0:8], image), up_ref, g_pre, away_ref)


def keep_kernel(place_ref, g_act_ref, up_hbm, slope_hbm, out_ref, g_pre, up_ref, slope_ref, sems):
    image = place_ref[0]
    rows = pl.ds(pl.multiple_of(image * PATCHES, PATCHES), PATCHES)
    slope_copy = pltpu.make_async_copy(slope_hbm.at[rows, :], slope_ref, sems.at[0])
    up_copy = pltpu.make_async_copy(up_hbm, up_ref, sems.at[1])
    slope_copy.start()
    up_copy.start()
    blocks = [place_ref[1 + i] for i in range(4)]
    slope_copy.wait()
    up_copy.wait()
    back_rows(
        blocks, slope_ref, pick_row(g_act_ref[...], image), up_ref, g_pre, out_ref
    )


def loss_and_away(place, scale, ids, pooled, gain, text, w_down, up_t, slope, copies):
    units, width = up_t.shape
    return pl.pallas_call(
        loss_kernel,
        in_specs=[SMEM] * 3 + [VMEM] * 3 + [HBM] * 3,
        out_shape=[
            jax.ShapeDtypeStruct((2, width), F32),
            jax.ShapeDtypeStruct((copies, 1, width), F32),
            jax.ShapeDtypeStruct((2, width), F32),
            jax.ShapeDtypeStruct((2, units), F32),
            jax.ShapeDtypeStruct((PATCHES, width), BF16),
        ],
        scratch_shapes=[
            pltpu.VMEM((8, width), F32),
            pltpu.VMEM((PATCHES, units), BF16),
            pltpu.VMEM((units, width), BF16),
            pltpu.VMEM((units, width), BF16),
            pltpu.VMEM((PATCHES, units), F32),
            pltpu.SemaphoreType.DMA((3,)),
        ],
        compiler_params=LARGE,
        cost_estimate=pl.CostEstimate(
            flops=2 * PATCHES * width * units,
            bytes_accessed=6 * units * width + 4 * PATCHES * units,
            transcendentals=0,
        ),
        name="loss_and_away",
    )(place, scale, ids, pooled, gain, text, w_down, up_t, slope)


def keep_rows(place, g_act, up_t, slope):
    units, width = up_t.shape
    return pl.pallas_call(
        keep_kernel,
        in_specs=[SMEM, VMEM, HBM, HBM],
        out_shape=jax.ShapeDtypeStruct((PATCHES, width), BF16),
        scratch_shapes=[
            pltpu.VMEM((PATCHES, units), BF16),
            pltpu.VMEM((units, width), BF16),
            pltpu.VMEM((PATCHES, units), F32),
            pltpu.SemaphoreType.DMA((2,)),
        ],
        compiler_params=LARGE,
        cost_estimate=pl.CostEstimate(
            flops=2 * PATCHES * width * units,
            bytes_accessed=4 * units * width + 4 * PATCHES * units,
            transcendentals=0,
        ),
        name="keep_rows",
    )(place, g_act, up_t, slope)


def finish_kernel(
    place_ref, keep_ref, other_ref, one_ref, two_ref, x_ref, hidden_ref, gain_ref, out_ref
):
    g_normed = keep_ref[...].astype(F32) + other_ref[...].astype(F32)
    g_normed = g_normed + one_ref[...].astype(F32) + two_ref[...].astype(F32)
    normed, inverse = norm_parts(x_ref[...].astype(F32))
    grad = norm_back(g_normed, gain_ref[...][None, :], normed, inverse)
    out_ref[...] = (grad + pick_row(hidden_ref[...], place_ref[0])).astype(BF16)


def finish(place, keep, other, got_one, got_two, patches, g_hidden, ln_gain):
    width = patches.shape[1]
    block = lambda index: pl.BlockSpec((BLOCK, width), index)
    return pl.pallas_call(
        finish_kernel,
        grid_spec=pltpu.PrefetchScalarGridSpec(
            num_scalar_prefetch=1,
            grid=(1,),
            in_specs=[
                block(lambda i, place: (3, 0)),
                block(lambda i, place: (3, 0)),
                block(lambda i, place: (1, 0)),
                block(lambda i, place: (0, 0)),
                block(lambda i, place: (place[0] * (PATCHES // BLOCK) + place[4], 0)),
                pl.BlockSpec((2, width), lambda i, place: (0, 0)),
                pl.BlockSpec((width,), lambda i, place: (0,)),
            ],
            out_specs=block(lambda i, place: (0, 0)),
        ),
        out_shape=jax.ShapeDtypeStruct((BLOCK, width), BF16),
        compiler_params=SMALL,
        name="finish",
    )(place, keep, other, got_one, got_two, patches, g_hidden, ln_gain)


def place_kernel(place_ref, own, two, one, far, near, rest, out_ref):
    core = place_ref[0]
    low, high = slice(0, BLOCK), slice(BLOCK, 2 * BLOCK)
    moves = [
        (far, low, core, place_ref[1]),
        (one, low, core, place_ref[2]),
        (two, low, core, place_ref[3]),
        (own, low, core, place_ref[4]),
        (rest, high, 1 - core, place_ref[5]),
        (rest, low, 1 - core, place_ref[6]),
        (near, high, 1 - core, place_ref[7]),
        (near, low, 1 - core, place_ref[8]),
    ]
    for ref, rows, image, block in moves:
        start = pl.multiple_of(image * PATCHES + block * BLOCK, BLOCK)
        out_ref[pl.ds(start, BLOCK), :] = ref[rows, :]


def put_in_place(place, pieces, tokens):
    width = pieces[0].shape[1]
    return pl.pallas_call(
        place_kernel,
        in_specs=[SMEM] + [VMEM] * 6,
        out_shape=jax.ShapeDtypeStruct((tokens, width), BF16),
        compiler_params=SMALL,
        name="put_in_place",
    )(place, *pieces)


def swap(value, axis, partner):
    size = lax.axis_size(axis)
    return lax.ppermute(value, axis, [(i, partner(i)) for i in range(size)])


def swap_core(value):
    return swap(value, "tensor", lambda i: i ^ 1)


def step_one(i):
    return i ^ 2 if i % 2 == 0 else (3 - i // 2) * 2 + 1


def step_two(i):
    return (3 - i // 2) * 2 if i % 2 == 0 else i ^ 2


def exchange(copies, groups):
    return lax.all_to_all(
        copies, "dp", split_axis=0, concat_axis=0, axis_index_groups=groups
    )


def spread(rows, groups):
    copies = jnp.broadcast_to(rows[None], (len(groups[0]),) + rows.shape)
    return exchange(copies, groups)


def on_device(
    patches,
    ln_gain,
    w_up,
    b_up,
    w_down,
    b_down,
    head_gain,
    text_feats,
    pair_ids,
    log_sharpness,
    pairwise_logit_shift,
):
    width = text_feats.shape[1]
    batch = text_feats.shape[0] * lax.axis_size("dp")
    position = lax.axis_index("tensor")
    core = position % 2
    ring = position // 2
    u = ((ring == 1) | (ring == 2)).astype(jnp.int32)
    v = (ring >= 2).astype(jnp.int32)
    one, two = jnp.where(core == 0, u, v), jnp.where(core == 0, v, u)

    def order(hi, lo):
        return [3 - 2 * hi - lo, 2 - 2 * hi + lo, 2 * hi + 1 - lo, 2 * hi + lo]

    place = jnp.stack([core] + order(one, two) + order(two, one)).astype(jnp.int32)

    count = lax.axis_size("dp")
    side = math.isqrt(count)
    along_y = [[y * side + k for y in range(side)] for k in range(side)]
    along_xz = [[y * side + k for k in range(side)] for y in range(side)]

    packed, unit_text, text_len = pack_text(pair_ids, text_feats, side)
    text_len = text_len[:, :1]
    text_own = unit_text.astype(BF16)
    some_text = exchange(packed, along_y).reshape(2 * side, -1)

    up_t = w_up.T
    slope, part = forward(
        patches, ln_gain, up_t, b_up, w_down, b_down, lax.axis_size("tensor")
    )
    some_text, part = lax.optimization_barrier((some_text, part))
    text_all = spread(some_text, along_xz).reshape(batch, -1)
    pooled = lax.psum(part, "tensor")

    sharp = jnp.exp(log_sharpness[0])
    shift = pairwise_logit_shift[0]
    img_emb, img_copies, g_hidden, g_act, away = loss_and_away(
        place,
        jnp.stack([sharp, shift]),
        pair_ids,
        pooled,
        head_gain,
        text_all,
        w_down,
        up_t,
        slope,
        side,
    )

    other = swap_core(away)
    keep = keep_rows(place, g_act, up_t, slope)

    def both(start, count):
        rows = slice(start, start + count)
        return keep[rows].astype(F32) + other[rows].astype(F32)

    send_one = both(0, 128).astype(BF16)
    got_one = swap(send_one, "tensor", step_one)
    send_two = (both(128, 64) + got_one[:64].astype(F32)).astype(BF16)
    got_two = swap(send_two, "tensor", step_two)
    done = finish(place, keep, other, got_one, got_two, patches, g_hidden, ln_gain)

    from_two = swap(done, "tensor", step_two)
    from_one = swap(done, "tensor", step_one)
    far = swap(from_two, "tensor", step_one)
    near = swap_core(jnp.concatenate([done, from_two]))
    rest = swap_core(jnp.concatenate([from_one, far]))
    grad_patches = put_in_place(
        place, (done, from_two, from_one, far, near, rest), patches.shape[0]
    )

    img_copies, _ = lax.optimization_barrier((img_copies, send_one))
    some_img = exchange(img_copies, along_y).reshape(side, width)
    some_img, _ = lax.optimization_barrier((some_img, send_two))
    img_all = spread(some_img, along_xz).reshape(count, width)
    img_all, _ = lax.optimization_barrier((img_all, done))
    ids_all = text_all[:, width].astype(jnp.int32).reshape(count, 2)
    ids_all = jnp.where(core == 0, ids_all[:, 0], ids_all[:, 1])
    logits = sharp * jnp.dot(text_own.astype(F32), img_all.T, precision=HIGH) + shift
    sign = jnp.where(pair_ids[:, None] == ids_all[None, :], 1.0, -1.0)
    logit_grad = -LOSS_SCALE * sign * jax.nn.sigmoid(-sign * logits) / batch
    g_text = sharp * jnp.dot(logit_grad, img_all, precision=HIGH)
    g_text = g_text + swap_core(g_text)
    grad_text = (
        g_text - unit_text * jnp.sum(unit_text * g_text, axis=-1, keepdims=True)
    ) / text_len
    return grad_patches, grad_text


def solution(mesh):
    in_specs = (
        P("dp", None),
        P(),
        P(None, "tensor"),
        P("tensor"),
        P("tensor", None),
        P(),
        P(),
        P("dp", None),
        P("dp"),
        P(),
        P(),
    )
    out_specs = (P("dp", None), P("dp", None))
    return jax.shard_map(
        on_device, mesh=mesh, in_specs=in_specs, out_specs=out_specs, check_vma=False
    )
```

```python
import functools
import math

import jax
import jax.numpy as jnp
from jax import lax
from jax.experimental import pallas as pl
from jax.experimental.pallas import tpu as pltpu
from jax.sharding import PartitionSpec as P

PATCHES = 256
BLOCK = 64
EPS = 1e-06
LOSS_SCALE = 131072.0
F32 = jnp.float32
BF16 = jnp.bfloat16
LAST = (((1,), (1,)), ((), ()))
SMEM = pl.BlockSpec(memory_space=pltpu.SMEM)
HBM = pl.BlockSpec(memory_space=pltpu.HBM)
VMEM = pl.BlockSpec(memory_space=pltpu.VMEM)
LARGE = pltpu.CompilerParams(vmem_limit_bytes=60 * 1024 * 1024)
SMALL = pltpu.CompilerParams(vmem_limit_bytes=16 * 1024 * 1024)


def places(position):
    core, ring = position & 1, position >> 1
    u, v = (ring ^ (ring >> 1)) & 1, ring >> 1
    swap = core * (u ^ v)
    return core, u ^ swap, v ^ swap


def order(one, two):
    return [3 - 2 * one - two, 2 - 2 * one + two, 2 * one + 1 - two, 2 * one + two]


def norm_parts(values):
    centre = values - jnp.mean(values, axis=-1, keepdims=True)
    inverse = lax.rsqrt(jnp.mean(centre * centre, axis=-1, keepdims=True) + EPS)
    return centre * inverse, inverse


def norm_back(grad_out, gain, normed, inverse):
    scaled = grad_out * gain
    return inverse * (
        scaled
        - jnp.mean(scaled, axis=-1, keepdims=True)
        - normed * jnp.mean(scaled * normed, axis=-1, keepdims=True)
    )


def split_stack(values):
    high = values.astype(BF16).astype(F32)
    rest = values - high
    mid = rest.astype(BF16).astype(F32)
    low = rest - mid
    return jnp.concatenate([high, mid, low, jnp.zeros_like(high)], axis=0).astype(BF16)


def unstack(sums):
    return (sums[0:8] + sums[8:16]) + sums[16:24]


def image_features(pooled_ref, gain):
    rows = pooled_ref[...]
    pooled = jnp.concatenate([rows] * 4, axis=0)
    feat_n, feat_s = norm_parts(pooled)
    features = feat_n * gain
    feat_len = jnp.sqrt(jnp.sum(features * features, axis=-1, keepdims=True) + EPS)
    return feat_n, feat_s, feat_len, features / feat_len


def pack_kernel(ids_ref, text_ref, pooled_ref, gain_ref, pack_ref, unit_ref, len_ref):
    text = text_ref[...].astype(F32)
    length = jnp.sqrt(jnp.sum(text * text, axis=-1, keepdims=True) + EPS)
    unit = text / length
    unit_ref[...] = unit
    len_ref[...] = jnp.broadcast_to(length, len_ref.shape)
    row = lax.broadcasted_iota(jnp.int32, (2, 128), 0)
    lane = lax.broadcasted_iota(jnp.int32, (2, 128), 1)
    ids = jnp.where(row == 0, ids_ref[0], ids_ref[1])
    ids = jnp.where(lane == 0, ids, 0).astype(F32)
    img_emb = image_features(pooled_ref, gain_ref[...][None, :])[3][0:2]
    packed = jnp.concatenate([unit, ids, img_emb], axis=1).astype(BF16)
    for copy in range(pack_ref.shape[0]):
        pack_ref[copy] = packed


def pack(pair_ids, text_feats, pooled, head_gain, copies):
    width = text_feats.shape[1]
    return pl.pallas_call(
        pack_kernel,
        in_specs=[SMEM] + [VMEM] * 3,
        out_shape=[
            jax.ShapeDtypeStruct((copies, 2, 2 * width + 128), BF16),
            jax.ShapeDtypeStruct((2, width), F32),
            jax.ShapeDtypeStruct((2, 128), F32),
        ],
        compiler_params=SMALL,
        cost_estimate=pl.CostEstimate(
            flops=30_000_000_000, bytes_accessed=100_000, transcendentals=0
        ),
        name="pack",
    )(pair_ids, text_feats, pooled, head_gain)


def forward_kernel(
    n_tensor, x_ref, gain_ref, bias_ref, b_down_ref, up_hbm, down_hbm,
    slope_ref, part_ref, up_ref, down_ref, act_sum, x_sum, sems,
):
    step = pl.program_id(0)
    image = step // 2
    up_copy = pltpu.make_async_copy(up_hbm, up_ref, sems.at[0])
    down_copy = pltpu.make_async_copy(down_hbm, down_ref, sems.at[1])

    @pl.when(step == 0)
    def _():
        up_copy.start()
        act_sum[...] = jnp.zeros_like(act_sum)
        x_sum[...] = jnp.zeros_like(x_sum)

    x = x_ref[...].astype(F32)
    normed, _ = norm_parts(x)
    normed = (normed * gain_ref[...][None, :]).astype(BF16)

    @pl.when(step == 0)
    def _():
        up_copy.wait()
        down_copy.start()

    pre = lax.dot_general(normed, up_ref[...], LAST, preferred_element_type=F32)
    pre = pre + bias_ref[...][None, :]
    root = math.sqrt(2.0 / math.pi)
    square = pre * pre
    tanh = jnp.tanh(root * (pre + 0.044715 * (square * pre)))
    half = 0.5 * (1.0 + tanh)
    act = (pre * half).astype(BF16).astype(F32)
    slope_ref[...] = half + (0.5 * root) * pre * (1.0 - tanh * tanh) * (
        1.0 + (3.0 * 0.044715) * square
    )

    def add(total, values):
        row = lax.broadcasted_iota(jnp.int32, total.shape, 0)
        sums = jnp.sum(values, axis=0, keepdims=True)
        total[...] += jnp.where(row == image, sums, 0.0)

    add(act_sum, act)
    add(x_sum, x)

    @pl.when(step == pl.num_programs(0) - 1)
    def _():
        down_copy.wait()
        stack = split_stack(act_sum[...] * (1.0 / PATCHES))
        mlp = unstack(jnp.dot(stack, down_ref[...], preferred_element_type=F32))
        rest = x_sum[...] * (1.0 / PATCHES) + b_down_ref[...][None, :]
        part_ref[...] = (mlp + rest * (1.0 / n_tensor))[0:2]


def forward(patches, ln_gain, up_t, b_up, w_down, b_down, n_tensor):
    tokens, width = patches.shape
    units = up_t.shape[0]
    rows = 128
    vector = lambda size: pl.BlockSpec((size,), lambda i: (0,))
    return pl.pallas_call(
        functools.partial(forward_kernel, n_tensor),
        grid=(tokens // rows,),
        in_specs=[
            pl.BlockSpec((rows, width), lambda i: (i, 0)),
            vector(width),
            vector(units),
            vector(width),
            HBM,
            HBM,
        ],
        out_specs=[
            pl.BlockSpec((rows, units), lambda i: (i, 0)),
            pl.BlockSpec((2, width), lambda i: (0, 0)),
        ],
        out_shape=[
            jax.ShapeDtypeStruct((tokens, units), F32),
            jax.ShapeDtypeStruct((2, width), F32),
        ],
        scratch_shapes=[
            pltpu.VMEM((units, width), BF16),
            pltpu.VMEM((units, width), BF16),
            pltpu.VMEM((8, units), F32),
            pltpu.VMEM((8, width), F32),
            pltpu.SemaphoreType.DMA((2,)),
        ],
        compiler_params=LARGE,
        cost_estimate=pl.CostEstimate(
            flops=2 * tokens * width * units,
            bytes_accessed=2 * tokens * width + 4 * units * width + 4 * tokens * units,
            transcendentals=tokens * units,
        ),
        name="forward",
    )(patches, ln_gain, b_up, b_down, up_t, w_down)


def pick_row(rows, index):
    row = lax.broadcasted_iota(jnp.int32, rows.shape, 0)
    return jnp.sum(jnp.where(row == index, rows, 0.0), axis=0, keepdims=True)


def pair_grad(queries, keys, ids_ref, id_columns, sharp, shift):
    batch = keys.shape[0]
    logits = sharp * unstack(
        lax.dot_general(split_stack(queries), keys, LAST, preferred_element_type=F32)
    ) + shift
    lane = lax.broadcasted_iota(jnp.int32, (16, 128), 1)
    first_lane = jnp.where(lane == 0, 1.0, 0.0).astype(BF16)
    ids = lax.dot_general(first_lane, id_columns, LAST, preferred_element_type=F32)[0:8]
    row = lax.broadcasted_iota(jnp.int32, (8, batch), 0)
    own = jnp.where(row == 0, ids_ref[0], ids_ref[1]).astype(F32)
    sign = jnp.where(ids == own, 1.0, -1.0)
    logit_grad = -LOSS_SCALE * sign * jax.nn.sigmoid(-sign * logits) / batch
    logit_grad = jnp.where(row < 2, logit_grad, 0.0)
    return sharp * unstack(
        jnp.dot(split_stack(logit_grad), keys, preferred_element_type=F32)
    )


def scalars(sharp_ref, shift_ref):
    return jnp.exp(jnp.full((8, 1), sharp_ref[0], F32)), shift_ref[0]


def loss_kernel(
    place_ref, sharp_ref, shift_ref, ids_ref, pooled_ref, gain_ref, rows_ref, down_ref,
    up_ref, slope_ref, hidden_ref, away_ref, keep_ref, g_pre,
):
    width = pooled_ref.shape[1]
    core, one, two = places(place_ref[0])
    gain = gain_ref[...][None, :]
    feat_n, feat_s, feat_len, img_emb = image_features(pooled_ref, gain)
    g_img = pair_grad(
        img_emb, rows_ref[:, 0:width], ids_ref, rows_ref[:, width : width + 128],
        *scalars(sharp_ref, shift_ref),
    )
    g_feat = (
        g_img - img_emb * jnp.sum(img_emb * g_img, axis=-1, keepdims=True)
    ) / feat_len
    g_hidden = norm_back(g_feat, gain, feat_n, feat_s) * (1.0 / PATCHES)
    hidden_ref[...] = g_hidden[0:2]
    g_rows = jnp.concatenate([g_hidden, jnp.zeros_like(g_hidden)], axis=0).astype(BF16)
    g_act = lax.dot_general(g_rows, down_ref[...], LAST, preferred_element_type=F32)[0:8]
    for image, blocks, out_ref in (
        (1 - core, order(two, one), away_ref),
        (core, order(one, two), keep_ref),
    ):
        row = pick_row(g_act, image)
        for spot, block in enumerate(blocks):
            start = pl.multiple_of(image * PATCHES + block * BLOCK, BLOCK)
            g_pre[spot * BLOCK : (spot + 1) * BLOCK, :] = (
                slope_ref[pl.ds(start, BLOCK), :] * row
            ).astype(BF16)
        out_ref[...] = jnp.dot(
            g_pre[...], up_ref[...], preferred_element_type=F32
        ).astype(BF16)


def loss_and_back(place, sharp, shift, ids, pooled, gain, rows, w_down, up_t, slope):
    units, width = up_t.shape
    return pl.pallas_call(
        loss_kernel,
        in_specs=[SMEM] * 4 + [VMEM] * 6,
        out_shape=[
            jax.ShapeDtypeStruct((2, width), F32),
            jax.ShapeDtypeStruct((PATCHES, width), BF16),
            jax.ShapeDtypeStruct((PATCHES, width), BF16),
        ],
        scratch_shapes=[pltpu.VMEM((PATCHES, units), BF16)],
        compiler_params=SMALL,
        cost_estimate=pl.CostEstimate(
            flops=4 * PATCHES * width * units,
            bytes_accessed=6 * units * width + 8 * PATCHES * units,
            transcendentals=0,
        ),
        name="loss_and_back",
    )(place, sharp, shift, ids, pooled, gain, rows, w_down, up_t, slope)


def text_kernel(sharp_ref, shift_ref, ids_ref, unit_ref, len_ref, rows_ref, out_ref):
    width = unit_ref.shape[1]
    unit = unit_ref[...]
    queries = jnp.concatenate([unit] * 4, axis=0).astype(BF16).astype(F32)
    g_text = pair_grad(
        queries, rows_ref[:, width + 128 :], ids_ref, rows_ref[:, width : width + 128],
        *scalars(sharp_ref, shift_ref),
    )[0:2]
    along = jnp.sum(unit * g_text, axis=-1, keepdims=True)
    out_ref[...] = (g_text - unit * along) / len_ref[:, 0:1]


def text_grad(sharp, shift, ids, unit, length, rows):
    return pl.pallas_call(
        text_kernel,
        in_specs=[SMEM] * 3 + [VMEM] * 3,
        out_shape=jax.ShapeDtypeStruct(unit.shape, F32),
        compiler_params=SMALL,
        cost_estimate=pl.CostEstimate(
            flops=1_000_000_000, bytes_accessed=600_000, transcendentals=0
        ),
        name="text_grad",
    )(sharp, shift, ids, unit, length, rows)


def finish_kernel(
    place_ref, keep_ref, other_ref, one_ref, two_ref, x_ref, hidden_ref, gain_ref, out_ref
):
    g_normed = keep_ref[...].astype(F32) + other_ref[...].astype(F32)
    g_normed = g_normed + one_ref[...].astype(F32) + two_ref[...].astype(F32)
    normed, inverse = norm_parts(x_ref[...].astype(F32))
    grad = norm_back(g_normed, gain_ref[...][None, :], normed, inverse)
    out_ref[...] = (grad + pick_row(hidden_ref[...], place_ref[0] & 1)).astype(BF16)


def finish(place, keep, other, got_one, got_two, patches, g_hidden, ln_gain):
    width = patches.shape[1]
    block = lambda index: pl.BlockSpec((BLOCK, width), index)

    def own_block(i, place):
        core, one, two = places(place[0])
        return core * (PATCHES // BLOCK) + 2 * one + two, 0

    return pl.pallas_call(
        finish_kernel,
        grid_spec=pltpu.PrefetchScalarGridSpec(
            num_scalar_prefetch=1,
            grid=(1,),
            in_specs=[
                block(lambda i, place: (3, 0)),
                block(lambda i, place: (3, 0)),
                block(lambda i, place: (1, 0)),
                block(lambda i, place: (0, 0)),
                block(own_block),
                pl.BlockSpec((2, width), lambda i, place: (0, 0)),
                pl.BlockSpec((width,), lambda i, place: (0,)),
            ],
            out_specs=block(lambda i, place: (0, 0)),
        ),
        out_shape=jax.ShapeDtypeStruct((BLOCK, width), BF16),
        compiler_params=SMALL,
        name="finish",
    )(place, keep, other, got_one, got_two, patches, g_hidden, ln_gain)


def place_kernel(place_ref, own, two, one, far, near, rest, out_ref):
    core, one_bit, two_bit = places(place_ref[0])
    low, high = slice(0, BLOCK), slice(BLOCK, 2 * BLOCK)
    mine, theirs = order(one_bit, two_bit), order(two_bit, one_bit)
    moves = [
        (far, low, core, mine[0]),
        (one, low, core, mine[1]),
        (two, low, core, mine[2]),
        (own, low, core, mine[3]),
        (rest, high, 1 - core, theirs[0]),
        (rest, low, 1 - core, theirs[1]),
        (near, high, 1 - core, theirs[2]),
        (near, low, 1 - core, theirs[3]),
    ]
    for ref, rows, image, block in moves:
        start = pl.multiple_of(image * PATCHES + block * BLOCK, BLOCK)
        out_ref[pl.ds(start, BLOCK), :] = ref[rows, :]


def put_in_place(place, pieces, tokens):
    width = pieces[0].shape[1]
    return pl.pallas_call(
        place_kernel,
        in_specs=[SMEM] + [VMEM] * 6,
        out_shape=jax.ShapeDtypeStruct((tokens, width), BF16),
        compiler_params=SMALL,
        name="put_in_place",
    )(place, *pieces)


def swap(value, axis, partner):
    size = lax.axis_size(axis)
    return lax.ppermute(value, axis, [(i, partner(i)) for i in range(size)])


def swap_core(value):
    return swap(value, "tensor", lambda i: i ^ 1)


def step_one(i):
    return i ^ 2 if i % 2 == 0 else (3 - i // 2) * 2 + 1


def step_two(i):
    return (3 - i // 2) * 2 if i % 2 == 0 else i ^ 2


def exchange(copies, groups):
    return lax.all_to_all(
        copies, "dp", split_axis=0, concat_axis=0, axis_index_groups=groups
    )


def spread(rows, groups):
    copies = jnp.broadcast_to(rows[None], (len(groups[0]),) + rows.shape)
    return exchange(copies, groups)


def on_device(
    patches,
    ln_gain,
    w_up,
    b_up,
    w_down,
    b_down,
    head_gain,
    text_feats,
    pair_ids,
    log_sharpness,
    pairwise_logit_shift,
):
    batch = text_feats.shape[0] * lax.axis_size("dp")
    place = lax.axis_index("tensor").astype(jnp.int32).reshape(1)

    up_t = w_up.T
    slope, part = forward(
        patches, ln_gain, up_t, b_up, w_down, b_down, lax.axis_size("tensor")
    )
    pooled = part + swap_core(part)
    pooled = pooled + swap(pooled, "tensor", step_one)
    pooled = pooled + swap(pooled, "tensor", step_two)

    side = math.isqrt(lax.axis_size("dp"))
    along_y = [[y * side + k for y in range(side)] for k in range(side)]
    along_xz = [[y * side + k for k in range(side)] for y in range(side)]
    packed, unit_text, text_len = pack(pair_ids, text_feats, pooled, head_gain, side)
    some_rows = exchange(packed, along_y).reshape(2 * side, -1)
    rows = spread(some_rows, along_xz).reshape(batch, -1)

    g_hidden, away, keep = loss_and_back(
        place,
        log_sharpness,
        pairwise_logit_shift,
        pair_ids,
        pooled,
        head_gain,
        rows,
        w_down,
        up_t,
        slope,
    )

    other = swap_core(away)

    def both(start, count):
        rows = slice(start, start + count)
        return keep[rows].astype(F32) + other[rows].astype(F32)

    send_one = both(0, 128).astype(BF16)
    got_one = swap(send_one, "tensor", step_one)
    send_two = (both(128, 64) + got_one[:64].astype(F32)).astype(BF16)
    got_two = swap(send_two, "tensor", step_two)
    done = finish(place, keep, other, got_one, got_two, patches, g_hidden, ln_gain)

    from_two = swap(done, "tensor", step_two)
    from_one = swap(done, "tensor", step_one)
    far = swap(from_two, "tensor", step_one)
    near = swap_core(jnp.concatenate([done, from_two]))
    rest = swap_core(jnp.concatenate([from_one, far]))
    grad_patches = put_in_place(
        place, (done, from_two, from_one, far, near, rest), patches.shape[0]
    )

    rows, _ = lax.optimization_barrier((rows, send_one))
    grad_text = text_grad(
        log_sharpness, pairwise_logit_shift, pair_ids, unit_text, text_len, rows
    )
    return grad_patches, grad_text


def solution(mesh):
    in_specs = (
        P("dp", None),
        P(),
        P(None, "tensor"),
        P("tensor"),
        P("tensor", None),
        P(),
        P(),
        P("dp", None),
        P("dp"),
        P(),
        P(),
    )
    out_specs = (P("dp", None), P("dp", None))
    return jax.shard_map(
        on_device, mesh=mesh, in_specs=in_specs, out_specs=out_specs, check_vma=False
    )
```

```python
import functools
import math

import jax
import jax.numpy as jnp
from jax import lax
from jax.experimental import pallas as pl
from jax.experimental.pallas import tpu as pltpu
from jax.sharding import PartitionSpec as P

PATCHES = 256
BLOCK = 64
EPS = 1e-06
LOSS_SCALE = 131072.0
F32 = jnp.float32
BF16 = jnp.bfloat16
LAST = (((1,), (1,)), ((), ()))
SMEM = pl.BlockSpec(memory_space=pltpu.SMEM)
HBM = pl.BlockSpec(memory_space=pltpu.HBM)
VMEM = pl.BlockSpec(memory_space=pltpu.VMEM)
LARGE = pltpu.CompilerParams(vmem_limit_bytes=60 * 1024 * 1024)
SMALL = pltpu.CompilerParams(vmem_limit_bytes=16 * 1024 * 1024)


def places(position):
    core, ring = position & 1, position >> 1
    u, v = (ring ^ (ring >> 1)) & 1, ring >> 1
    swap = core * (u ^ v)
    return core, u ^ swap, v ^ swap


def order(one, two):
    return [3 - 2 * one - two, 2 - 2 * one + two, 2 * one + 1 - two, 2 * one + two]


def norm_parts(values):
    centre = values - jnp.mean(values, axis=-1, keepdims=True)
    inverse = lax.rsqrt(jnp.mean(centre * centre, axis=-1, keepdims=True) + EPS)
    return centre * inverse, inverse


def norm_back(grad_out, gain, normed, inverse):
    scaled = grad_out * gain
    return inverse * (
        scaled
        - jnp.mean(scaled, axis=-1, keepdims=True)
        - normed * jnp.mean(scaled * normed, axis=-1, keepdims=True)
    )


def split_stack(values):
    high = values.astype(BF16).astype(F32)
    rest = values - high
    mid = rest.astype(BF16).astype(F32)
    low = rest - mid
    return jnp.concatenate([high, mid, low, jnp.zeros_like(high)], axis=0).astype(BF16)


def unstack(sums):
    return (sums[0:8] + sums[8:16]) + sums[16:24]


def image_features(pooled_ref, gain):
    rows = pooled_ref[...]
    pooled = jnp.concatenate([rows] * 4, axis=0)
    feat_n, feat_s = norm_parts(pooled)
    features = feat_n * gain
    feat_len = jnp.sqrt(jnp.sum(features * features, axis=-1, keepdims=True) + EPS)
    return feat_n, feat_s, feat_len, features / feat_len


def pack_kernel(ids_ref, text_ref, pack_ref, unit_ref, len_ref):
    text = text_ref[...].astype(F32)
    length = jnp.sqrt(jnp.sum(text * text, axis=-1, keepdims=True) + EPS)
    unit = text / length
    unit_ref[...] = unit
    len_ref[...] = jnp.broadcast_to(length, len_ref.shape)
    row = lax.broadcasted_iota(jnp.int32, (2, 128), 0)
    lane = lax.broadcasted_iota(jnp.int32, (2, 128), 1)
    ids = jnp.where(row == 0, ids_ref[0], ids_ref[1])
    ids = jnp.where(lane == 0, ids, 0).astype(F32)
    packed = jnp.concatenate([unit, ids], axis=1).astype(BF16)
    for copy in range(pack_ref.shape[0]):
        pack_ref[copy] = packed


def pack(pair_ids, text_feats, copies):
    width = text_feats.shape[1]
    return pl.pallas_call(
        pack_kernel,
        in_specs=[SMEM, VMEM],
        out_shape=[
            jax.ShapeDtypeStruct((copies, 2, width + 128), BF16),
            jax.ShapeDtypeStruct((2, width), F32),
            jax.ShapeDtypeStruct((2, 128), F32),
        ],
        compiler_params=SMALL,
        name="pack",
    )(pair_ids, text_feats)


def forward_kernel(
    n_tensor, x_ref, gain_ref, bias_ref, b_down_ref, up_hbm, down_hbm,
    slope_ref, part_ref, up_ref, down_ref, act_sum, x_sum, sems,
):
    step = pl.program_id(0)
    image = step // 2
    third = x_ref.shape[1] // 3

    def copies(source, target, first):
        parts = [pl.ds(part * third, third) for part in range(3)]
        return [
            pltpu.make_async_copy(source.at[:, part], target.at[:, part], sems.at[first + i])
            for i, part in enumerate(parts)
        ]

    up_copies = copies(up_hbm, up_ref, 0)
    down_copies = copies(down_hbm, down_ref, 3)

    @pl.when(step == 0)
    def _():
        for copy in up_copies:
            copy.start()
        act_sum[...] = jnp.zeros_like(act_sum)
        x_sum[...] = jnp.zeros_like(x_sum)

    x = x_ref[...].astype(F32)
    normed, _ = norm_parts(x)
    normed = (normed * gain_ref[...][None, :]).astype(BF16)

    @pl.when(step == 0)
    def _():
        for copy in up_copies:
            copy.wait()
        for copy in down_copies:
            copy.start()

    pre = lax.dot_general(normed, up_ref[...], LAST, preferred_element_type=F32)
    pre = pre + bias_ref[...][None, :]
    root = math.sqrt(2.0 / math.pi)
    square = pre * pre
    tanh = jnp.tanh(root * (pre + 0.044715 * (square * pre)))
    half = 0.5 * (1.0 + tanh)
    act = (pre * half).astype(BF16).astype(F32)
    slope = half + (0.5 * root) * pre * (1.0 - tanh * tanh) * (
        1.0 + (3.0 * 0.044715) * square
    )
    slope_ref[...] = slope.astype(BF16)

    def add(total, values):
        row = lax.broadcasted_iota(jnp.int32, total.shape, 0)
        sums = jnp.sum(values, axis=0, keepdims=True)
        total[...] += jnp.where(row == image, sums, 0.0)

    add(act_sum, act)
    add(x_sum, x)

    @pl.when(step == pl.num_programs(0) - 1)
    def _():
        for copy in down_copies:
            copy.wait()
        stack = split_stack(act_sum[...] * (1.0 / PATCHES))
        mlp = unstack(jnp.dot(stack, down_ref[...], preferred_element_type=F32))
        rest = x_sum[...] * (1.0 / PATCHES) + b_down_ref[...][None, :]
        part_ref[...] = (mlp + rest * (1.0 / n_tensor))[0:2]


def forward(patches, ln_gain, up_t, b_up, w_down, b_down, n_tensor):
    tokens, width = patches.shape
    units = up_t.shape[0]
    rows = 128
    vector = lambda size: pl.BlockSpec((size,), lambda i: (0,))
    return pl.pallas_call(
        functools.partial(forward_kernel, n_tensor),
        grid=(tokens // rows,),
        in_specs=[
            pl.BlockSpec((rows, width), lambda i: (i, 0)),
            vector(width),
            vector(units),
            vector(width),
            HBM,
            HBM,
        ],
        out_specs=[
            pl.BlockSpec((rows, units), lambda i: (i, 0)),
            pl.BlockSpec((2, width), lambda i: (0, 0)),
        ],
        out_shape=[
            jax.ShapeDtypeStruct((tokens, units), BF16),
            jax.ShapeDtypeStruct((2, width), F32),
        ],
        scratch_shapes=[
            pltpu.VMEM((units, width), BF16),
            pltpu.VMEM((units, width), BF16),
            pltpu.VMEM((8, units), F32),
            pltpu.VMEM((8, width), F32),
            pltpu.SemaphoreType.DMA((6,)),
        ],
        compiler_params=LARGE,
        cost_estimate=pl.CostEstimate(
            flops=2 * tokens * width * units,
            bytes_accessed=2 * tokens * width + 4 * units * width + 4 * tokens * units,
            transcendentals=tokens * units,
        ),
        name="forward",
    )(patches, ln_gain, b_up, b_down, up_t, w_down)


def pick_row(rows, index):
    row = lax.broadcasted_iota(jnp.int32, rows.shape, 0)
    return jnp.sum(jnp.where(row == index, rows, 0.0), axis=0, keepdims=True)


def image_features(rows, gain):
    feat_n, feat_s = norm_parts(jnp.concatenate([rows] * 4, axis=0))
    features = feat_n * gain
    feat_len = jnp.sqrt(jnp.sum(features * features, axis=-1, keepdims=True) + EPS)
    return feat_n, feat_s, feat_len, features / feat_len


def pair_grad(queries, keys, ids_ref, id_columns, sharp, shift):
    batch = keys.shape[0]
    logits = sharp * unstack(
        lax.dot_general(split_stack(queries), keys, LAST, preferred_element_type=F32)
    ) + shift
    lane = lax.broadcasted_iota(jnp.int32, (16, 128), 1)
    first_lane = jnp.where(lane == 0, 1.0, 0.0).astype(BF16)
    ids = lax.dot_general(first_lane, id_columns, LAST, preferred_element_type=F32)[0:8]
    row = lax.broadcasted_iota(jnp.int32, (8, batch), 0)
    own = jnp.where(row == 0, ids_ref[0], ids_ref[1]).astype(F32)
    sign = jnp.where(ids == own, 1.0, -1.0)
    logit_grad = -LOSS_SCALE * sign * jax.nn.sigmoid(-sign * logits) / batch
    logit_grad = jnp.where(row < 2, logit_grad, 0.0)
    return sharp * unstack(
        jnp.dot(split_stack(logit_grad), keys, preferred_element_type=F32)
    )


def scalars(sharp_ref, shift_ref):
    return jnp.exp(jnp.full((8, 1), sharp_ref[0], F32)), shift_ref[0]


def loss_kernel(
    place_ref, sharp_ref, shift_ref, ids_ref, pooled_ref, gain_ref, rows_ref, down_ref,
    up_ref, slope_ref, img_ref, hidden_ref, away_ref, keep_ref, g_pre,
):
    width = gain_ref.shape[0]
    core, one, two = places(place_ref[0])
    gain = gain_ref[...][None, :]
    feat_n, feat_s, feat_len, img_emb = image_features(pooled_ref[...], gain)
    for copy in range(img_ref.shape[0]):
        img_ref[copy] = img_emb[0:2].astype(BF16)
    g_img = pair_grad(
        img_emb, rows_ref[:, 0:width], ids_ref, rows_ref[:, width : width + 128],
        *scalars(sharp_ref, shift_ref),
    )
    g_feat = (
        g_img - img_emb * jnp.sum(img_emb * g_img, axis=-1, keepdims=True)
    ) / feat_len
    g_hidden = norm_back(g_feat, gain, feat_n, feat_s) * (1.0 / PATCHES)
    hidden_ref[...] = g_hidden[0:2]
    g_rows = jnp.concatenate([g_hidden, jnp.zeros_like(g_hidden)], axis=0).astype(BF16)
    g_act = lax.dot_general(g_rows, down_ref[...], LAST, preferred_element_type=F32)[0:8]
    for image, blocks, out_ref in (
        (1 - core, order(two, one), away_ref),
        (core, order(one, two), keep_ref),
    ):
        row = pick_row(g_act, image)
        for spot, block in enumerate(blocks):
            start = pl.multiple_of(image * PATCHES + block * BLOCK, BLOCK)
            g_pre[spot * BLOCK : (spot + 1) * BLOCK, :] = (
                slope_ref[pl.ds(start, BLOCK), :].astype(F32) * row
            ).astype(BF16)
        out_ref[...] = jnp.dot(
            g_pre[...], up_ref[...], preferred_element_type=F32
        ).astype(BF16)


def loss_and_back(
    place, sharp, shift, ids, pooled, gain, rows, w_down, up_t, slope, copies
):
    units, width = up_t.shape
    return pl.pallas_call(
        loss_kernel,
        in_specs=[SMEM] * 4 + [VMEM] * 6,
        out_shape=[
            jax.ShapeDtypeStruct((copies, 2, width), BF16),
            jax.ShapeDtypeStruct((2, width), F32),
            jax.ShapeDtypeStruct((PATCHES, width), BF16),
            jax.ShapeDtypeStruct((PATCHES, width), BF16),
        ],
        scratch_shapes=[pltpu.VMEM((PATCHES, units), BF16)],
        compiler_params=SMALL,
        cost_estimate=pl.CostEstimate(
            flops=4 * PATCHES * width * units,
            bytes_accessed=6 * units * width + 8 * PATCHES * units,
            transcendentals=0,
        ),
        name="loss_and_back",
    )(place, sharp, shift, ids, pooled, gain, rows, w_down, up_t, slope)


def text_kernel(
    sharp_ref, shift_ref, ids_ref, unit_ref, len_ref, img_ref, rows_ref, out_ref
):
    width = unit_ref.shape[1]
    unit = unit_ref[...]
    queries = jnp.concatenate([unit] * 4, axis=0).astype(BF16).astype(F32)
    g_text = pair_grad(
        queries, img_ref[...], ids_ref, rows_ref[:, width : width + 128],
        *scalars(sharp_ref, shift_ref),
    )[0:2]
    along = jnp.sum(unit * g_text, axis=-1, keepdims=True)
    out_ref[...] = (g_text - unit * along) / len_ref[:, 0:1]


def text_grad(sharp, shift, ids, unit, length, images, rows):
    return pl.pallas_call(
        text_kernel,
        in_specs=[SMEM] * 3 + [VMEM] * 4,
        out_shape=jax.ShapeDtypeStruct(unit.shape, F32),
        compiler_params=SMALL,
        cost_estimate=pl.CostEstimate(
            flops=1_000_000_000, bytes_accessed=600_000, transcendentals=0
        ),
        name="text_grad",
    )(sharp, shift, ids, unit, length, images, rows)


def finish_kernel(
    place_ref, keep_ref, other_ref, one_ref, two_ref, x_ref, hidden_ref, gain_ref, out_ref
):
    g_normed = keep_ref[...].astype(F32) + other_ref[...].astype(F32)
    g_normed = g_normed + one_ref[...].astype(F32) + two_ref[...].astype(F32)
    normed, inverse = norm_parts(x_ref[...].astype(F32))
    grad = norm_back(g_normed, gain_ref[...][None, :], normed, inverse)
    out_ref[...] = (grad + pick_row(hidden_ref[...], place_ref[0] & 1)).astype(BF16)


def finish(place, keep, other, got_one, got_two, patches, g_hidden, ln_gain):
    width = patches.shape[1]
    block = lambda index: pl.BlockSpec((BLOCK, width), index)

    def own_block(i, place):
        core, one, two = places(place[0])
        return core * (PATCHES // BLOCK) + 2 * one + two, 0

    return pl.pallas_call(
        finish_kernel,
        grid_spec=pltpu.PrefetchScalarGridSpec(
            num_scalar_prefetch=1,
            grid=(1,),
            in_specs=[
                block(lambda i, place: (3, 0)),
                block(lambda i, place: (3, 0)),
                block(lambda i, place: (1, 0)),
                block(lambda i, place: (0, 0)),
                block(own_block),
                pl.BlockSpec((2, width), lambda i, place: (0, 0)),
                pl.BlockSpec((width,), lambda i, place: (0,)),
            ],
            out_specs=block(lambda i, place: (0, 0)),
        ),
        out_shape=jax.ShapeDtypeStruct((BLOCK, width), BF16),
        compiler_params=SMALL,
        name="finish",
    )(place, keep, other, got_one, got_two, patches, g_hidden, ln_gain)


def place_kernel(place_ref, own, two, one, far, near, rest, out_ref):
    core, one_bit, two_bit = places(place_ref[0])
    low, high = slice(0, BLOCK), slice(BLOCK, 2 * BLOCK)
    mine, theirs = order(one_bit, two_bit), order(two_bit, one_bit)
    moves = [
        (far, low, core, mine[0]),
        (one, low, core, mine[1]),
        (two, low, core, mine[2]),
        (own, low, core, mine[3]),
        (rest, high, 1 - core, theirs[0]),
        (rest, low, 1 - core, theirs[1]),
        (near, high, 1 - core, theirs[2]),
        (near, low, 1 - core, theirs[3]),
    ]
    for ref, rows, image, block in moves:
        start = pl.multiple_of(image * PATCHES + block * BLOCK, BLOCK)
        out_ref[pl.ds(start, BLOCK), :] = ref[rows, :]


def put_in_place(place, pieces, tokens):
    width = pieces[0].shape[1]
    return pl.pallas_call(
        place_kernel,
        in_specs=[SMEM] + [VMEM] * 6,
        out_shape=jax.ShapeDtypeStruct((tokens, width), BF16),
        compiler_params=SMALL,
        name="put_in_place",
    )(place, *pieces)


def swap(value, axis, partner):
    size = lax.axis_size(axis)
    return lax.ppermute(value, axis, [(i, partner(i)) for i in range(size)])


def swap_core(value):
    return swap(value, "tensor", lambda i: i ^ 1)


def step_one(i):
    return i ^ 2 if i % 2 == 0 else (3 - i // 2) * 2 + 1


def step_two(i):
    return (3 - i // 2) * 2 if i % 2 == 0 else i ^ 2


def exchange(copies, groups):
    return lax.all_to_all(
        copies, "dp", split_axis=0, concat_axis=0, axis_index_groups=groups
    )


def spread(rows, groups):
    copies = jnp.broadcast_to(rows[None], (len(groups[0]),) + rows.shape)
    return exchange(copies, groups)


def on_device(
    patches,
    ln_gain,
    w_up,
    b_up,
    w_down,
    b_down,
    head_gain,
    text_feats,
    pair_ids,
    log_sharpness,
    pairwise_logit_shift,
):
    batch = text_feats.shape[0] * lax.axis_size("dp")
    place = lax.axis_index("tensor").astype(jnp.int32).reshape(1)

    side = math.isqrt(lax.axis_size("dp"))
    along_y = [[y * side + k for y in range(side)] for k in range(side)]
    along_xz = [[y * side + k for k in range(side)] for y in range(side)]
    packed, unit_text, text_len = pack(pair_ids, text_feats, side)
    some_text = exchange(packed, along_y).reshape(2 * side, -1)

    up_t = w_up.T
    slope, part = forward(
        patches, ln_gain, up_t, b_up, w_down, b_down, lax.axis_size("tensor")
    )
    some_text, part = lax.optimization_barrier((some_text, part))
    rows = spread(some_text, along_xz).reshape(batch, -1)
    pooled = lax.psum(part, "tensor")
    img_copies, g_hidden, away, keep = loss_and_back(
        place,
        log_sharpness,
        pairwise_logit_shift,
        pair_ids,
        pooled,
        head_gain,
        rows,
        w_down,
        up_t,
        slope,
        side,
    )

    other = swap_core(away)

    def both(start, count):
        part = slice(start, start + count)
        return keep[part].astype(F32) + other[part].astype(F32)

    send_one = both(0, 128).astype(BF16)
    got_one = swap(send_one, "tensor", step_one)
    img_copies, _ = lax.optimization_barrier((img_copies, send_one))
    some_img = exchange(img_copies, along_y).reshape(2 * side, -1)
    got_one, some_img = lax.optimization_barrier((got_one, some_img))
    send_two = (both(128, 64) + got_one[:64].astype(F32)).astype(BF16)
    got_two = swap(send_two, "tensor", step_two)
    images = spread(some_img, along_xz).reshape(batch, -1)
    done = finish(place, keep, other, got_one, got_two, patches, g_hidden, ln_gain)

    from_two = swap(done, "tensor", step_two)
    from_one = swap(done, "tensor", step_one)
    far = swap(from_two, "tensor", step_one)
    near = swap_core(jnp.concatenate([done, from_two]))
    from_one, images = lax.optimization_barrier((from_one, images))
    rest = swap_core(jnp.concatenate([from_one, far]))
    grad_patches = put_in_place(
        place, (done, from_two, from_one, far, near, rest), patches.shape[0]
    )

    grad_text = text_grad(
        log_sharpness,
        pairwise_logit_shift,
        pair_ids,
        unit_text,
        text_len,
        images,
        rows,
    )
    return grad_patches, grad_text


def solution(mesh):
    in_specs = (
        P("dp", None),
        P(),
        P(None, "tensor"),
        P("tensor"),
        P("tensor", None),
        P(),
        P(),
        P("dp", None),
        P("dp"),
        P(),
        P(),
    )
    out_specs = (P("dp", None), P("dp", None))
    return jax.shard_map(
        on_device, mesh=mesh, in_specs=in_specs, out_specs=out_specs, check_vma=False
    )
```

```python
import functools
import math

import jax
import jax.numpy as jnp
from jax import lax
from jax.experimental import pallas as pl
from jax.experimental.pallas import tpu as pltpu
from jax.sharding import PartitionSpec as P

PATCHES = 256
BLOCK = 64
EPS = 1e-06
LOSS_SCALE = 131072.0
F32 = jnp.float32
BF16 = jnp.bfloat16
LAST = (((1,), (1,)), ((), ()))
SMEM = pl.BlockSpec(memory_space=pltpu.SMEM)
VMEM = pl.BlockSpec(memory_space=pltpu.VMEM)
SMALL = pltpu.CompilerParams(vmem_limit_bytes=16 * 1024 * 1024)


def places(position):
    core, ring = position & 1, position >> 1
    u, v = (ring ^ (ring >> 1)) & 1, ring >> 1
    swap = core * (u ^ v)
    return core, u ^ swap, v ^ swap


def order(one, two):
    return [3 - 2 * one - two, 2 - 2 * one + two, 2 * one + 1 - two, 2 * one + two]


def norm_parts(values):
    centre = values - jnp.mean(values, axis=-1, keepdims=True)
    inverse = lax.rsqrt(jnp.mean(centre * centre, axis=-1, keepdims=True) + EPS)
    return centre * inverse, inverse


def norm_back(grad_out, gain, normed, inverse):
    scaled = grad_out * gain
    return inverse * (
        scaled
        - jnp.mean(scaled, axis=-1, keepdims=True)
        - normed * jnp.mean(scaled * normed, axis=-1, keepdims=True)
    )


def split_stack(values):
    high = values.astype(BF16).astype(F32)
    rest = values - high
    mid = rest.astype(BF16).astype(F32)
    low = rest - mid
    return jnp.concatenate([high, mid, low, jnp.zeros_like(high)], axis=0).astype(BF16)


def unstack(sums):
    return (sums[0:8] + sums[8:16]) + sums[16:24]


def image_features(pooled_ref, gain):
    rows = pooled_ref[...]
    pooled = jnp.concatenate([rows] * 4, axis=0)
    feat_n, feat_s = norm_parts(pooled)
    features = feat_n * gain
    feat_len = jnp.sqrt(jnp.sum(features * features, axis=-1, keepdims=True) + EPS)
    return feat_n, feat_s, feat_len, features / feat_len


def pack_kernel(ids_ref, text_ref, pack_ref, unit_ref, len_ref):
    text = text_ref[...].astype(F32)
    length = jnp.sqrt(jnp.sum(text * text, axis=-1, keepdims=True) + EPS)
    unit = text / length
    unit_ref[...] = unit
    len_ref[...] = jnp.broadcast_to(length, len_ref.shape)
    row = lax.broadcasted_iota(jnp.int32, (2, 128), 0)
    lane = lax.broadcasted_iota(jnp.int32, (2, 128), 1)
    ids = jnp.where(row == 0, ids_ref[0], ids_ref[1])
    ids = jnp.where(lane == 0, ids, 0).astype(F32)
    packed = jnp.concatenate([unit, ids], axis=1).astype(BF16)
    for copy in range(pack_ref.shape[0]):
        pack_ref[copy] = packed


def pack(pair_ids, text_feats, copies):
    width = text_feats.shape[1]
    return pl.pallas_call(
        pack_kernel,
        in_specs=[SMEM, VMEM],
        out_shape=[
            jax.ShapeDtypeStruct((copies, 2, width + 128), BF16),
            jax.ShapeDtypeStruct((2, width), F32),
            jax.ShapeDtypeStruct((2, 128), F32),
        ],
        compiler_params=SMALL,
        cost_estimate=pl.CostEstimate(
            flops=30_000_000_000, bytes_accessed=100_000, transcendentals=0
        ),
        name="pack",
    )(pair_ids, text_feats)


def forward_kernel(
    n_tensor, x_ref, gain_ref, bias_ref, b_down_ref, up_ref, down_ref,
    slope_ref, part_ref, act_sum, x_sum,
):
    step = pl.program_id(0)
    image = step // 2
    @pl.when(step == 0)
    def _():
        act_sum[...] = jnp.zeros_like(act_sum)
        x_sum[...] = jnp.zeros_like(x_sum)

    x = x_ref[...].astype(F32)
    normed, _ = norm_parts(x)
    normed = (normed * gain_ref[...][None, :]).astype(BF16)

    pre = lax.dot_general(normed, up_ref[...], LAST, preferred_element_type=F32)
    pre = pre + bias_ref[...][None, :]
    root = math.sqrt(2.0 / math.pi)
    square = pre * pre
    tanh = jnp.tanh(root * (pre + 0.044715 * (square * pre)))
    half = 0.5 * (1.0 + tanh)
    act = (pre * half).astype(BF16).astype(F32)
    slope = half + (0.5 * root) * pre * (1.0 - tanh * tanh) * (
        1.0 + (3.0 * 0.044715) * square
    )
    slope_ref[...] = slope.astype(BF16)

    def add(total, values):
        row = lax.broadcasted_iota(jnp.int32, total.shape, 0)
        sums = jnp.sum(values, axis=0, keepdims=True)
        total[...] += jnp.where(row == image, sums, 0.0)

    add(act_sum, act)
    add(x_sum, x)

    @pl.when(step == pl.num_programs(0) - 1)
    def _():
        stack = split_stack(act_sum[...] * (1.0 / PATCHES))
        mlp = unstack(jnp.dot(stack, down_ref[...], preferred_element_type=F32))
        rest = x_sum[...] * (1.0 / PATCHES) + b_down_ref[...][None, :]
        part = (mlp + rest * (1.0 / n_tensor))[0:2]
        for copy in range(n_tensor):
            part_ref[copy] = part


def forward(patches, ln_gain, up_t, b_up, w_down, b_down, n_tensor):
    tokens, width = patches.shape
    units = up_t.shape[0]
    rows = 128
    vector = lambda size: pl.BlockSpec((size,), lambda i: (0,))
    return pl.pallas_call(
        functools.partial(forward_kernel, n_tensor),
        grid=(tokens // rows,),
        in_specs=[
            pl.BlockSpec((rows, width), lambda i: (i, 0)),
            vector(width),
            vector(units),
            vector(width),
            pl.BlockSpec((units, width), lambda i: (0, 0)),
            pl.BlockSpec((units, width), lambda i: (0, 0)),
        ],
        out_specs=[
            pl.BlockSpec((rows, units), lambda i: (i, 0)),
            pl.BlockSpec((n_tensor, 2, width), lambda i: (0, 0, 0)),
        ],
        out_shape=[
            jax.ShapeDtypeStruct((tokens, units), BF16),
            jax.ShapeDtypeStruct((n_tensor, 2, width), F32),
        ],
        scratch_shapes=[
            pltpu.VMEM((8, units), F32),
            pltpu.VMEM((8, width), F32),
        ],
        compiler_params=SMALL,
        cost_estimate=pl.CostEstimate(
            flops=2 * tokens * width * units,
            bytes_accessed=2 * tokens * width + 4 * units * width + 4 * tokens * units,
            transcendentals=tokens * units,
        ),
        name="forward",
    )(patches, ln_gain, b_up, b_down, up_t, w_down)


def pick_row(rows, index):
    row = lax.broadcasted_iota(jnp.int32, rows.shape, 0)
    return jnp.sum(jnp.where(row == index, rows, 0.0), axis=0, keepdims=True)


def image_features(rows, gain):
    feat_n, feat_s = norm_parts(jnp.concatenate([rows] * 4, axis=0))
    features = feat_n * gain
    feat_len = jnp.sqrt(jnp.sum(features * features, axis=-1, keepdims=True) + EPS)
    return feat_n, feat_s, feat_len, features / feat_len


def pair_grad(queries, keys, ids_ref, id_columns, sharp, shift):
    batch = keys.shape[0]
    logits = sharp * unstack(
        lax.dot_general(split_stack(queries), keys, LAST, preferred_element_type=F32)
    ) + shift
    lane = lax.broadcasted_iota(jnp.int32, (16, 128), 1)
    first_lane = jnp.where(lane == 0, 1.0, 0.0).astype(BF16)
    ids = lax.dot_general(first_lane, id_columns, LAST, preferred_element_type=F32)[0:8]
    row = lax.broadcasted_iota(jnp.int32, (8, batch), 0)
    own = jnp.where(row == 0, ids_ref[0], ids_ref[1]).astype(F32)
    sign = jnp.where(ids == own, 1.0, -1.0)
    logit_grad = -LOSS_SCALE * sign * jax.nn.sigmoid(-sign * logits) / batch
    logit_grad = jnp.where(row < 2, logit_grad, 0.0)
    return sharp * unstack(
        jnp.dot(split_stack(logit_grad), keys, preferred_element_type=F32)
    )


def scalars(sharp_ref, shift_ref):
    return jnp.exp(sharp_ref[...][None, :]), shift_ref[...][None, :]


def loss_kernel(
    place_ref, ids_ref, sharp_ref, shift_ref, parts_ref, gain_ref, rows_ref, down_ref,
    up_ref, slope_ref, img_ref, hidden_ref, away_ref, keep_ref, g_pre,
):
    width = gain_ref.shape[0]
    core, one, two = places(place_ref[0])
    gain = gain_ref[...][None, :]
    pooled = parts_ref[0]
    for part in range(1, parts_ref.shape[0]):
        pooled = pooled + parts_ref[part]
    feat_n, feat_s, feat_len, img_emb = image_features(pooled, gain)
    for copy in range(img_ref.shape[0]):
        img_ref[copy] = img_emb[0:2].astype(BF16)
    g_img = pair_grad(
        img_emb, rows_ref[:, 0:width], ids_ref, rows_ref[:, width : width + 128],
        *scalars(sharp_ref, shift_ref),
    )
    g_feat = (
        g_img - img_emb * jnp.sum(img_emb * g_img, axis=-1, keepdims=True)
    ) / feat_len
    g_hidden = norm_back(g_feat, gain, feat_n, feat_s) * (1.0 / PATCHES)
    hidden_ref[...] = g_hidden[0:2]
    g_rows = jnp.concatenate([g_hidden, jnp.zeros_like(g_hidden)], axis=0).astype(BF16)
    g_act = lax.dot_general(g_rows, down_ref[...], LAST, preferred_element_type=F32)[0:8]
    for image, blocks, out_ref in (
        (1 - core, order(two, one), away_ref),
        (core, order(one, two), keep_ref),
    ):
        row = pick_row(g_act, image)
        for spot, block in enumerate(blocks):
            start = pl.multiple_of(image * PATCHES + block * BLOCK, BLOCK)
            g_pre[spot * BLOCK : (spot + 1) * BLOCK, :] = (
                slope_ref[pl.ds(start, BLOCK), :].astype(F32) * row
            ).astype(BF16)
        out_ref[...] = jnp.dot(
            g_pre[...], up_ref[...], preferred_element_type=F32
        ).astype(BF16)


def loss_and_back(
    place, sharp, shift, ids, parts, gain, rows, w_down, up_t, slope, copies
):
    units, width = up_t.shape
    return pl.pallas_call(
        loss_kernel,
        in_specs=[SMEM] * 2 + [VMEM] * 8,
        out_shape=[
            jax.ShapeDtypeStruct((copies, 2, width), BF16),
            jax.ShapeDtypeStruct((2, width), F32),
            jax.ShapeDtypeStruct((PATCHES, width), BF16),
            jax.ShapeDtypeStruct((PATCHES, width), BF16),
        ],
        scratch_shapes=[pltpu.VMEM((PATCHES, units), BF16)],
        compiler_params=SMALL,
        cost_estimate=pl.CostEstimate(
            flops=4 * PATCHES * width * units,
            bytes_accessed=6 * units * width + 8 * PATCHES * units,
            transcendentals=0,
        ),
        name="loss_and_back",
    )(place, ids, sharp, shift, parts, gain, rows, w_down, up_t, slope)


def text_kernel(
    ids_ref, sharp_ref, shift_ref, unit_ref, len_ref, img_ref, rows_ref, out_ref
):
    width = unit_ref.shape[1]
    unit = unit_ref[...]
    queries = jnp.concatenate([unit] * 4, axis=0).astype(BF16).astype(F32)
    g_text = pair_grad(
        queries, img_ref[...], ids_ref, rows_ref[:, width : width + 128],
        *scalars(sharp_ref, shift_ref),
    )[0:2]
    along = jnp.sum(unit * g_text, axis=-1, keepdims=True)
    out_ref[...] = (g_text - unit * along) / len_ref[:, 0:1]


def text_grad(sharp, shift, ids, unit, length, images, rows):
    return pl.pallas_call(
        text_kernel,
        in_specs=[SMEM] + [VMEM] * 6,
        out_shape=jax.ShapeDtypeStruct(unit.shape, F32),
        compiler_params=SMALL,
        cost_estimate=pl.CostEstimate(
            flops=1_000_000_000, bytes_accessed=600_000, transcendentals=0
        ),
        name="text_grad",
    )(ids, sharp, shift, unit, length, images, rows)


def finish_kernel(
    place_ref, keep_ref, other_ref, one_ref, two_ref, x_ref, hidden_ref, gain_ref, out_ref
):
    g_normed = keep_ref[...].astype(F32) + other_ref[...].astype(F32)
    g_normed = g_normed + one_ref[...].astype(F32) + two_ref[...].astype(F32)
    normed, inverse = norm_parts(x_ref[...].astype(F32))
    grad = norm_back(g_normed, gain_ref[...][None, :], normed, inverse)
    out_ref[...] = (grad + pick_row(hidden_ref[...], place_ref[0] & 1)).astype(BF16)


def finish(place, keep, other, got_one, got_two, patches, g_hidden, ln_gain):
    width = patches.shape[1]
    block = lambda index: pl.BlockSpec((BLOCK, width), index)

    def own_block(i, place):
        core, one, two = places(place[0])
        return core * (PATCHES // BLOCK) + 2 * one + two, 0

    return pl.pallas_call(
        finish_kernel,
        grid_spec=pltpu.PrefetchScalarGridSpec(
            num_scalar_prefetch=1,
            grid=(1,),
            in_specs=[
                block(lambda i, place: (3, 0)),
                block(lambda i, place: (3, 0)),
                block(lambda i, place: (1, 0)),
                block(lambda i, place: (0, 0)),
                block(own_block),
                pl.BlockSpec((2, width), lambda i, place: (0, 0)),
                pl.BlockSpec((width,), lambda i, place: (0,)),
            ],
            out_specs=block(lambda i, place: (0, 0)),
        ),
        out_shape=jax.ShapeDtypeStruct((BLOCK, width), BF16),
        compiler_params=SMALL,
        name="finish",
    )(place, keep, other, got_one, got_two, patches, g_hidden, ln_gain)


def place_kernel(place_ref, own, two, one, far, near, rest, out_ref):
    core, one_bit, two_bit = places(place_ref[0])
    low, high = slice(0, BLOCK), slice(BLOCK, 2 * BLOCK)
    mine, theirs = order(one_bit, two_bit), order(two_bit, one_bit)
    moves = [
        (far, low, core, mine[0]),
        (one, low, core, mine[1]),
        (two, low, core, mine[2]),
        (own, low, core, mine[3]),
        (rest, high, 1 - core, theirs[0]),
        (rest, low, 1 - core, theirs[1]),
        (near, high, 1 - core, theirs[2]),
        (near, low, 1 - core, theirs[3]),
    ]
    for ref, rows, image, block in moves:
        start = pl.multiple_of(image * PATCHES + block * BLOCK, BLOCK)
        out_ref[pl.ds(start, BLOCK), :] = ref[rows, :]


def put_in_place(place, pieces, tokens):
    width = pieces[0].shape[1]
    return pl.pallas_call(
        place_kernel,
        in_specs=[SMEM] + [VMEM] * 6,
        out_shape=jax.ShapeDtypeStruct((tokens, width), BF16),
        compiler_params=SMALL,
        name="put_in_place",
    )(place, *pieces)


def swap(value, axis, partner):
    size = lax.axis_size(axis)
    return lax.ppermute(value, axis, [(i, partner(i)) for i in range(size)])


def swap_core(value):
    return swap(value, "tensor", lambda i: i ^ 1)


def step_one(i):
    return i ^ 2 if i % 2 == 0 else (3 - i // 2) * 2 + 1


def step_two(i):
    return (3 - i // 2) * 2 if i % 2 == 0 else i ^ 2


def exchange(copies, groups, axis="dp"):
    return lax.all_to_all(
        copies, axis, split_axis=0, concat_axis=0, axis_index_groups=groups
    )


def spread(rows, groups):
    copies = jnp.broadcast_to(rows[None], (len(groups[0]),) + rows.shape)
    return exchange(copies, groups)


def on_device(
    patches,
    ln_gain,
    w_up,
    b_up,
    w_down,
    b_down,
    head_gain,
    text_feats,
    pair_ids,
    log_sharpness,
    pairwise_logit_shift,
):
    batch = text_feats.shape[0] * lax.axis_size("dp")
    place = lax.axis_index("tensor").astype(jnp.int32).reshape(1)

    side = math.isqrt(lax.axis_size("dp"))
    along_y = [[y * side + k for y in range(side)] for k in range(side)]
    along_xz = [[y * side + k for k in range(side)] for y in range(side)]
    packed, unit_text, text_len = pack(pair_ids, text_feats, side)
    some_text = exchange(packed, along_y).reshape(2 * side, -1)

    up_t = w_up.T
    some_text, first_gain = lax.optimization_barrier((some_text, ln_gain))
    rows = spread(some_text, along_xz).reshape(batch, -1)
    slope, parts = forward(
        patches, first_gain, up_t, b_up, w_down, b_down, lax.axis_size("tensor")
    )
    parts, rows = lax.optimization_barrier((parts, rows))
    parts = exchange(parts, None, "tensor")
    img_copies, g_hidden, away, keep = loss_and_back(
        place,
        log_sharpness,
        pairwise_logit_shift,
        pair_ids,
        parts,
        head_gain,
        rows,
        w_down,
        up_t,
        slope,
        side,
    )

    other = swap_core(away)

    def both(start, count):
        part = slice(start, start + count)
        return keep[part].astype(F32) + other[part].astype(F32)

    send_one = both(0, 128).astype(BF16)
    got_one = swap(send_one, "tensor", step_one)
    img_copies, _ = lax.optimization_barrier((img_copies, send_one))
    some_img = exchange(img_copies, along_y).reshape(2 * side, -1)
    got_one, some_img = lax.optimization_barrier((got_one, some_img))
    send_two = (both(128, 64) + got_one[:64].astype(F32)).astype(BF16)
    got_two = swap(send_two, "tensor", step_two)
    images = spread(some_img, along_xz).reshape(batch, -1)
    done = finish(place, keep, other, got_one, got_two, patches, g_hidden, ln_gain)

    from_two = swap(done, "tensor", step_two)
    from_one = swap(done, "tensor", step_one)
    far = swap(from_two, "tensor", step_one)
    near = swap_core(jnp.concatenate([done, from_two]))
    from_one, images = lax.optimization_barrier((from_one, images))
    rest = swap_core(jnp.concatenate([from_one, far]))
    grad_patches = put_in_place(
        place, (done, from_two, from_one, far, near, rest), patches.shape[0]
    )

    grad_text = text_grad(
        log_sharpness,
        pairwise_logit_shift,
        pair_ids,
        unit_text,
        text_len,
        images,
        rows,
    )
    return grad_patches, grad_text


def solution(mesh):
    in_specs = (
        P("dp", None),
        P(),
        P(None, "tensor"),
        P("tensor"),
        P("tensor", None),
        P(),
        P(),
        P("dp", None),
        P("dp"),
        P(),
        P(),
    )
    out_specs = (P("dp", None), P("dp", None))
    return jax.shard_map(
        on_device, mesh=mesh, in_specs=in_specs, out_specs=out_specs, check_vma=False
    )
```

```python
import functools
import math

import jax
import jax.numpy as jnp
from jax import lax
from jax.experimental import pallas as pl
from jax.experimental.pallas import tpu as pltpu
from jax.sharding import PartitionSpec as P

PATCHES = 256
BLOCK = 64
EPS = 1e-06
LOSS_SCALE = 131072.0
F32 = jnp.float32
BF16 = jnp.bfloat16
LAST = (((1,), (1,)), ((), ()))
SMEM = pl.BlockSpec(memory_space=pltpu.SMEM)
VMEM = pl.BlockSpec(memory_space=pltpu.VMEM)
SMALL = pltpu.CompilerParams(vmem_limit_bytes=16 * 1024 * 1024)


def places(position):
    core, ring = position & 1, position >> 1
    u, v = (ring ^ (ring >> 1)) & 1, ring >> 1
    swap = core * (u ^ v)
    return core, u ^ swap, v ^ swap


def order(one, two):
    return [3 - 2 * one - two, 2 - 2 * one + two, 2 * one + 1 - two, 2 * one + two]


def norm_parts(values):
    centre = values - jnp.mean(values, axis=-1, keepdims=True)
    inverse = lax.rsqrt(jnp.mean(centre * centre, axis=-1, keepdims=True) + EPS)
    return centre * inverse, inverse


def norm_back(grad_out, gain, normed, inverse):
    scaled = grad_out * gain
    return inverse * (
        scaled
        - jnp.mean(scaled, axis=-1, keepdims=True)
        - normed * jnp.mean(scaled * normed, axis=-1, keepdims=True)
    )


def split_stack(values):
    high = values.astype(BF16).astype(F32)
    rest = values - high
    mid = rest.astype(BF16).astype(F32)
    low = rest - mid
    return jnp.concatenate([high, mid, low, jnp.zeros_like(high)], axis=0).astype(BF16)


def unstack(sums):
    return (sums[0:8] + sums[8:16]) + sums[16:24]


def image_features(pooled_ref, gain):
    rows = pooled_ref[...]
    pooled = jnp.concatenate([rows] * 4, axis=0)
    feat_n, feat_s = norm_parts(pooled)
    features = feat_n * gain
    feat_len = jnp.sqrt(jnp.sum(features * features, axis=-1, keepdims=True) + EPS)
    return feat_n, feat_s, feat_len, features / feat_len


def pack_kernel(ids_ref, text_ref, pack_ref, unit_ref, len_ref):
    text = text_ref[...].astype(F32)
    length = jnp.sqrt(jnp.sum(text * text, axis=-1, keepdims=True) + EPS)
    unit = text / length
    unit_ref[...] = unit
    len_ref[...] = jnp.broadcast_to(length, len_ref.shape)
    row = lax.broadcasted_iota(jnp.int32, (2, 128), 0)
    lane = lax.broadcasted_iota(jnp.int32, (2, 128), 1)
    ids = jnp.where(row == 0, ids_ref[0], ids_ref[1])
    ids = jnp.where(lane == 0, ids, 0).astype(F32)
    packed = jnp.concatenate([unit, ids], axis=1).astype(BF16)
    for copy in range(pack_ref.shape[0]):
        pack_ref[copy] = packed


def pack(pair_ids, text_feats, copies):
    width = text_feats.shape[1]
    return pl.pallas_call(
        pack_kernel,
        in_specs=[SMEM, VMEM],
        out_shape=[
            jax.ShapeDtypeStruct((copies, 2, width + 128), BF16),
            jax.ShapeDtypeStruct((2, width), F32),
            jax.ShapeDtypeStruct((2, 128), F32),
        ],
        compiler_params=SMALL,
        cost_estimate=pl.CostEstimate(
            flops=30_000_000_000, bytes_accessed=100_000, transcendentals=0
        ),
        name="pack",
    )(pair_ids, text_feats)


def forward_kernel(
    n_tensor, x_ref, gain_ref, bias_ref, b_down_ref, up_ref, down_ref,
    slope_ref, part_ref, act_sum, x_sum,
):
    step = pl.program_id(0)
    image = step // 2
    @pl.when(step == 0)
    def _():
        act_sum[...] = jnp.zeros_like(act_sum)
        x_sum[...] = jnp.zeros_like(x_sum)

    x = x_ref[...].astype(F32)
    normed, _ = norm_parts(x)
    normed = (normed * gain_ref[...][None, :]).astype(BF16)

    pre = lax.dot_general(normed, up_ref[...], LAST, preferred_element_type=F32)
    pre = pre + bias_ref[...][None, :]
    root = math.sqrt(2.0 / math.pi)
    square = pre * pre
    tanh = jnp.tanh(root * (pre + 0.044715 * (square * pre)))
    half = 0.5 * (1.0 + tanh)
    act = (pre * half).astype(BF16).astype(F32)
    slope = half + (0.5 * root) * pre * (1.0 - tanh * tanh) * (
        1.0 + (3.0 * 0.044715) * square
    )
    slope_ref[...] = slope.astype(BF16)

    def add(total, values):
        row = lax.broadcasted_iota(jnp.int32, total.shape, 0)
        sums = jnp.sum(values, axis=0, keepdims=True)
        total[...] += jnp.where(row == image, sums, 0.0)

    add(act_sum, act)
    add(x_sum, x)

    @pl.when(step == pl.num_programs(0) - 1)
    def _():
        stack = split_stack(act_sum[...] * (1.0 / PATCHES))
        mlp = unstack(jnp.dot(stack, down_ref[...], preferred_element_type=F32))
        rest = x_sum[...] * (1.0 / PATCHES) + b_down_ref[...][None, :]
        part = (mlp + rest * (1.0 / n_tensor))[0:2]
        for copy in range(n_tensor):
            part_ref[copy] = part


def forward(patches, ln_gain, up_t, b_up, w_down, b_down, n_tensor):
    tokens, width = patches.shape
    units = up_t.shape[0]
    rows = 128
    vector = lambda size: pl.BlockSpec((size,), lambda i: (0,))
    return pl.pallas_call(
        functools.partial(forward_kernel, n_tensor),
        grid=(tokens // rows,),
        in_specs=[
            pl.BlockSpec((rows, width), lambda i: (i, 0)),
            vector(width),
            vector(units),
            vector(width),
            pl.BlockSpec((units, width), lambda i: (0, 0)),
            pl.BlockSpec((units, width), lambda i: (0, 0)),
        ],
        out_specs=[
            pl.BlockSpec((rows, units), lambda i: (i, 0)),
            pl.BlockSpec((n_tensor, 2, width), lambda i: (0, 0, 0)),
        ],
        out_shape=[
            jax.ShapeDtypeStruct((tokens, units), BF16),
            jax.ShapeDtypeStruct((n_tensor, 2, width), F32),
        ],
        scratch_shapes=[
            pltpu.VMEM((8, units), F32),
            pltpu.VMEM((8, width), F32),
        ],
        compiler_params=SMALL,
        cost_estimate=pl.CostEstimate(
            flops=2 * tokens * width * units,
            bytes_accessed=2 * tokens * width + 4 * units * width + 4 * tokens * units,
            transcendentals=tokens * units,
        ),
        name="forward",
    )(patches, ln_gain, b_up, b_down, up_t, w_down)


def pick_row(rows, index):
    row = lax.broadcasted_iota(jnp.int32, rows.shape, 0)
    return jnp.sum(jnp.where(row == index, rows, 0.0), axis=0, keepdims=True)


def image_features(rows, gain):
    feat_n, feat_s = norm_parts(jnp.concatenate([rows] * 4, axis=0))
    features = feat_n * gain
    feat_len = jnp.sqrt(jnp.sum(features * features, axis=-1, keepdims=True) + EPS)
    return feat_n, feat_s, feat_len, features / feat_len


def pair_grad(queries, keys, ids_ref, id_columns, sharp, shift):
    batch = keys.shape[0]
    logits = sharp * unstack(
        lax.dot_general(split_stack(queries), keys, LAST, preferred_element_type=F32)
    ) + shift
    lane = lax.broadcasted_iota(jnp.int32, (16, 128), 1)
    first_lane = jnp.where(lane == 0, 1.0, 0.0).astype(BF16)
    ids = lax.dot_general(first_lane, id_columns, LAST, preferred_element_type=F32)[0:8]
    row = lax.broadcasted_iota(jnp.int32, (8, batch), 0)
    own = jnp.where(row == 0, ids_ref[0], ids_ref[1]).astype(F32)
    sign = jnp.where(ids == own, 1.0, -1.0)
    logit_grad = -LOSS_SCALE * sign * jax.nn.sigmoid(-sign * logits) / batch
    logit_grad = jnp.where(row < 2, logit_grad, 0.0)
    return sharp * unstack(
        jnp.dot(split_stack(logit_grad), keys, preferred_element_type=F32)
    )


def scalars(sharp_ref, shift_ref):
    return jnp.exp(sharp_ref[...][None, :]), shift_ref[...][None, :]


def loss_kernel(
    place_ref, ids_ref, sharp_ref, shift_ref, parts_ref, gain_ref, rows_ref, down_ref,
    up_ref, slope_ref, img_ref, hidden_ref, away_ref, keep_ref, g_pre,
):
    width = gain_ref.shape[0]
    core, one, two = places(place_ref[0])
    gain = gain_ref[...][None, :]
    pooled = parts_ref[0]
    for part in range(1, parts_ref.shape[0]):
        pooled = pooled + parts_ref[part]
    feat_n, feat_s, feat_len, img_emb = image_features(pooled, gain)
    for copy in range(img_ref.shape[0]):
        img_ref[copy] = img_emb[0:2].astype(BF16)
    g_img = pair_grad(
        img_emb, rows_ref[:, 0:width], ids_ref, rows_ref[:, width : width + 128],
        *scalars(sharp_ref, shift_ref),
    )
    g_feat = (
        g_img - img_emb * jnp.sum(img_emb * g_img, axis=-1, keepdims=True)
    ) / feat_len
    g_hidden = norm_back(g_feat, gain, feat_n, feat_s) * (1.0 / PATCHES)
    hidden_ref[...] = g_hidden[0:2]
    g_rows = jnp.concatenate([g_hidden, jnp.zeros_like(g_hidden)], axis=0).astype(BF16)
    g_act = lax.dot_general(g_rows, down_ref[...], LAST, preferred_element_type=F32)[0:8]
    for image, blocks, out_ref in (
        (1 - core, order(two, one), away_ref),
        (core, order(one, two), keep_ref),
    ):
        row = pick_row(g_act, image)
        for spot, block in enumerate(blocks):
            start = pl.multiple_of(image * PATCHES + block * BLOCK, BLOCK)
            g_pre[spot * BLOCK : (spot + 1) * BLOCK, :] = (
                slope_ref[pl.ds(start, BLOCK), :].astype(F32) * row
            ).astype(BF16)
        out_ref[...] = jnp.dot(
            g_pre[...], up_ref[...], preferred_element_type=F32
        ).astype(BF16)


def loss_and_back(
    place, sharp, shift, ids, parts, gain, rows, w_down, up_t, slope, copies
):
    units, width = up_t.shape
    return pl.pallas_call(
        loss_kernel,
        in_specs=[SMEM] * 2 + [VMEM] * 8,
        out_shape=[
            jax.ShapeDtypeStruct((copies, 2, width), BF16),
            jax.ShapeDtypeStruct((2, width), F32),
            jax.ShapeDtypeStruct((PATCHES, width), BF16),
            jax.ShapeDtypeStruct((PATCHES, width), BF16),
        ],
        scratch_shapes=[pltpu.VMEM((PATCHES, units), BF16)],
        compiler_params=SMALL,
        cost_estimate=pl.CostEstimate(
            flops=4 * PATCHES * width * units,
            bytes_accessed=6 * units * width + 8 * PATCHES * units,
            transcendentals=0,
        ),
        name="loss_and_back",
    )(place, ids, sharp, shift, parts, gain, rows, w_down, up_t, slope)


def text_kernel(
    ids_ref, sharp_ref, shift_ref, unit_ref, len_ref, img_ref, columns_ref, out_ref
):
    unit = unit_ref[...]
    queries = jnp.concatenate([unit] * 4, axis=0).astype(BF16).astype(F32)
    g_text = pair_grad(
        queries, img_ref[...], ids_ref, columns_ref[...],
        *scalars(sharp_ref, shift_ref),
    )[0:2]
    along = jnp.sum(unit * g_text, axis=-1, keepdims=True)
    out_ref[...] = (g_text - unit * along) / len_ref[:, 0:1]


def text_grad(sharp, shift, ids, unit, length, images, columns):
    return pl.pallas_call(
        text_kernel,
        in_specs=[SMEM] + [VMEM] * 6,
        out_shape=jax.ShapeDtypeStruct(unit.shape, F32),
        compiler_params=SMALL,
        cost_estimate=pl.CostEstimate(
            flops=1_000_000_000, bytes_accessed=600_000, transcendentals=0
        ),
        name="text_grad",
    )(ids, sharp, shift, unit, length, images, columns)


def finish_kernel(
    place_ref, keep_ref, other_ref, one_ref, two_ref, x_ref, hidden_ref, gain_ref, out_ref
):
    g_normed = keep_ref[...].astype(F32) + other_ref[...].astype(F32)
    g_normed = g_normed + one_ref[...].astype(F32) + two_ref[...].astype(F32)
    normed, inverse = norm_parts(x_ref[...].astype(F32))
    grad = norm_back(g_normed, gain_ref[...][None, :], normed, inverse)
    out_ref[...] = (grad + pick_row(hidden_ref[...], place_ref[0] & 1)).astype(BF16)


def finish(place, keep, other, got_one, got_two, patches, g_hidden, ln_gain):
    width = patches.shape[1]
    block = lambda index: pl.BlockSpec((BLOCK, width), index)

    def own_block(i, place):
        core, one, two = places(place[0])
        return core * (PATCHES // BLOCK) + 2 * one + two, 0

    return pl.pallas_call(
        finish_kernel,
        grid_spec=pltpu.PrefetchScalarGridSpec(
            num_scalar_prefetch=1,
            grid=(1,),
            in_specs=[
                block(lambda i, place: (3, 0)),
                block(lambda i, place: (3, 0)),
                block(lambda i, place: (1, 0)),
                block(lambda i, place: (0, 0)),
                block(own_block),
                pl.BlockSpec((2, width), lambda i, place: (0, 0)),
                pl.BlockSpec((width,), lambda i, place: (0,)),
            ],
            out_specs=block(lambda i, place: (0, 0)),
        ),
        out_shape=jax.ShapeDtypeStruct((BLOCK, width), BF16),
        compiler_params=SMALL,
        name="finish",
    )(place, keep, other, got_one, got_two, patches, g_hidden, ln_gain)


def place_kernel(place_ref, own, two, one, near, rest, out_ref):
    core, one_bit, two_bit = places(place_ref[0])
    low, high = slice(0, BLOCK), slice(BLOCK, 2 * BLOCK)
    mine, theirs = order(one_bit, two_bit), order(two_bit, one_bit)
    moves = [
        (one, high, core, mine[0]),
        (one, low, core, mine[1]),
        (two, low, core, mine[2]),
        (own, low, core, mine[3]),
        (rest, high, 1 - core, theirs[0]),
        (rest, low, 1 - core, theirs[1]),
        (near, high, 1 - core, theirs[2]),
        (near, low, 1 - core, theirs[3]),
    ]
    for ref, rows, image, block in moves:
        start = pl.multiple_of(image * PATCHES + block * BLOCK, BLOCK)
        out_ref[pl.ds(start, BLOCK), :] = ref[rows, :]


def put_in_place(place, pieces, tokens):
    width = pieces[0].shape[1]
    return pl.pallas_call(
        place_kernel,
        in_specs=[SMEM] + [VMEM] * 5,
        out_shape=jax.ShapeDtypeStruct((tokens, width), BF16),
        compiler_params=SMALL,
        name="put_in_place",
    )(place, *pieces)


def swap(value, axis, partner):
    size = lax.axis_size(axis)
    return lax.ppermute(value, axis, [(i, partner(i)) for i in range(size)])


def swap_core(value):
    return swap(value, "tensor", lambda i: i ^ 1)


def step_one(i):
    return i ^ 2 if i % 2 == 0 else (3 - i // 2) * 2 + 1


def step_two(i):
    return (3 - i // 2) * 2 if i % 2 == 0 else i ^ 2


def exchange(copies, groups, axis="dp"):
    return lax.all_to_all(
        copies, axis, split_axis=0, concat_axis=0, axis_index_groups=groups
    )


def spread(rows, groups):
    copies = jnp.broadcast_to(rows[None], (len(groups[0]),) + rows.shape)
    return exchange(copies, groups)


def on_device(
    patches,
    ln_gain,
    w_up,
    b_up,
    w_down,
    b_down,
    head_gain,
    text_feats,
    pair_ids,
    log_sharpness,
    pairwise_logit_shift,
):
    batch = text_feats.shape[0] * lax.axis_size("dp")
    place = lax.axis_index("tensor").astype(jnp.int32).reshape(1)

    side = math.isqrt(lax.axis_size("dp"))
    along_y = [[y * side + k for y in range(side)] for k in range(side)]
    along_xz = [[y * side + k for k in range(side)] for y in range(side)]
    packed, unit_text, text_len = pack(pair_ids, text_feats, side)
    some_text = exchange(packed, along_y).reshape(2 * side, -1)

    up_t = w_up.T
    some_text, first_gain = lax.optimization_barrier((some_text, ln_gain))
    rows = spread(some_text, along_xz).reshape(batch, -1)
    slope, parts = forward(
        patches, first_gain, up_t, b_up, w_down, b_down, lax.axis_size("tensor")
    )
    parts, rows = lax.optimization_barrier((parts, rows))
    parts = exchange(parts, None, "tensor")
    img_copies, g_hidden, away, keep = loss_and_back(
        place,
        log_sharpness,
        pairwise_logit_shift,
        pair_ids,
        parts,
        head_gain,
        rows,
        w_down,
        up_t,
        slope,
        side,
    )

    other = swap_core(away)

    def both(start, count):
        part = slice(start, start + count)
        return keep[part].astype(F32) + other[part].astype(F32)

    send_one = both(0, 128).astype(BF16)
    got_one = swap(send_one, "tensor", step_one)
    img_copies, _ = lax.optimization_barrier((img_copies, send_one))
    some_img = exchange(img_copies, along_xz).reshape(2 * side, -1)
    got_one, some_img = lax.optimization_barrier((got_one, some_img))
    send_two = (both(128, 64) + got_one[:64].astype(F32)).astype(BF16)
    got_two = swap(send_two, "tensor", step_two)
    images = spread(some_img, along_y).reshape(batch, -1)
    done = finish(place, keep, other, got_one, got_two, patches, g_hidden, ln_gain)

    from_two = swap(done, "tensor", step_two)
    pair = jnp.concatenate([done, from_two])
    from_one = swap(pair, "tensor", step_one)
    near = swap_core(pair)
    rest = swap_core(from_one)
    grad_patches = put_in_place(
        place, (done, from_two, from_one, near, rest), patches.shape[0]
    )

    ids = rows[:, -128:].reshape(side, side, 2, 128).swapaxes(0, 1).reshape(batch, 128)
    grad_text = text_grad(
        log_sharpness,
        pairwise_logit_shift,
        pair_ids,
        unit_text,
        text_len,
        images,
        ids,
    )
    return grad_patches, grad_text


def solution(mesh):
    in_specs = (
        P("dp", None),
        P(),
        P(None, "tensor"),
        P("tensor"),
        P("tensor", None),
        P(),
        P(),
        P("dp", None),
        P("dp"),
        P(),
        P(),
    )
    out_specs = (P("dp", None), P("dp", None))
    return jax.shard_map(
        on_device, mesh=mesh, in_specs=in_specs, out_specs=out_specs, check_vma=False
    )
```

```python
import functools
import math

import jax
import jax.numpy as jnp
from jax import lax
from jax.experimental import pallas as pl
from jax.experimental.pallas import tpu as pltpu
from jax.sharding import PartitionSpec as P

PATCHES = 256
BLOCK = 64
EPS = 1e-06
LOSS_SCALE = 131072.0
F32 = jnp.float32
BF16 = jnp.bfloat16
LAST = (((1,), (1,)), ((), ()))
SMEM = pl.BlockSpec(memory_space=pltpu.SMEM)
VMEM = pl.BlockSpec(memory_space=pltpu.VMEM)
SMALL = pltpu.CompilerParams(vmem_limit_bytes=16 * 1024 * 1024)


def places(position):
    core, ring = position & 1, position >> 1
    u, v = (ring ^ (ring >> 1)) & 1, ring >> 1
    swap = core * (u ^ v)
    return core, u ^ swap, v ^ swap


def order(one, two):
    return [3 - 2 * one - two, 2 - 2 * one + two, 2 * one + 1 - two, 2 * one + two]


def norm_parts(values):
    centre = values - jnp.mean(values, axis=-1, keepdims=True)
    inverse = lax.rsqrt(jnp.mean(centre * centre, axis=-1, keepdims=True) + EPS)
    return centre * inverse, inverse


def norm_back(grad_out, gain, normed, inverse):
    scaled = grad_out * gain
    return inverse * (
        scaled
        - jnp.mean(scaled, axis=-1, keepdims=True)
        - normed * jnp.mean(scaled * normed, axis=-1, keepdims=True)
    )


def split_stack(values):
    high = values.astype(BF16).astype(F32)
    rest = values - high
    mid = rest.astype(BF16).astype(F32)
    low = rest - mid
    return jnp.concatenate([high, mid, low, jnp.zeros_like(high)], axis=0).astype(BF16)


def unstack(sums):
    return (sums[0:8] + sums[8:16]) + sums[16:24]


def image_features(pooled_ref, gain):
    rows = pooled_ref[...]
    pooled = jnp.concatenate([rows] * 4, axis=0)
    feat_n, feat_s = norm_parts(pooled)
    features = feat_n * gain
    feat_len = jnp.sqrt(jnp.sum(features * features, axis=-1, keepdims=True) + EPS)
    return feat_n, feat_s, feat_len, features / feat_len


def pack_kernel(ids_ref, text_ref, pack_ref, unit_ref, len_ref):
    text = text_ref[...].astype(F32)
    length = jnp.sqrt(jnp.sum(text * text, axis=-1, keepdims=True) + EPS)
    unit = text / length
    unit_ref[...] = unit
    len_ref[...] = jnp.broadcast_to(length, len_ref.shape)
    row = lax.broadcasted_iota(jnp.int32, (2, 128), 0)
    lane = lax.broadcasted_iota(jnp.int32, (2, 128), 1)
    ids = jnp.where(row == 0, ids_ref[0], ids_ref[1])
    ids = jnp.where(lane == 0, ids, 0).astype(F32)
    packed = jnp.concatenate([unit, ids], axis=1).astype(BF16)
    for copy in range(pack_ref.shape[0]):
        pack_ref[copy] = packed


def pack(pair_ids, text_feats, copies):
    width = text_feats.shape[1]
    return pl.pallas_call(
        pack_kernel,
        in_specs=[SMEM, VMEM],
        out_shape=[
            jax.ShapeDtypeStruct((copies, 2, width + 128), BF16),
            jax.ShapeDtypeStruct((2, width), F32),
            jax.ShapeDtypeStruct((2, 128), F32),
        ],
        compiler_params=SMALL,
        cost_estimate=pl.CostEstimate(
            flops=30_000_000_000, bytes_accessed=100_000, transcendentals=0
        ),
        name="pack",
    )(pair_ids, text_feats)


def forward_kernel(
    n_tensor, x_ref, gain_ref, bias_ref, b_down_ref, up_ref, down_ref,
    slope_ref, part_ref, act_sum, x_sum,
):
    step = pl.program_id(0)
    image = step // 2
    @pl.when(step == 0)
    def _():
        act_sum[...] = jnp.zeros_like(act_sum)
        x_sum[...] = jnp.zeros_like(x_sum)

    x = x_ref[...].astype(F32)
    normed, _ = norm_parts(x)
    normed = (normed * gain_ref[...][None, :]).astype(BF16)

    pre = lax.dot_general(normed, up_ref[...], LAST, preferred_element_type=F32)
    pre = pre + bias_ref[...][None, :]
    root = math.sqrt(2.0 / math.pi)
    square = pre * pre
    tanh = jnp.tanh(root * (pre + 0.044715 * (square * pre)))
    half = 0.5 * (1.0 + tanh)
    act = (pre * half).astype(BF16).astype(F32)
    slope = half + (0.5 * root) * pre * (1.0 - tanh * tanh) * (
        1.0 + (3.0 * 0.044715) * square
    )
    slope_ref[...] = slope.astype(BF16)

    def add(total, values):
        row = lax.broadcasted_iota(jnp.int32, total.shape, 0)
        sums = jnp.sum(values, axis=0, keepdims=True)
        total[...] += jnp.where(row == image, sums, 0.0)

    add(act_sum, act)
    add(x_sum, x)

    @pl.when(step == pl.num_programs(0) - 1)
    def _():
        stack = split_stack(act_sum[...] * (1.0 / PATCHES))
        mlp = unstack(jnp.dot(stack, down_ref[...], preferred_element_type=F32))
        rest = x_sum[...] * (1.0 / PATCHES) + b_down_ref[...][None, :]
        part = (mlp + rest * (1.0 / n_tensor))[0:2]
        for copy in range(n_tensor):
            part_ref[copy] = part


def forward(patches, ln_gain, up_t, b_up, w_down, b_down, n_tensor):
    tokens, width = patches.shape
    units = up_t.shape[0]
    rows = 128
    vector = lambda size: pl.BlockSpec((size,), lambda i: (0,))
    return pl.pallas_call(
        functools.partial(forward_kernel, n_tensor),
        grid=(tokens // rows,),
        in_specs=[
            pl.BlockSpec((rows, width), lambda i: (i, 0)),
            vector(width),
            vector(units),
            vector(width),
            pl.BlockSpec((units, width), lambda i: (0, 0)),
            pl.BlockSpec((units, width), lambda i: (0, 0)),
        ],
        out_specs=[
            pl.BlockSpec((rows, units), lambda i: (i, 0)),
            pl.BlockSpec((n_tensor, 2, width), lambda i: (0, 0, 0)),
        ],
        out_shape=[
            jax.ShapeDtypeStruct((tokens, units), BF16),
            jax.ShapeDtypeStruct((n_tensor, 2, width), F32),
        ],
        scratch_shapes=[
            pltpu.VMEM((8, units), F32),
            pltpu.VMEM((8, width), F32),
        ],
        compiler_params=SMALL,
        cost_estimate=pl.CostEstimate(
            flops=2 * tokens * width * units,
            bytes_accessed=2 * tokens * width + 4 * units * width + 4 * tokens * units,
            transcendentals=tokens * units,
        ),
        name="forward",
    )(patches, ln_gain, b_up, b_down, up_t, w_down)


def pick_row(rows, index):
    row = lax.broadcasted_iota(jnp.int32, rows.shape, 0)
    return jnp.sum(jnp.where(row == index, rows, 0.0), axis=0, keepdims=True)


def image_features(rows, gain):
    feat_n, feat_s = norm_parts(jnp.concatenate([rows] * 4, axis=0))
    features = feat_n * gain
    feat_len = jnp.sqrt(jnp.sum(features * features, axis=-1, keepdims=True) + EPS)
    return feat_n, feat_s, feat_len, features / feat_len


def pair_grad(queries, keys, ids_ref, id_columns, sharp, shift):
    batch = keys.shape[0]
    logits = sharp * unstack(
        lax.dot_general(split_stack(queries), keys, LAST, preferred_element_type=F32)
    ) + shift
    lane = lax.broadcasted_iota(jnp.int32, (16, 128), 1)
    first_lane = jnp.where(lane == 0, 1.0, 0.0).astype(BF16)
    ids = lax.dot_general(first_lane, id_columns, LAST, preferred_element_type=F32)[0:8]
    row = lax.broadcasted_iota(jnp.int32, (8, batch), 0)
    own = jnp.where(row == 0, ids_ref[0], ids_ref[1]).astype(F32)
    sign = jnp.where(ids == own, 1.0, -1.0)
    logit_grad = -LOSS_SCALE * sign * jax.nn.sigmoid(-sign * logits) / batch
    logit_grad = jnp.where(row < 2, logit_grad, 0.0)
    return sharp * unstack(
        jnp.dot(split_stack(logit_grad), keys, preferred_element_type=F32)
    )


def scalars(sharp_ref, shift_ref):
    return jnp.exp(sharp_ref[...][None, :]), shift_ref[...][None, :]


def loss_kernel(
    place_ref, ids_ref, sharp_ref, shift_ref, parts_ref, gain_ref, rows_ref, down_ref,
    up_ref, slope_ref, img_ref, hidden_ref, away_ref, keep_ref, g_pre,
):
    width = gain_ref.shape[0]
    core, one, two = places(place_ref[0])
    gain = gain_ref[...][None, :]
    pooled = parts_ref[0]
    for part in range(1, parts_ref.shape[0]):
        pooled = pooled + parts_ref[part]
    feat_n, feat_s, feat_len, img_emb = image_features(pooled, gain)
    for copy in range(img_ref.shape[0]):
        img_ref[copy] = img_emb[0:2].astype(BF16)
    g_img = pair_grad(
        img_emb, rows_ref[:, 0:width], ids_ref, rows_ref[:, width : width + 128],
        *scalars(sharp_ref, shift_ref),
    )
    g_feat = (
        g_img - img_emb * jnp.sum(img_emb * g_img, axis=-1, keepdims=True)
    ) / feat_len
    g_hidden = norm_back(g_feat, gain, feat_n, feat_s) * (1.0 / PATCHES)
    hidden_ref[...] = g_hidden[0:2]
    g_rows = jnp.concatenate([g_hidden, jnp.zeros_like(g_hidden)], axis=0).astype(BF16)
    g_act = lax.dot_general(g_rows, down_ref[...], LAST, preferred_element_type=F32)[0:8]
    for image, blocks, out_ref in (
        (1 - core, order(two, one), away_ref),
        (core, order(one, two), keep_ref),
    ):
        row = pick_row(g_act, image)
        for spot, block in enumerate(blocks):
            start = pl.multiple_of(image * PATCHES + block * BLOCK, BLOCK)
            g_pre[spot * BLOCK : (spot + 1) * BLOCK, :] = (
                slope_ref[pl.ds(start, BLOCK), :].astype(F32) * row
            ).astype(BF16)
        out_ref[...] = jnp.dot(
            g_pre[...], up_ref[...], preferred_element_type=F32
        ).astype(BF16)


def loss_and_back(
    place, sharp, shift, ids, parts, gain, rows, w_down, up_t, slope, copies
):
    units, width = up_t.shape
    return pl.pallas_call(
        loss_kernel,
        in_specs=[SMEM] * 2 + [VMEM] * 8,
        out_shape=[
            jax.ShapeDtypeStruct((copies, 2, width), BF16),
            jax.ShapeDtypeStruct((2, width), F32),
            jax.ShapeDtypeStruct((PATCHES, width), BF16),
            jax.ShapeDtypeStruct((PATCHES, width), BF16),
        ],
        scratch_shapes=[pltpu.VMEM((PATCHES, units), BF16)],
        compiler_params=SMALL,
        cost_estimate=pl.CostEstimate(
            flops=4 * PATCHES * width * units,
            bytes_accessed=6 * units * width + 8 * PATCHES * units,
            transcendentals=0,
        ),
        name="loss_and_back",
    )(place, ids, sharp, shift, parts, gain, rows, w_down, up_t, slope)


def text_kernel(
    ids_ref, sharp_ref, shift_ref, unit_ref, len_ref, img_ref, columns_ref, out_ref
):
    unit = unit_ref[...]
    queries = jnp.concatenate([unit] * 4, axis=0).astype(BF16).astype(F32)
    g_text = pair_grad(
        queries, img_ref[...], ids_ref, columns_ref[...],
        *scalars(sharp_ref, shift_ref),
    )[0:2]
    along = jnp.sum(unit * g_text, axis=-1, keepdims=True)
    out_ref[...] = (g_text - unit * along) / len_ref[:, 0:1]


def text_grad(sharp, shift, ids, unit, length, images, columns):
    return pl.pallas_call(
        text_kernel,
        in_specs=[SMEM] + [VMEM] * 6,
        out_shape=jax.ShapeDtypeStruct(unit.shape, F32),
        compiler_params=SMALL,
        cost_estimate=pl.CostEstimate(
            flops=1_000_000_000, bytes_accessed=600_000, transcendentals=0
        ),
        name="text_grad",
    )(ids, sharp, shift, unit, length, images, columns)


def finish_kernel(
    place_ref, keep_ref, other_ref, one_ref, two_ref, x_ref, hidden_ref, gain_ref, out_ref
):
    g_normed = keep_ref[...].astype(F32) + other_ref[...].astype(F32)
    g_normed = g_normed + one_ref[...].astype(F32) + two_ref[...].astype(F32)
    normed, inverse = norm_parts(x_ref[...].astype(F32))
    grad = norm_back(g_normed, gain_ref[...][None, :], normed, inverse)
    out_ref[...] = (grad + pick_row(hidden_ref[...], place_ref[0] & 1)).astype(BF16)


def finish(place, keep, other, got_one, got_two, patches, g_hidden, ln_gain):
    width = patches.shape[1]
    block = lambda index: pl.BlockSpec((BLOCK, width), index)

    def own_block(i, place):
        core, one, two = places(place[0])
        return core * (PATCHES // BLOCK) + 2 * one + two, 0

    return pl.pallas_call(
        finish_kernel,
        grid_spec=pltpu.PrefetchScalarGridSpec(
            num_scalar_prefetch=1,
            grid=(1,),
            in_specs=[
                block(lambda i, place: (3, 0)),
                block(lambda i, place: (3, 0)),
                block(lambda i, place: (1, 0)),
                block(lambda i, place: (0, 0)),
                block(own_block),
                pl.BlockSpec((2, width), lambda i, place: (0, 0)),
                pl.BlockSpec((width,), lambda i, place: (0,)),
            ],
            out_specs=block(lambda i, place: (0, 0)),
        ),
        out_shape=jax.ShapeDtypeStruct((BLOCK, width), BF16),
        compiler_params=SMALL,
        name="finish",
    )(place, keep, other, got_one, got_two, patches, g_hidden, ln_gain)


def place_kernel(place_ref, own, two, one, near, rest, out_ref):
    core, one_bit, two_bit = places(place_ref[0])
    low, high = slice(0, BLOCK), slice(BLOCK, 2 * BLOCK)
    mine, theirs = order(one_bit, two_bit), order(two_bit, one_bit)
    moves = [
        (one, high, core, mine[0]),
        (one, low, core, mine[1]),
        (two, low, core, mine[2]),
        (own, low, core, mine[3]),
        (rest, high, 1 - core, theirs[0]),
        (rest, low, 1 - core, theirs[1]),
        (near, high, 1 - core, theirs[2]),
        (near, low, 1 - core, theirs[3]),
    ]
    for ref, rows, image, block in moves:
        start = pl.multiple_of(image * PATCHES + block * BLOCK, BLOCK)
        out_ref[pl.ds(start, BLOCK), :] = ref[rows, :]


def put_in_place(place, pieces, tokens):
    width = pieces[0].shape[1]
    return pl.pallas_call(
        place_kernel,
        in_specs=[SMEM] + [VMEM] * 5,
        out_shape=jax.ShapeDtypeStruct((tokens, width), BF16),
        compiler_params=SMALL,
        name="put_in_place",
    )(place, *pieces)


def swap(value, axis, partner):
    size = lax.axis_size(axis)
    return lax.ppermute(value, axis, [(i, partner(i)) for i in range(size)])


def swap_core(value):
    return swap(value, "tensor", lambda i: i ^ 1)


def step_one(i):
    return i ^ 2 if i % 2 == 0 else (3 - i // 2) * 2 + 1


def step_two(i):
    return (3 - i // 2) * 2 if i % 2 == 0 else i ^ 2


def exchange(copies, groups, axis="dp"):
    return lax.all_to_all(
        copies, axis, split_axis=0, concat_axis=0, axis_index_groups=groups
    )


def copies_of(rows, count):
    return jnp.broadcast_to(rows[None], (count,) + rows.shape)


def on_device(
    patches,
    ln_gain,
    w_up,
    b_up,
    w_down,
    b_down,
    head_gain,
    text_feats,
    pair_ids,
    log_sharpness,
    pairwise_logit_shift,
):
    batch = text_feats.shape[0] * lax.axis_size("dp")
    place = lax.axis_index("tensor").astype(jnp.int32).reshape(1)

    count = lax.axis_size("dp")
    n_x, n_lo = 4, 2
    n_yz = count // n_x
    rest_of = [y * n_x * n_lo + lo for y in range(n_yz // n_lo) for lo in range(n_lo)]
    along_x = [[place + x * n_lo for x in range(n_x)] for place in rest_of]
    along_yz = [[place + x * n_lo for place in rest_of] for x in range(n_x)]
    packed, unit_text, text_len = pack(pair_ids, text_feats, n_yz)
    some_text = exchange(packed, along_yz).reshape(2 * n_yz, -1)

    up_t = w_up.T
    some_text, first_gain = lax.optimization_barrier((some_text, ln_gain))
    rows = exchange(copies_of(some_text, n_x), along_x).reshape(batch, -1)
    slope, parts = forward(
        patches, first_gain, up_t, b_up, w_down, b_down, lax.axis_size("tensor")
    )
    parts, rows = lax.optimization_barrier((parts, rows))
    parts = exchange(parts, None, "tensor")
    img_copies, g_hidden, away, keep = loss_and_back(
        place,
        log_sharpness,
        pairwise_logit_shift,
        pair_ids,
        parts,
        head_gain,
        rows,
        w_down,
        up_t,
        slope,
        n_x,
    )

    other = swap_core(away)

    def both(start, count):
        part = slice(start, start + count)
        return keep[part].astype(F32) + other[part].astype(F32)

    send_one = both(0, 128).astype(BF16)
    got_one = swap(send_one, "tensor", step_one)
    img_copies, _ = lax.optimization_barrier((img_copies, send_one))
    some_img = exchange(img_copies, along_x).reshape(2 * n_x, -1)
    got_one, some_img = lax.optimization_barrier((got_one, some_img))
    send_two = (both(128, 64) + got_one[:64].astype(F32)).astype(BF16)
    got_two = swap(send_two, "tensor", step_two)
    some_img, _ = lax.optimization_barrier((some_img, send_two))
    img_copies = copies_of(some_img, n_yz)
    got_two, img_copies = lax.optimization_barrier((got_two, img_copies))
    images = exchange(img_copies, along_yz).reshape(batch, -1)
    done = finish(place, keep, other, got_one, got_two, patches, g_hidden, ln_gain)

    from_two = swap(done, "tensor", step_two)
    pair = jnp.concatenate([done, from_two])
    from_one = swap(pair, "tensor", step_one)
    near = swap_core(pair)
    from_one, images = lax.optimization_barrier((from_one, images))
    rest = swap_core(from_one)
    grad_patches = put_in_place(
        place, (done, from_two, from_one, near, rest), patches.shape[0]
    )

    ids = rows[:, -128:].reshape(n_x, n_yz, 2, 128).swapaxes(0, 1).reshape(batch, 128)
    grad_text = text_grad(
        log_sharpness,
        pairwise_logit_shift,
        pair_ids,
        unit_text,
        text_len,
        images,
        ids,
    )
    return grad_patches, grad_text


def solution(mesh):
    in_specs = (
        P("dp", None),
        P(),
        P(None, "tensor"),
        P("tensor"),
        P("tensor", None),
        P(),
        P(),
        P("dp", None),
        P("dp"),
        P(),
        P(),
    )
    out_specs = (P("dp", None), P("dp", None))
    return jax.shard_map(
        on_device, mesh=mesh, in_specs=in_specs, out_specs=out_specs, check_vma=False
    )
```

```python
import functools
import math

import jax
import jax.numpy as jnp
from jax import lax
from jax.experimental import pallas as pl
from jax.experimental.pallas import tpu as pltpu
from jax.sharding import PartitionSpec as P

PATCHES = 256
BLOCK = 64
EPS = 1e-06
LOSS_SCALE = 131072.0
F32 = jnp.float32
BF16 = jnp.bfloat16
LAST = (((1,), (1,)), ((), ()))
SMEM = pl.BlockSpec(memory_space=pltpu.SMEM)
VMEM = pl.BlockSpec(memory_space=pltpu.VMEM)
SMALL = pltpu.CompilerParams(vmem_limit_bytes=16 * 1024 * 1024)


def places(position):
    core, ring = position & 1, position >> 1
    u, v = (ring ^ (ring >> 1)) & 1, ring >> 1
    swap = core * (u ^ v)
    return core, u ^ swap, v ^ swap


def order(one, two):
    return [3 - 2 * one - two, 2 - 2 * one + two, 2 * one + 1 - two, 2 * one + two]


def norm_parts(values):
    centre = values - jnp.mean(values, axis=-1, keepdims=True)
    inverse = lax.rsqrt(jnp.mean(centre * centre, axis=-1, keepdims=True) + EPS)
    return centre * inverse, inverse


def norm_back(grad_out, gain, normed, inverse):
    scaled = grad_out * gain
    return inverse * (
        scaled
        - jnp.mean(scaled, axis=-1, keepdims=True)
        - normed * jnp.mean(scaled * normed, axis=-1, keepdims=True)
    )


def split_stack(values):
    high = values.astype(BF16).astype(F32)
    rest = values - high
    mid = rest.astype(BF16).astype(F32)
    low = rest - mid
    return jnp.concatenate([high, mid, low, jnp.zeros_like(high)], axis=0).astype(BF16)


def unstack(sums):
    return (sums[0:8] + sums[8:16]) + sums[16:24]


def image_features(pooled_ref, gain):
    rows = pooled_ref[...]
    pooled = jnp.concatenate([rows] * 4, axis=0)
    feat_n, feat_s = norm_parts(pooled)
    features = feat_n * gain
    feat_len = jnp.sqrt(jnp.sum(features * features, axis=-1, keepdims=True) + EPS)
    return feat_n, feat_s, feat_len, features / feat_len


def pack_kernel(ids_ref, text_ref, pack_ref, unit_ref, len_ref):
    text = text_ref[...].astype(F32)
    length = jnp.sqrt(jnp.sum(text * text, axis=-1, keepdims=True) + EPS)
    unit = text / length
    unit_ref[...] = unit
    len_ref[...] = jnp.broadcast_to(length, len_ref.shape)
    row = lax.broadcasted_iota(jnp.int32, (2, 128), 0)
    lane = lax.broadcasted_iota(jnp.int32, (2, 128), 1)
    ids = jnp.where(row == 0, ids_ref[0], ids_ref[1])
    ids = jnp.where(lane == 0, ids, 0).astype(F32)
    packed = jnp.concatenate([unit, ids], axis=1).astype(BF16)
    for copy in range(pack_ref.shape[0]):
        pack_ref[copy] = packed


def pack(pair_ids, text_feats, copies):
    width = text_feats.shape[1]
    return pl.pallas_call(
        pack_kernel,
        in_specs=[SMEM, VMEM],
        out_shape=[
            jax.ShapeDtypeStruct((copies, 2, width + 128), BF16),
            jax.ShapeDtypeStruct((2, width), F32),
            jax.ShapeDtypeStruct((2, 128), F32),
        ],
        compiler_params=SMALL,
        cost_estimate=pl.CostEstimate(
            flops=30_000_000_000, bytes_accessed=100_000, transcendentals=0
        ),
        name="pack",
    )(pair_ids, text_feats)


def forward_kernel(
    n_tensor, x_ref, gain_ref, bias_ref, b_down_ref, up_ref, down_ref,
    slope_ref, part_ref, act_sum, x_sum,
):
    step = pl.program_id(0)
    image = step // 2
    @pl.when(step == 0)
    def _():
        act_sum[...] = jnp.zeros_like(act_sum)
        x_sum[...] = jnp.zeros_like(x_sum)

    x = x_ref[...].astype(F32)
    normed, _ = norm_parts(x)
    normed = (normed * gain_ref[...][None, :]).astype(BF16)

    pre = lax.dot_general(normed, up_ref[...], LAST, preferred_element_type=F32)
    pre = pre + bias_ref[...][None, :]
    root = math.sqrt(2.0 / math.pi)
    square = pre * pre
    tanh = jnp.tanh(root * (pre + 0.044715 * (square * pre)))
    half = 0.5 * (1.0 + tanh)
    act = (pre * half).astype(BF16).astype(F32)
    slope = half + (0.5 * root) * pre * (1.0 - tanh * tanh) * (
        1.0 + (3.0 * 0.044715) * square
    )
    slope_ref[...] = slope.astype(BF16)

    def add(total, values):
        row = lax.broadcasted_iota(jnp.int32, total.shape, 0)
        sums = jnp.sum(values, axis=0, keepdims=True)
        total[...] += jnp.where(row == image, sums, 0.0)

    add(act_sum, act)
    add(x_sum, x)

    @pl.when(step == pl.num_programs(0) - 1)
    def _():
        stack = split_stack(act_sum[...] * (1.0 / PATCHES))
        mlp = unstack(jnp.dot(stack, down_ref[...], preferred_element_type=F32))
        rest = x_sum[...] * (1.0 / PATCHES) + b_down_ref[...][None, :]
        part = (mlp + rest * (1.0 / n_tensor))[0:2]
        for copy in range(n_tensor):
            part_ref[copy] = part


def forward(patches, ln_gain, up_t, b_up, w_down, b_down, n_tensor):
    tokens, width = patches.shape
    units = up_t.shape[0]
    rows = 128
    vector = lambda size: pl.BlockSpec((size,), lambda i: (0,))
    return pl.pallas_call(
        functools.partial(forward_kernel, n_tensor),
        grid=(tokens // rows,),
        in_specs=[
            pl.BlockSpec((rows, width), lambda i: (i, 0)),
            vector(width),
            vector(units),
            vector(width),
            pl.BlockSpec((units, width), lambda i: (0, 0)),
            pl.BlockSpec((units, width), lambda i: (0, 0)),
        ],
        out_specs=[
            pl.BlockSpec((rows, units), lambda i: (i, 0)),
            pl.BlockSpec((n_tensor, 2, width), lambda i: (0, 0, 0)),
        ],
        out_shape=[
            jax.ShapeDtypeStruct((tokens, units), BF16),
            jax.ShapeDtypeStruct((n_tensor, 2, width), F32),
        ],
        scratch_shapes=[
            pltpu.VMEM((8, units), F32),
            pltpu.VMEM((8, width), F32),
        ],
        compiler_params=SMALL,
        cost_estimate=pl.CostEstimate(
            flops=2 * tokens * width * units,
            bytes_accessed=2 * tokens * width + 4 * units * width + 4 * tokens * units,
            transcendentals=tokens * units,
        ),
        name="forward",
    )(patches, ln_gain, b_up, b_down, up_t, w_down)


def pick_row(rows, index):
    row = lax.broadcasted_iota(jnp.int32, rows.shape, 0)
    return jnp.sum(jnp.where(row == index, rows, 0.0), axis=0, keepdims=True)


def image_features(rows, gain):
    feat_n, feat_s = norm_parts(jnp.concatenate([rows] * 4, axis=0))
    features = feat_n * gain
    feat_len = jnp.sqrt(jnp.sum(features * features, axis=-1, keepdims=True) + EPS)
    return feat_n, feat_s, feat_len, features / feat_len


def pair_grad(queries, keys, ids_ref, id_columns, sharp, shift):
    batch = keys.shape[0]
    logits = sharp * unstack(
        lax.dot_general(split_stack(queries), keys, LAST, preferred_element_type=F32)
    ) + shift
    lane = lax.broadcasted_iota(jnp.int32, (16, 128), 1)
    first_lane = jnp.where(lane == 0, 1.0, 0.0).astype(BF16)
    ids = lax.dot_general(first_lane, id_columns, LAST, preferred_element_type=F32)[0:8]
    row = lax.broadcasted_iota(jnp.int32, (8, batch), 0)
    own = jnp.where(row == 0, ids_ref[0], ids_ref[1]).astype(F32)
    sign = jnp.where(ids == own, 1.0, -1.0)
    logit_grad = -LOSS_SCALE * sign * jax.nn.sigmoid(-sign * logits) / batch
    logit_grad = jnp.where(row < 2, logit_grad, 0.0)
    return sharp * unstack(
        jnp.dot(split_stack(logit_grad), keys, preferred_element_type=F32)
    )


def scalars(sharp_ref, shift_ref):
    return jnp.exp(sharp_ref[...][None, :]), shift_ref[...][None, :]


def loss_kernel(
    place_ref, ids_ref, sharp_ref, shift_ref, parts_ref, gain_ref, rows_ref, down_ref,
    up_ref, slope_ref, img_ref, hidden_ref, away_ref, keep_ref, g_pre,
):
    width = gain_ref.shape[0]
    core, one, two = places(place_ref[0])
    gain = gain_ref[...][None, :]
    pooled = parts_ref[0]
    for part in range(1, parts_ref.shape[0]):
        pooled = pooled + parts_ref[part]
    feat_n, feat_s, feat_len, img_emb = image_features(pooled, gain)
    for copy in range(img_ref.shape[0]):
        img_ref[copy] = img_emb[0:2].astype(BF16)
    g_img = pair_grad(
        img_emb, rows_ref[:, 0:width], ids_ref, rows_ref[:, width : width + 128],
        *scalars(sharp_ref, shift_ref),
    )
    g_feat = (
        g_img - img_emb * jnp.sum(img_emb * g_img, axis=-1, keepdims=True)
    ) / feat_len
    g_hidden = norm_back(g_feat, gain, feat_n, feat_s) * (1.0 / PATCHES)
    hidden_ref[...] = g_hidden[0:2]
    g_rows = jnp.concatenate([g_hidden, jnp.zeros_like(g_hidden)], axis=0).astype(BF16)
    g_act = lax.dot_general(g_rows, down_ref[...], LAST, preferred_element_type=F32)[0:8]
    for image, blocks, out_ref in (
        (1 - core, order(two, one), away_ref),
        (core, order(one, two), keep_ref),
    ):
        row = pick_row(g_act, image)
        for spot, block in enumerate(blocks):
            start = pl.multiple_of(image * PATCHES + block * BLOCK, BLOCK)
            g_pre[spot * BLOCK : (spot + 1) * BLOCK, :] = (
                slope_ref[pl.ds(start, BLOCK), :].astype(F32) * row
            ).astype(BF16)
        out_ref[...] = jnp.dot(
            g_pre[...], up_ref[...], preferred_element_type=F32
        ).astype(BF16)


def loss_and_back(
    place, sharp, shift, ids, parts, gain, rows, w_down, up_t, slope, copies
):
    units, width = up_t.shape
    return pl.pallas_call(
        loss_kernel,
        in_specs=[SMEM] * 2 + [VMEM] * 8,
        out_shape=[
            jax.ShapeDtypeStruct((copies, 2, width), BF16),
            jax.ShapeDtypeStruct((2, width), F32),
            jax.ShapeDtypeStruct((PATCHES, width), BF16),
            jax.ShapeDtypeStruct((PATCHES, width), BF16),
        ],
        scratch_shapes=[pltpu.VMEM((PATCHES, units), BF16)],
        compiler_params=SMALL,
        cost_estimate=pl.CostEstimate(
            flops=4 * PATCHES * width * units,
            bytes_accessed=6 * units * width + 8 * PATCHES * units,
            transcendentals=0,
        ),
        name="loss_and_back",
    )(place, ids, sharp, shift, parts, gain, rows, w_down, up_t, slope)


def text_kernel(
    ids_ref, sharp_ref, shift_ref, unit_ref, len_ref, img_ref, columns_ref, out_ref
):
    unit = unit_ref[...]
    queries = jnp.concatenate([unit] * 4, axis=0).astype(BF16).astype(F32)
    g_text = pair_grad(
        queries, img_ref[...], ids_ref, columns_ref[...],
        *scalars(sharp_ref, shift_ref),
    )[0:2]
    along = jnp.sum(unit * g_text, axis=-1, keepdims=True)
    out_ref[...] = (g_text - unit * along) / len_ref[:, 0:1]


def text_grad(sharp, shift, ids, unit, length, images, columns):
    return pl.pallas_call(
        text_kernel,
        in_specs=[SMEM] + [VMEM] * 6,
        out_shape=jax.ShapeDtypeStruct(unit.shape, F32),
        compiler_params=SMALL,
        cost_estimate=pl.CostEstimate(
            flops=1_000_000_000, bytes_accessed=600_000, transcendentals=0
        ),
        name="text_grad",
    )(ids, sharp, shift, unit, length, images, columns)


def finish_kernel(
    place_ref, keep_ref, other_ref, one_ref, two_ref, x_ref, hidden_ref, gain_ref, out_ref
):
    g_normed = keep_ref[...].astype(F32) + other_ref[...].astype(F32)
    g_normed = g_normed + one_ref[...].astype(F32) + two_ref[...].astype(F32)
    normed, inverse = norm_parts(x_ref[...].astype(F32))
    grad = norm_back(g_normed, gain_ref[...][None, :], normed, inverse)
    out_ref[...] = (grad + pick_row(hidden_ref[...], place_ref[0] & 1)).astype(BF16)


def finish(place, keep, other, got_one, got_two, patches, g_hidden, ln_gain):
    width = patches.shape[1]
    block = lambda index: pl.BlockSpec((BLOCK, width), index)

    def own_block(i, place):
        core, one, two = places(place[0])
        return core * (PATCHES // BLOCK) + 2 * one + two, 0

    return pl.pallas_call(
        finish_kernel,
        grid_spec=pltpu.PrefetchScalarGridSpec(
            num_scalar_prefetch=1,
            grid=(1,),
            in_specs=[
                block(lambda i, place: (3, 0)),
                block(lambda i, place: (3, 0)),
                block(lambda i, place: (1, 0)),
                block(lambda i, place: (0, 0)),
                block(own_block),
                pl.BlockSpec((2, width), lambda i, place: (0, 0)),
                pl.BlockSpec((width,), lambda i, place: (0,)),
            ],
            out_specs=block(lambda i, place: (0, 0)),
        ),
        out_shape=jax.ShapeDtypeStruct((BLOCK, width), BF16),
        compiler_params=SMALL,
        cost_estimate=pl.CostEstimate(
            flops=5_000_000_000, bytes_accessed=1_000_000, transcendentals=0
        ),
        name="finish",
    )(place, keep, other, got_one, got_two, patches, g_hidden, ln_gain)


def place_kernel(place_ref, own, two, one, near, rest, out_ref):
    core, one_bit, two_bit = places(place_ref[0])
    low, high = slice(0, BLOCK), slice(BLOCK, 2 * BLOCK)
    mine, theirs = order(one_bit, two_bit), order(two_bit, one_bit)
    moves = [
        (one, high, core, mine[0]),
        (one, low, core, mine[1]),
        (two, low, core, mine[2]),
        (own, low, core, mine[3]),
        (rest, high, 1 - core, theirs[0]),
        (rest, low, 1 - core, theirs[1]),
        (near, high, 1 - core, theirs[2]),
        (near, low, 1 - core, theirs[3]),
    ]
    for ref, rows, image, block in moves:
        start = pl.multiple_of(image * PATCHES + block * BLOCK, BLOCK)
        out_ref[pl.ds(start, BLOCK), :] = ref[rows, :]


def put_in_place(place, pieces, tokens):
    width = pieces[0].shape[1]
    return pl.pallas_call(
        place_kernel,
        in_specs=[SMEM] + [VMEM] * 5,
        out_shape=jax.ShapeDtypeStruct((tokens, width), BF16),
        compiler_params=SMALL,
        name="put_in_place",
    )(place, *pieces)


def swap(value, axis, partner):
    size = lax.axis_size(axis)
    return lax.ppermute(value, axis, [(i, partner(i)) for i in range(size)])


def swap_core(value):
    return swap(value, "tensor", lambda i: i ^ 1)


def step_one(i):
    return i ^ 2 if i % 2 == 0 else (3 - i // 2) * 2 + 1


def step_two(i):
    return (3 - i // 2) * 2 if i % 2 == 0 else i ^ 2


def exchange(copies, groups, axis="dp"):
    return lax.all_to_all(
        copies, axis, split_axis=0, concat_axis=0, axis_index_groups=groups
    )


def spread(rows, groups):
    copies = jnp.broadcast_to(rows[None], (len(groups[0]),) + rows.shape)
    return exchange(copies, groups)


def on_device(
    patches,
    ln_gain,
    w_up,
    b_up,
    w_down,
    b_down,
    head_gain,
    text_feats,
    pair_ids,
    log_sharpness,
    pairwise_logit_shift,
):
    batch = text_feats.shape[0] * lax.axis_size("dp")
    place = lax.axis_index("tensor").astype(jnp.int32).reshape(1)

    side = math.isqrt(lax.axis_size("dp"))
    along_y = [[y * side + k for y in range(side)] for k in range(side)]
    along_xz = [[y * side + k for k in range(side)] for y in range(side)]
    packed, unit_text, text_len = pack(pair_ids, text_feats, side)
    some_text = exchange(packed, along_y).reshape(2 * side, -1)

    up_t = w_up.T
    some_text, first_gain = lax.optimization_barrier((some_text, ln_gain))
    rows = spread(some_text, along_xz).reshape(batch, -1)
    slope, parts = forward(
        patches, first_gain, up_t, b_up, w_down, b_down, lax.axis_size("tensor")
    )
    parts, rows = lax.optimization_barrier((parts, rows))
    parts = exchange(parts, None, "tensor")
    img_copies, g_hidden, away, keep = loss_and_back(
        place,
        log_sharpness,
        pairwise_logit_shift,
        pair_ids,
        parts,
        head_gain,
        rows,
        w_down,
        up_t,
        slope,
        side,
    )

    other = swap_core(away)

    def both(start, count):
        part = slice(start, start + count)
        return keep[part].astype(F32) + other[part].astype(F32)

    send_one = both(0, 128).astype(BF16)
    got_one = swap(send_one, "tensor", step_one)
    img_copies, _ = lax.optimization_barrier((img_copies, send_one))
    some_img = exchange(img_copies, along_xz).reshape(2 * side, -1)
    got_one, some_img = lax.optimization_barrier((got_one, some_img))
    send_two = (both(128, 64) + got_one[:64].astype(F32)).astype(BF16)
    got_two = swap(send_two, "tensor", step_two)
    some_img, _ = lax.optimization_barrier((some_img, send_two))
    images = spread(some_img, along_y).reshape(batch, -1)
    done = finish(place, keep, other, got_one, got_two, patches, g_hidden, ln_gain)

    from_two = swap(done, "tensor", step_two)
    ids = rows[:, -128:].reshape(side, side, 2, 128).swapaxes(0, 1).reshape(batch, 128)
    grad_text = text_grad(
        log_sharpness,
        pairwise_logit_shift,
        pair_ids,
        unit_text,
        text_len,
        images,
        ids,
    )
    from_two, grad_text = lax.optimization_barrier((from_two, grad_text))
    pair = jnp.concatenate([done, from_two])
    from_one = swap(pair, "tensor", step_one)
    near = swap_core(pair)
    rest = swap_core(from_one)
    grad_patches = put_in_place(
        place, (done, from_two, from_one, near, rest), patches.shape[0]
    )

    return grad_patches, grad_text


def solution(mesh):
    in_specs = (
        P("dp", None),
        P(),
        P(None, "tensor"),
        P("tensor"),
        P("tensor", None),
        P(),
        P(),
        P("dp", None),
        P("dp"),
        P(),
        P(),
    )
    out_specs = (P("dp", None), P("dp", None))
    return jax.shard_map(
        on_device, mesh=mesh, in_specs=in_specs, out_specs=out_specs, check_vma=False
    )
```

```python
import functools
import math

import jax
import jax.numpy as jnp
from jax import lax
from jax.experimental import pallas as pl
from jax.experimental.pallas import tpu as pltpu
from jax.sharding import PartitionSpec as P

PATCHES = 256
BLOCK = 64
EPS = 1e-06
LOSS_SCALE = 131072.0
F32 = jnp.float32
BF16 = jnp.bfloat16
LAST = (((1,), (1,)), ((), ()))
SMEM = pl.BlockSpec(memory_space=pltpu.SMEM)
VMEM = pl.BlockSpec(memory_space=pltpu.VMEM)
SMALL = pltpu.CompilerParams(vmem_limit_bytes=16 * 1024 * 1024)


def places(position):
    core, ring = position & 1, position >> 1
    u, v = (ring ^ (ring >> 1)) & 1, ring >> 1
    swap = core * (u ^ v)
    return core, u ^ swap, v ^ swap


def order(one, two):
    return [3 - 2 * one - two, 2 - 2 * one + two, 2 * one + 1 - two, 2 * one + two]


def norm_parts(values):
    centre = values - jnp.mean(values, axis=-1, keepdims=True)
    inverse = lax.rsqrt(jnp.mean(centre * centre, axis=-1, keepdims=True) + EPS)
    return centre * inverse, inverse


def norm_back(grad_out, gain, normed, inverse):
    scaled = grad_out * gain
    return inverse * (
        scaled
        - jnp.mean(scaled, axis=-1, keepdims=True)
        - normed * jnp.mean(scaled * normed, axis=-1, keepdims=True)
    )


def split_stack(values):
    high = values.astype(BF16).astype(F32)
    rest = values - high
    mid = rest.astype(BF16).astype(F32)
    low = rest - mid
    return jnp.concatenate([high, mid, low, jnp.zeros_like(high)], axis=0).astype(BF16)


def unstack(sums):
    return (sums[0:8] + sums[8:16]) + sums[16:24]


def image_features(pooled_ref, gain):
    rows = pooled_ref[...]
    pooled = jnp.concatenate([rows] * 4, axis=0)
    feat_n, feat_s = norm_parts(pooled)
    features = feat_n * gain
    feat_len = jnp.sqrt(jnp.sum(features * features, axis=-1, keepdims=True) + EPS)
    return feat_n, feat_s, feat_len, features / feat_len


def pack_kernel(ids_ref, text_ref, pack_ref, unit_ref, len_ref):
    text = text_ref[...].astype(F32)
    length = jnp.sqrt(jnp.sum(text * text, axis=-1, keepdims=True) + EPS)
    unit = text / length
    unit_ref[...] = unit
    len_ref[...] = jnp.broadcast_to(length, len_ref.shape)
    row = lax.broadcasted_iota(jnp.int32, (2, 128), 0)
    lane = lax.broadcasted_iota(jnp.int32, (2, 128), 1)
    ids = jnp.where(row == 0, ids_ref[0], ids_ref[1])
    ids = jnp.where(lane == 0, ids, 0).astype(F32)
    packed = jnp.concatenate([unit, ids], axis=1).astype(BF16)
    for copy in range(pack_ref.shape[0]):
        pack_ref[copy] = packed


def pack(pair_ids, text_feats, copies):
    width = text_feats.shape[1]
    return pl.pallas_call(
        pack_kernel,
        in_specs=[SMEM, VMEM],
        out_shape=[
            jax.ShapeDtypeStruct((copies, 2, width + 128), BF16),
            jax.ShapeDtypeStruct((2, width), F32),
            jax.ShapeDtypeStruct((2, 128), F32),
        ],
        compiler_params=SMALL,
        cost_estimate=pl.CostEstimate(
            flops=30_000_000_000, bytes_accessed=100_000, transcendentals=0
        ),
        name="pack",
    )(pair_ids, text_feats)


def forward_kernel(
    n_tensor, x_ref, gain_ref, bias_ref, b_down_ref, up_ref, down_ref,
    slope_ref, part_ref, act_sum, x_sum,
):
    step = pl.program_id(0)
    image = step // 2
    @pl.when(step == 0)
    def _():
        act_sum[...] = jnp.zeros_like(act_sum)
        x_sum[...] = jnp.zeros_like(x_sum)

    x = x_ref[...].astype(F32)
    normed, _ = norm_parts(x)
    normed = (normed * gain_ref[...][None, :]).astype(BF16)

    pre = lax.dot_general(normed, up_ref[...], LAST, preferred_element_type=F32)
    pre = pre + bias_ref[...][None, :]
    root = math.sqrt(2.0 / math.pi)
    square = pre * pre
    tanh = jnp.tanh(root * (pre + 0.044715 * (square * pre)))
    half = 0.5 * (1.0 + tanh)
    act = (pre * half).astype(BF16).astype(F32)
    slope = half + (0.5 * root) * pre * (1.0 - tanh * tanh) * (
        1.0 + (3.0 * 0.044715) * square
    )
    slope_ref[...] = slope.astype(BF16)

    def add(total, values):
        row = lax.broadcasted_iota(jnp.int32, total.shape, 0)
        sums = jnp.sum(values, axis=0, keepdims=True)
        total[...] += jnp.where(row == image, sums, 0.0)

    add(act_sum, act)
    add(x_sum, x)

    @pl.when(step == pl.num_programs(0) - 1)
    def _():
        stack = split_stack(act_sum[...] * (1.0 / PATCHES))
        mlp = unstack(jnp.dot(stack, down_ref[...], preferred_element_type=F32))
        rest = x_sum[...] * (1.0 / PATCHES) + b_down_ref[...][None, :]
        part = (mlp + rest * (1.0 / n_tensor))[0:2]
        for copy in range(n_tensor):
            part_ref[copy] = part


def forward(patches, ln_gain, up_t, b_up, w_down, b_down, n_tensor):
    tokens, width = patches.shape
    units = up_t.shape[0]
    rows = 128
    vector = lambda size: pl.BlockSpec((size,), lambda i: (0,))
    return pl.pallas_call(
        functools.partial(forward_kernel, n_tensor),
        grid=(tokens // rows,),
        in_specs=[
            pl.BlockSpec((rows, width), lambda i: (i, 0)),
            vector(width),
            vector(units),
            vector(width),
            pl.BlockSpec((units, width), lambda i: (0, 0)),
            pl.BlockSpec((units, width), lambda i: (0, 0)),
        ],
        out_specs=[
            pl.BlockSpec((rows, units), lambda i: (i, 0)),
            pl.BlockSpec((n_tensor, 2, width), lambda i: (0, 0, 0)),
        ],
        out_shape=[
            jax.ShapeDtypeStruct((tokens, units), BF16),
            jax.ShapeDtypeStruct((n_tensor, 2, width), F32),
        ],
        scratch_shapes=[
            pltpu.VMEM((8, units), F32),
            pltpu.VMEM((8, width), F32),
        ],
        compiler_params=SMALL,
        cost_estimate=pl.CostEstimate(
            flops=2 * tokens * width * units,
            bytes_accessed=2 * tokens * width + 4 * units * width + 4 * tokens * units,
            transcendentals=tokens * units,
        ),
        name="forward",
    )(patches, ln_gain, b_up, b_down, up_t, w_down)


def pick_row(rows, index):
    row = lax.broadcasted_iota(jnp.int32, rows.shape, 0)
    return jnp.sum(jnp.where(row == index, rows, 0.0), axis=0, keepdims=True)


def image_features(rows, gain):
    feat_n, feat_s = norm_parts(jnp.concatenate([rows] * 4, axis=0))
    features = feat_n * gain
    feat_len = jnp.sqrt(jnp.sum(features * features, axis=-1, keepdims=True) + EPS)
    return feat_n, feat_s, feat_len, features / feat_len


def pair_grad(queries, keys, ids_ref, id_columns, sharp, shift):
    batch = keys.shape[0]
    logits = sharp * unstack(
        lax.dot_general(split_stack(queries), keys, LAST, preferred_element_type=F32)
    ) + shift
    lane = lax.broadcasted_iota(jnp.int32, (16, 128), 1)
    first_lane = jnp.where(lane == 0, 1.0, 0.0).astype(BF16)
    ids = lax.dot_general(first_lane, id_columns, LAST, preferred_element_type=F32)[0:8]
    row = lax.broadcasted_iota(jnp.int32, (8, batch), 0)
    own = jnp.where(row == 0, ids_ref[0], ids_ref[1]).astype(F32)
    sign = jnp.where(ids == own, 1.0, -1.0)
    logit_grad = -LOSS_SCALE * sign * jax.nn.sigmoid(-sign * logits) / batch
    logit_grad = jnp.where(row < 2, logit_grad, 0.0)
    return sharp * unstack(
        jnp.dot(split_stack(logit_grad), keys, preferred_element_type=F32)
    )


def scalars(sharp_ref, shift_ref):
    return jnp.exp(sharp_ref[...][None, :]), shift_ref[...][None, :]


def loss_kernel(
    place_ref, ids_ref, sharp_ref, shift_ref, parts_ref, gain_ref, rows_ref, down_ref,
    up_ref, slope_ref, img_ref, hidden_ref, away_ref, keep_ref, g_pre,
):
    width = gain_ref.shape[0]
    core, one, two = places(place_ref[0])
    gain = gain_ref[...][None, :]
    pooled = parts_ref[0]
    for part in range(1, parts_ref.shape[0]):
        pooled = pooled + parts_ref[part]
    feat_n, feat_s, feat_len, img_emb = image_features(pooled, gain)
    for copy in range(img_ref.shape[0]):
        img_ref[copy] = img_emb[0:2].astype(BF16)
    g_img = pair_grad(
        img_emb, rows_ref[:, 0:width], ids_ref, rows_ref[:, width : width + 128],
        *scalars(sharp_ref, shift_ref),
    )
    g_feat = (
        g_img - img_emb * jnp.sum(img_emb * g_img, axis=-1, keepdims=True)
    ) / feat_len
    g_hidden = norm_back(g_feat, gain, feat_n, feat_s) * (1.0 / PATCHES)
    hidden_ref[...] = g_hidden[0:2]
    g_rows = jnp.concatenate([g_hidden, jnp.zeros_like(g_hidden)], axis=0).astype(BF16)
    g_act = lax.dot_general(g_rows, down_ref[...], LAST, preferred_element_type=F32)[0:8]
    for image, blocks, out_ref in (
        (1 - core, order(two, one), away_ref),
        (core, order(one, two), keep_ref),
    ):
        row = pick_row(g_act, image)
        for spot, block in enumerate(blocks):
            start = pl.multiple_of(image * PATCHES + block * BLOCK, BLOCK)
            g_pre[spot * BLOCK : (spot + 1) * BLOCK, :] = (
                slope_ref[pl.ds(start, BLOCK), :].astype(F32) * row
            ).astype(BF16)
        out_ref[...] = jnp.dot(
            g_pre[...], up_ref[...], preferred_element_type=F32
        ).astype(BF16)


def loss_and_back(
    place, sharp, shift, ids, parts, gain, rows, w_down, up_t, slope, copies
):
    units, width = up_t.shape
    return pl.pallas_call(
        loss_kernel,
        in_specs=[SMEM] * 2 + [VMEM] * 8,
        out_shape=[
            jax.ShapeDtypeStruct((copies, 2, width), BF16),
            jax.ShapeDtypeStruct((2, width), F32),
            jax.ShapeDtypeStruct((PATCHES, width), BF16),
            jax.ShapeDtypeStruct((PATCHES, width), BF16),
        ],
        scratch_shapes=[pltpu.VMEM((PATCHES, units), BF16)],
        compiler_params=SMALL,
        cost_estimate=pl.CostEstimate(
            flops=4 * PATCHES * width * units,
            bytes_accessed=6 * units * width + 8 * PATCHES * units,
            transcendentals=0,
        ),
        name="loss_and_back",
    )(place, ids, sharp, shift, parts, gain, rows, w_down, up_t, slope)


def text_kernel(
    ids_ref, sharp_ref, shift_ref, unit_ref, len_ref, img_ref, columns_ref, out_ref
):
    unit = unit_ref[...]
    queries = jnp.concatenate([unit] * 4, axis=0).astype(BF16).astype(F32)
    g_text = pair_grad(
        queries, img_ref[...], ids_ref, columns_ref[...],
        *scalars(sharp_ref, shift_ref),
    )[0:2]
    along = jnp.sum(unit * g_text, axis=-1, keepdims=True)
    out_ref[...] = (g_text - unit * along) / len_ref[:, 0:1]


def text_grad(sharp, shift, ids, unit, length, images, columns):
    return pl.pallas_call(
        text_kernel,
        in_specs=[SMEM] + [VMEM] * 6,
        out_shape=jax.ShapeDtypeStruct(unit.shape, F32),
        compiler_params=SMALL,
        cost_estimate=pl.CostEstimate(
            flops=1_000_000_000, bytes_accessed=600_000, transcendentals=0
        ),
        name="text_grad",
    )(ids, sharp, shift, unit, length, images, columns)


def finish_kernel(place_ref, mine_ref, one_ref, two_ref, x_ref, hidden_ref, gain_ref, out_ref):
    g_normed = mine_ref[...] + one_ref[BLOCK:, :].astype(F32) + two_ref[...].astype(F32)
    normed, inverse = norm_parts(x_ref[...].astype(F32))
    grad = norm_back(g_normed, gain_ref[...][None, :], normed, inverse)
    out_ref[...] = (grad + pick_row(hidden_ref[...], place_ref[0] & 1)).astype(BF16)


def finish(place, mine, got_one, got_two, own_x, g_hidden, ln_gain):
    return pl.pallas_call(
        finish_kernel,
        in_specs=[SMEM] + [VMEM] * 6,
        out_shape=jax.ShapeDtypeStruct(mine.shape, BF16),
        compiler_params=SMALL,
        cost_estimate=pl.CostEstimate(
            flops=5_000_000_000, bytes_accessed=1_000_000, transcendentals=0
        ),
        name="finish",
    )(place, mine, got_one, got_two, own_x, g_hidden, ln_gain)


def place_kernel(place_ref, own, two, one, near, rest, out_ref):
    core, one_bit, two_bit = places(place_ref[0])
    low, high = slice(0, BLOCK), slice(BLOCK, 2 * BLOCK)
    mine, theirs = order(one_bit, two_bit), order(two_bit, one_bit)
    moves = [
        (one, high, core, mine[0]),
        (one, low, core, mine[1]),
        (two, low, core, mine[2]),
        (own, low, core, mine[3]),
        (rest, high, 1 - core, theirs[0]),
        (rest, low, 1 - core, theirs[1]),
        (near, high, 1 - core, theirs[2]),
        (near, low, 1 - core, theirs[3]),
    ]
    for ref, rows, image, block in moves:
        start = pl.multiple_of(image * PATCHES + block * BLOCK, BLOCK)
        out_ref[pl.ds(start, BLOCK), :] = ref[rows, :]


def put_in_place(place, pieces, tokens):
    width = pieces[0].shape[1]
    return pl.pallas_call(
        place_kernel,
        in_specs=[SMEM] + [VMEM] * 5,
        out_shape=jax.ShapeDtypeStruct((tokens, width), BF16),
        compiler_params=SMALL,
        name="put_in_place",
    )(place, *pieces)


def swap(value, axis, partner):
    size = lax.axis_size(axis)
    return lax.ppermute(value, axis, [(i, partner(i)) for i in range(size)])


def swap_core(value):
    return swap(value, "tensor", lambda i: i ^ 1)


def step_one(i):
    return i ^ 2 if i % 2 == 0 else (3 - i // 2) * 2 + 1


def step_two(i):
    return (3 - i // 2) * 2 if i % 2 == 0 else i ^ 2


def exchange(copies, groups, axis="dp"):
    return lax.all_to_all(
        copies, axis, split_axis=0, concat_axis=0, axis_index_groups=groups
    )


def spread(rows, groups):
    copies = jnp.broadcast_to(rows[None], (len(groups[0]),) + rows.shape)
    return exchange(copies, groups)


def on_device(
    patches,
    ln_gain,
    w_up,
    b_up,
    w_down,
    b_down,
    head_gain,
    text_feats,
    pair_ids,
    log_sharpness,
    pairwise_logit_shift,
):
    batch = text_feats.shape[0] * lax.axis_size("dp")
    place = lax.axis_index("tensor").astype(jnp.int32).reshape(1)

    side = math.isqrt(lax.axis_size("dp"))
    along_y = [[y * side + k for y in range(side)] for k in range(side)]
    along_xz = [[y * side + k for k in range(side)] for y in range(side)]
    packed, unit_text, text_len = pack(pair_ids, text_feats, side)
    some_text = exchange(packed, along_y).reshape(2 * side, -1)

    up_t = w_up.T
    some_text, first_gain = lax.optimization_barrier((some_text, ln_gain))
    rows = spread(some_text, along_xz).reshape(batch, -1)
    slope, parts = forward(
        patches, first_gain, up_t, b_up, w_down, b_down, lax.axis_size("tensor")
    )
    parts, rows = lax.optimization_barrier((parts, rows))
    parts = exchange(parts, None, "tensor")
    img_copies, g_hidden, away, keep = loss_and_back(
        place,
        log_sharpness,
        pairwise_logit_shift,
        pair_ids,
        parts,
        head_gain,
        rows,
        w_down,
        up_t,
        slope,
        side,
    )

    other = swap_core(away)

    def both(start, count):
        part = slice(start, start + count)
        return keep[part].astype(F32) + other[part].astype(F32)

    send_one = both(0, 128).astype(BF16)
    got_one = swap(send_one, "tensor", step_one)
    img_copies, _ = lax.optimization_barrier((img_copies, send_one))
    some_img = exchange(img_copies, along_xz).reshape(2 * side, -1)
    core, one, two = places(place[0])
    own_start = core * PATCHES + (2 * one + two) * BLOCK
    own_x = lax.dynamic_slice_in_dim(patches, own_start, BLOCK, 0)
    got_one, some_img, travels, mine, own_x = lax.optimization_barrier(
        (got_one, some_img, both(128, 64), both(192, 64), own_x)
    )
    send_two = (travels + got_one[:BLOCK].astype(F32)).astype(BF16)
    got_two = swap(send_two, "tensor", step_two)
    some_img, _ = lax.optimization_barrier((some_img, send_two))
    images = spread(some_img, along_y).reshape(batch, -1)
    done = finish(place, mine, got_one, got_two, own_x, g_hidden, ln_gain)

    from_two = swap(done, "tensor", step_two)
    ids = rows[:, -128:].reshape(side, side, 2, 128).swapaxes(0, 1).reshape(batch, 128)
    grad_text = text_grad(
        log_sharpness,
        pairwise_logit_shift,
        pair_ids,
        unit_text,
        text_len,
        images,
        ids,
    )
    from_two, grad_text = lax.optimization_barrier((from_two, grad_text))
    pair = jnp.concatenate([done, from_two])
    from_one = swap(pair, "tensor", step_one)
    near = swap_core(pair)
    rest = swap_core(from_one)
    grad_patches = put_in_place(
        place, (done, from_two, from_one, near, rest), patches.shape[0]
    )

    return grad_patches, grad_text


def solution(mesh):
    in_specs = (
        P("dp", None),
        P(),
        P(None, "tensor"),
        P("tensor"),
        P("tensor", None),
        P(),
        P(),
        P("dp", None),
        P("dp"),
        P(),
        P(),
    )
    out_specs = (P("dp", None), P("dp", None))
    return jax.shard_map(
        on_device, mesh=mesh, in_specs=in_specs, out_specs=out_specs, check_vma=False
    )
```

```python
import functools
import math

import jax
import jax.numpy as jnp
from jax import lax
from jax.experimental import pallas as pl
from jax.experimental.pallas import tpu as pltpu
from jax.sharding import PartitionSpec as P

PATCHES = 256
BLOCK = 64
EPS = 1e-06
LOSS_SCALE = 131072.0
F32 = jnp.float32
BF16 = jnp.bfloat16
LAST = (((1,), (1,)), ((), ()))
SMEM = pl.BlockSpec(memory_space=pltpu.SMEM)
VMEM = pl.BlockSpec(memory_space=pltpu.VMEM)
SMALL = pltpu.CompilerParams(vmem_limit_bytes=16 * 1024 * 1024)


def places(position):
    core, ring = position & 1, position >> 1
    u, v = (ring ^ (ring >> 1)) & 1, ring >> 1
    swap = core * (u ^ v)
    return core, u ^ swap, v ^ swap


def order(one, two):
    return [3 - 2 * one - two, 2 - 2 * one + two, 2 * one + 1 - two, 2 * one + two]


def norm_parts(values):
    centre = values - jnp.mean(values, axis=-1, keepdims=True)
    inverse = lax.rsqrt(jnp.mean(centre * centre, axis=-1, keepdims=True) + EPS)
    return centre * inverse, inverse


def norm_back(grad_out, gain, normed, inverse):
    scaled = grad_out * gain
    return inverse * (
        scaled
        - jnp.mean(scaled, axis=-1, keepdims=True)
        - normed * jnp.mean(scaled * normed, axis=-1, keepdims=True)
    )


def split_stack(values):
    high = values.astype(BF16).astype(F32)
    rest = values - high
    mid = rest.astype(BF16).astype(F32)
    low = rest - mid
    return jnp.concatenate([high, mid, low, jnp.zeros_like(high)], axis=0).astype(BF16)


def unstack(sums):
    return (sums[0:8] + sums[8:16]) + sums[16:24]


def image_features(pooled_ref, gain):
    rows = pooled_ref[...]
    pooled = jnp.concatenate([rows] * 4, axis=0)
    feat_n, feat_s = norm_parts(pooled)
    features = feat_n * gain
    feat_len = jnp.sqrt(jnp.sum(features * features, axis=-1, keepdims=True) + EPS)
    return feat_n, feat_s, feat_len, features / feat_len


def pack_kernel(ids_ref, text_ref, pack_ref, unit_ref, len_ref):
    text = text_ref[...].astype(F32)
    length = jnp.sqrt(jnp.sum(text * text, axis=-1, keepdims=True) + EPS)
    unit = text / length
    unit_ref[...] = unit
    len_ref[...] = jnp.broadcast_to(length, len_ref.shape)
    row = lax.broadcasted_iota(jnp.int32, (2, 128), 0)
    lane = lax.broadcasted_iota(jnp.int32, (2, 128), 1)
    ids = jnp.where(row == 0, ids_ref[0], ids_ref[1])
    ids = jnp.where(lane == 0, ids, 0).astype(F32)
    packed = jnp.concatenate([unit, ids], axis=1).astype(BF16)
    for copy in range(pack_ref.shape[0]):
        pack_ref[copy] = packed


def pack(pair_ids, text_feats, copies):
    width = text_feats.shape[1]
    return pl.pallas_call(
        pack_kernel,
        in_specs=[SMEM, VMEM],
        out_shape=[
            jax.ShapeDtypeStruct((copies, 2, width + 128), BF16),
            jax.ShapeDtypeStruct((2, width), F32),
            jax.ShapeDtypeStruct((2, 128), F32),
        ],
        compiler_params=SMALL,
        cost_estimate=pl.CostEstimate(
            flops=30_000_000_000, bytes_accessed=100_000, transcendentals=0
        ),
        name="pack",
    )(pair_ids, text_feats)


def forward_kernel(
    n_tensor, x_ref, gain_ref, bias_ref, b_down_ref, up_ref, down_ref,
    slope_ref, part_ref, act_sum, x_sum,
):
    step = pl.program_id(0)
    image = step // 2
    @pl.when(step == 0)
    def _():
        act_sum[...] = jnp.zeros_like(act_sum)
        x_sum[...] = jnp.zeros_like(x_sum)

    x = x_ref[...].astype(F32)
    normed, _ = norm_parts(x)
    normed = (normed * gain_ref[...][None, :]).astype(BF16)

    pre = lax.dot_general(normed, up_ref[...], LAST, preferred_element_type=F32)
    pre = pre + bias_ref[...][None, :]
    root = math.sqrt(2.0 / math.pi)
    square = pre * pre
    tanh = jnp.tanh(root * (pre + 0.044715 * (square * pre)))
    half = 0.5 * (1.0 + tanh)
    act = (pre * half).astype(BF16).astype(F32)
    slope = half + (0.5 * root) * pre * (1.0 - tanh * tanh) * (
        1.0 + (3.0 * 0.044715) * square
    )
    slope_ref[...] = slope.astype(BF16)

    def add(total, values):
        row = lax.broadcasted_iota(jnp.int32, total.shape, 0)
        sums = jnp.sum(values, axis=0, keepdims=True)
        total[...] += jnp.where(row == image, sums, 0.0)

    add(act_sum, act)
    add(x_sum, x)

    @pl.when(step == pl.num_programs(0) - 1)
    def _():
        stack = split_stack(act_sum[...] * (1.0 / PATCHES))
        mlp = unstack(jnp.dot(stack, down_ref[...], preferred_element_type=F32))
        rest = x_sum[...] * (1.0 / PATCHES) + b_down_ref[...][None, :]
        part = (mlp + rest * (1.0 / n_tensor))[0:2]
        for copy in range(n_tensor):
            part_ref[copy] = part


def forward(patches, ln_gain, up_t, b_up, w_down, b_down, n_tensor):
    tokens, width = patches.shape
    units = up_t.shape[0]
    rows = 128
    vector = lambda size: pl.BlockSpec((size,), lambda i: (0,))
    return pl.pallas_call(
        functools.partial(forward_kernel, n_tensor),
        grid=(tokens // rows,),
        in_specs=[
            pl.BlockSpec((rows, width), lambda i: (i, 0)),
            vector(width),
            vector(units),
            vector(width),
            pl.BlockSpec((units, width), lambda i: (0, 0)),
            pl.BlockSpec((units, width), lambda i: (0, 0)),
        ],
        out_specs=[
            pl.BlockSpec((rows, units), lambda i: (i, 0)),
            pl.BlockSpec((n_tensor, 2, width), lambda i: (0, 0, 0)),
        ],
        out_shape=[
            jax.ShapeDtypeStruct((tokens, units), BF16),
            jax.ShapeDtypeStruct((n_tensor, 2, width), F32),
        ],
        scratch_shapes=[
            pltpu.VMEM((8, units), F32),
            pltpu.VMEM((8, width), F32),
        ],
        compiler_params=SMALL,
        cost_estimate=pl.CostEstimate(
            flops=2 * tokens * width * units,
            bytes_accessed=2 * tokens * width + 4 * units * width + 4 * tokens * units,
            transcendentals=tokens * units,
        ),
        name="forward",
    )(patches, ln_gain, b_up, b_down, up_t, w_down)


def pick_row(rows, index):
    row = lax.broadcasted_iota(jnp.int32, rows.shape, 0)
    return jnp.sum(jnp.where(row == index, rows, 0.0), axis=0, keepdims=True)


def image_features(rows, gain):
    feat_n, feat_s = norm_parts(jnp.concatenate([rows] * 4, axis=0))
    features = feat_n * gain
    feat_len = jnp.sqrt(jnp.sum(features * features, axis=-1, keepdims=True) + EPS)
    return feat_n, feat_s, feat_len, features / feat_len


def pair_grad(queries, keys, ids_ref, id_columns, sharp, shift):
    batch = keys.shape[0]
    logits = sharp * unstack(
        lax.dot_general(split_stack(queries), keys, LAST, preferred_element_type=F32)
    ) + shift
    lane = lax.broadcasted_iota(jnp.int32, (16, 128), 1)
    first_lane = jnp.where(lane == 0, 1.0, 0.0).astype(BF16)
    ids = lax.dot_general(first_lane, id_columns, LAST, preferred_element_type=F32)[0:8]
    row = lax.broadcasted_iota(jnp.int32, (8, batch), 0)
    own = jnp.where(row == 0, ids_ref[0], ids_ref[1]).astype(F32)
    sign = jnp.where(ids == own, 1.0, -1.0)
    logit_grad = -LOSS_SCALE * sign * jax.nn.sigmoid(-sign * logits) / batch
    logit_grad = jnp.where(row < 2, logit_grad, 0.0)
    return sharp * unstack(
        jnp.dot(split_stack(logit_grad), keys, preferred_element_type=F32)
    )


def scalars(sharp_ref, shift_ref):
    return jnp.exp(sharp_ref[...][None, :]), shift_ref[...][None, :]


def loss_kernel(
    place_ref, ids_ref, sharp_ref, shift_ref, parts_ref, gain_ref, rows_ref, down_ref,
    up_ref, slope_ref, img_ref, hidden_ref, away_ref, keep_ref, g_pre,
):
    width = gain_ref.shape[0]
    core, one, two = places(place_ref[0])
    gain = gain_ref[...][None, :]
    pooled = parts_ref[0]
    for part in range(1, parts_ref.shape[0]):
        pooled = pooled + parts_ref[part]
    feat_n, feat_s, feat_len, img_emb = image_features(pooled, gain)
    for copy in range(img_ref.shape[0]):
        img_ref[copy] = img_emb[0:2].astype(BF16)
    g_img = pair_grad(
        img_emb, rows_ref[:, 0:width], ids_ref, rows_ref[:, width : width + 128],
        *scalars(sharp_ref, shift_ref),
    )
    g_feat = (
        g_img - img_emb * jnp.sum(img_emb * g_img, axis=-1, keepdims=True)
    ) / feat_len
    g_hidden = norm_back(g_feat, gain, feat_n, feat_s) * (1.0 / PATCHES)
    hidden_ref[...] = g_hidden[0:2]
    g_rows = jnp.concatenate([g_hidden, jnp.zeros_like(g_hidden)], axis=0).astype(BF16)
    g_act = lax.dot_general(g_rows, down_ref[...], LAST, preferred_element_type=F32)[0:8]
    for image, blocks, out_ref in (
        (1 - core, order(two, one), away_ref),
        (core, order(one, two), keep_ref),
    ):
        row = pick_row(g_act, image)
        for spot, block in enumerate(blocks):
            start = pl.multiple_of(image * PATCHES + block * BLOCK, BLOCK)
            g_pre[spot * BLOCK : (spot + 1) * BLOCK, :] = (
                slope_ref[pl.ds(start, BLOCK), :].astype(F32) * row
            ).astype(BF16)
        out_ref[...] = jnp.dot(
            g_pre[...], up_ref[...], preferred_element_type=F32
        ).astype(BF16)


def loss_and_back(
    place, sharp, shift, ids, parts, gain, rows, w_down, up_t, slope, copies
):
    units, width = up_t.shape
    return pl.pallas_call(
        loss_kernel,
        in_specs=[SMEM] * 2 + [VMEM] * 8,
        out_shape=[
            jax.ShapeDtypeStruct((copies, 2, width), BF16),
            jax.ShapeDtypeStruct((2, width), F32),
            jax.ShapeDtypeStruct((PATCHES, width), BF16),
            jax.ShapeDtypeStruct((PATCHES, width), BF16),
        ],
        scratch_shapes=[pltpu.VMEM((PATCHES, units), BF16)],
        compiler_params=SMALL,
        cost_estimate=pl.CostEstimate(
            flops=4 * PATCHES * width * units,
            bytes_accessed=6 * units * width + 8 * PATCHES * units,
            transcendentals=0,
        ),
        name="loss_and_back",
    )(place, ids, sharp, shift, parts, gain, rows, w_down, up_t, slope)


def text_kernel(
    ids_ref, sharp_ref, shift_ref, unit_ref, len_ref, img_ref, columns_ref, out_ref
):
    unit = unit_ref[...]
    queries = jnp.concatenate([unit] * 4, axis=0).astype(BF16).astype(F32)
    g_text = pair_grad(
        queries, img_ref[...], ids_ref, columns_ref[...],
        *scalars(sharp_ref, shift_ref),
    )[0:2]
    along = jnp.sum(unit * g_text, axis=-1, keepdims=True)
    out_ref[...] = (g_text - unit * along) / len_ref[:, 0:1]


def text_grad(sharp, shift, ids, unit, length, images, columns):
    return pl.pallas_call(
        text_kernel,
        in_specs=[SMEM] + [VMEM] * 6,
        out_shape=jax.ShapeDtypeStruct(unit.shape, F32),
        compiler_params=SMALL,
        cost_estimate=pl.CostEstimate(
            flops=1_000_000_000, bytes_accessed=600_000, transcendentals=0
        ),
        name="text_grad",
    )(ids, sharp, shift, unit, length, images, columns)


def finish_kernel(place_ref, mine_ref, one_ref, two_ref, x_ref, hidden_ref, gain_ref, out_ref):
    g_normed = mine_ref[...] + one_ref[BLOCK:, :].astype(F32) + two_ref[...].astype(F32)
    normed, inverse = norm_parts(x_ref[...].astype(F32))
    grad = norm_back(g_normed, gain_ref[...][None, :], normed, inverse)
    out_ref[...] = (grad + pick_row(hidden_ref[...], place_ref[0] & 1)).astype(BF16)


def finish(place, mine, got_one, got_two, own_x, g_hidden, ln_gain):
    return pl.pallas_call(
        finish_kernel,
        in_specs=[SMEM] + [VMEM] * 6,
        out_shape=jax.ShapeDtypeStruct(mine.shape, BF16),
        compiler_params=SMALL,
        cost_estimate=pl.CostEstimate(
            flops=5_000_000_000, bytes_accessed=1_000_000, transcendentals=0
        ),
        name="finish",
    )(place, mine, got_one, got_two, own_x, g_hidden, ln_gain)


def place_kernel(place_ref, own, two, one, near, rest, out_ref):
    core, one_bit, two_bit = places(place_ref[0])
    low, high = slice(0, BLOCK), slice(BLOCK, 2 * BLOCK)
    mine, theirs = order(one_bit, two_bit), order(two_bit, one_bit)
    moves = [
        (one, high, core, mine[0]),
        (one, low, core, mine[1]),
        (two, low, core, mine[2]),
        (own, low, core, mine[3]),
        (rest, high, 1 - core, theirs[0]),
        (rest, low, 1 - core, theirs[1]),
        (near, high, 1 - core, theirs[2]),
        (near, low, 1 - core, theirs[3]),
    ]
    for ref, rows, image, block in moves:
        start = pl.multiple_of(image * PATCHES + block * BLOCK, BLOCK)
        out_ref[pl.ds(start, BLOCK), :] = ref[rows, :]


def put_in_place(place, pieces, tokens):
    width = pieces[0].shape[1]
    return pl.pallas_call(
        place_kernel,
        in_specs=[SMEM] + [VMEM] * 5,
        out_shape=jax.ShapeDtypeStruct((tokens, width), BF16),
        compiler_params=SMALL,
        name="put_in_place",
    )(place, *pieces)


def swap(value, axis, partner):
    size = lax.axis_size(axis)
    return lax.ppermute(value, axis, [(i, partner(i)) for i in range(size)])


def swap_core(value):
    return swap(value, "tensor", lambda i: i ^ 1)


def step_one(i):
    return i ^ 2 if i % 2 == 0 else (3 - i // 2) * 2 + 1


def step_two(i):
    return (3 - i // 2) * 2 if i % 2 == 0 else i ^ 2


def exchange(copies, groups, axis="dp"):
    return lax.all_to_all(
        copies, axis, split_axis=0, concat_axis=0, axis_index_groups=groups
    )


def spread(rows, groups):
    copies = jnp.broadcast_to(rows[None], (len(groups[0]),) + rows.shape)
    return exchange(copies, groups)


def on_device(
    patches,
    ln_gain,
    w_up,
    b_up,
    w_down,
    b_down,
    head_gain,
    text_feats,
    pair_ids,
    log_sharpness,
    pairwise_logit_shift,
):
    batch = text_feats.shape[0] * lax.axis_size("dp")
    place = lax.axis_index("tensor").astype(jnp.int32).reshape(1)

    side = math.isqrt(lax.axis_size("dp"))
    along_y = [[y * side + k for y in range(side)] for k in range(side)]
    along_xz = [[y * side + k for k in range(side)] for y in range(side)]
    packed, unit_text, text_len = pack(pair_ids, text_feats, side)
    some_text = exchange(packed, along_y).reshape(2 * side, -1)

    up_t = w_up.T
    some_text, first_gain = lax.optimization_barrier((some_text, ln_gain))
    rows = spread(some_text, along_xz).reshape(batch, -1)
    slope, parts = forward(
        patches, first_gain, up_t, b_up, w_down, b_down, lax.axis_size("tensor")
    )
    parts, rows = lax.optimization_barrier((parts, rows))
    parts = exchange(parts, None, "tensor")
    img_copies, g_hidden, away, keep = loss_and_back(
        place,
        log_sharpness,
        pairwise_logit_shift,
        pair_ids,
        parts,
        head_gain,
        rows,
        w_down,
        up_t,
        slope,
        side,
    )

    other = swap_core(away)

    def both(start, count):
        part = slice(start, start + count)
        return keep[part].astype(F32) + other[part].astype(F32)

    send_one = both(0, 128).astype(BF16)
    got_one = swap(send_one, "tensor", step_one)
    img_copies, _ = lax.optimization_barrier((img_copies, send_one))
    some_img = exchange(img_copies, along_xz).reshape(2 * side, -1)
    core, one, two = places(place[0])
    own_start = core * PATCHES + (2 * one + two) * BLOCK
    own_x = lax.dynamic_slice_in_dim(patches, own_start, BLOCK, 0)
    got_one, some_img, travels, mine, own_x = lax.optimization_barrier(
        (got_one, some_img, both(128, 64), both(192, 64), own_x)
    )
    send_two = (travels + got_one[:BLOCK].astype(F32)).astype(BF16)
    got_two = swap(send_two, "tensor", step_two)
    some_img, _ = lax.optimization_barrier((some_img, send_two))
    images = spread(some_img, along_y).reshape(batch, -1)
    done = finish(place, mine, got_one, got_two, own_x, g_hidden, ln_gain)

    from_two = swap(done, "tensor", step_two)
    ids = rows[:, -128:].reshape(side, side, 2, 128).swapaxes(0, 1).reshape(batch, 128)
    grad_text = text_grad(
        log_sharpness,
        pairwise_logit_shift,
        pair_ids,
        unit_text,
        text_len,
        images,
        ids,
    )
    pair = jnp.concatenate([done, from_two])
    from_one = swap(pair, "tensor", step_one)
    near = swap_core(pair)
    from_one, grad_text = lax.optimization_barrier((from_one, grad_text))
    rest = swap_core(from_one)
    grad_patches = put_in_place(
        place, (done, from_two, from_one, near, rest), patches.shape[0]
    )

    return grad_patches, grad_text


def solution(mesh):
    in_specs = (
        P("dp", None),
        P(),
        P(None, "tensor"),
        P("tensor"),
        P("tensor", None),
        P(),
        P(),
        P("dp", None),
        P("dp"),
        P(),
        P(),
    )
    out_specs = (P("dp", None), P("dp", None))
    return jax.shard_map(
        on_device, mesh=mesh, in_specs=in_specs, out_specs=out_specs, check_vma=False
    )
```
